32 devices in a mesh: dp: 8 (over z, y), mp: 4 (over x, core).
Axes of the slice: x: 2, y: 2, z: 4, core: 2. Of those that a mesh axis runs over, the one named last changes fastest.
Arguments:
- tokens: bfloat16 [16384, 768], P('dp'), may hold values from -6 to 6
- cotangent: bfloat16 [16384, 768], P('dp'), may hold values from -6 to 6
- seq_lengths: int32 [8, 2], P('dp'), may hold values from 512 to 1024, as said below
- source_slot: int32 [16384], P('dp'), may hold values from 0 to 2048, as said below
- ln1_gain: bfloat16 [768], replicated, may hold values from 0.5 to 1.5
- ln1_bias: bfloat16 [768], replicated, may hold values from -1.25 to 1.25
- qkv_weight: bfloat16 [768, 3, 768], P(None, None, 'mp'), may hold values from -0.21875 to 0.21875
- qv_bias: bfloat16 [2, 768], P(None, 'mp'), may hold values from -1.25 to 1.25
- output_projection_weight: bfloat16 [768, 768], P('mp'), may hold values from -1.75 to 1.75
- out_bias: bfloat16 [768], replicated, may hold values from -1.25 to 1.25
- ln2_gain: bfloat16 [768], replicated, may hold values from 0.5 to 1.5
- ln2_bias: bfloat16 [768], replicated, may hold values from -1.25 to 1.25
- fc_weight: bfloat16 [768, 3072], P(None, 'mp'), may hold values from -0.21875 to 0.21875
- fc_bias: bfloat16 [3072], P('mp'), may hold values from -1.25 to 1.25
- proj_weight: bfloat16 [3072, 768], P('mp'), may hold values from -0.109375 to 0.109375
- proj_bias: bfloat16 [768], replicated, may hold values from -1.25 to 1.25
Outputs:
- block_out: bfloat16 [16384, 768], P('dp')
- input_grad: bfloat16 [16384, 768], P('dp')
- ln1_gain_grad: float32 [768], replicated
- ln1_bias_grad: float32 [768], replicated
- qkv_weight_grad: float32 [768, 3, 768], P(None, None, 'mp')
- qv_bias_grad: float32 [2, 768], P(None, 'mp')
- out_weight_grad: float32 [768, 768], P('mp')
- out_bias_grad: float32 [768], replicated
- ln2_gain_grad: float32 [768], replicated
- ln2_bias_grad: float32 [768], replicated
- fc_weight_grad: float32 [768, 3072], P(None, 'mp')
- fc_bias_grad: float32 [3072], P('mp')
- proj_weight_grad: float32 [3072, 768], P('mp')
- proj_bias_grad: float32 [768], replicated
The draws below stay inside these ranges and needn't reach their ends.
Inputs may be any that keep to these rules, and one draw needn't show every extreme that they name: `seq_lengths`: each row gives the lengths of the two sequences packed one after the other from position 0 into a block of 2048 rows; the rest of the block is padding. On one device, drawn anew, both sequences of every block have 1024 tokens. `source_slot`: entry k * 2048 + p names the received row s (source device s // 256, that source's slot s % 256 for destination k) that lands at packed position p of device k; 2048 marks padding. Live positions of one device name distinct rows. Token t of a sequence comes from source (t + r) mod 8 for an r of its own. One source fills at most 256 slots for one destination, and on some device all 256 from every source.
All inputs are finite; a program needn't handle non-finite values.
Results may differ from the reference program's by a relative error of at most 0.019.
Values may be sent and summed in bfloat16 or wider, within the bound.
A program may use at most 192 MiB of HBM per device.

```python
import jax
import jax.numpy as jnp
from jax import lax

MODEL_DIMENSION = 768
H = 12
HD = 64
FF = 3072
MAXLEN = 1024
BLOCKS_DEV = 1
BLOCK = 2048
PACK = 2048
BLOCKS = 8
CAP = 256
SRC_ROWS = 2048
TOKENS = 16384
N_DP = 8
N_MP = 4


def plan_tables(key):
    len_key = jax.random.fold_in(key, 11)
    full_key = jax.random.fold_in(key, 12)
    turn_key = jax.random.fold_in(key, 13)
    total_blocks = BLOCKS_DEV * N_DP
    seq_lens = jax.random.randint(len_key, (total_blocks, 2), MAXLEN // 2, MAXLEN + 1)
    full_dev = jax.random.randint(full_key, (), 0, N_DP)
    owner_dev = jnp.arange(total_blocks) // BLOCKS_DEV
    seq_lens = jnp.where((owner_dev == full_dev)[:, None], MAXLEN, seq_lens).astype(jnp.int32)
    rotations = jax.random.randint(turn_key, (total_blocks, 2), 0, N_DP).astype(jnp.int32)
    sources = jnp.arange(N_DP).astype(jnp.int32)
    offset = (sources[None, None, :] - rotations[:, :, None]) % N_DP
    counts = (seq_lens[:, :, None] - offset + N_DP - 1) // N_DP
    per_block = jnp.sum(counts, axis=1).reshape(N_DP, BLOCKS_DEV, N_DP)
    before = (jnp.cumsum(per_block, axis=1) - per_block).reshape(total_blocks, N_DP)
    positions = jnp.arange(BLOCK).astype(jnp.int32)[None, :]
    first_len = seq_lens[:, :1]
    second = positions >= first_len
    token_pos = positions - jnp.where(second, first_len, 0)
    live_rows = positions < first_len + seq_lens[:, 1:]
    rotation = jnp.where(second, rotations[:, 1:], rotations[:, :1])
    source = (token_pos + rotation) % N_DP
    earlier = jnp.take_along_axis(before, source, axis=1) + jnp.where(second, jnp.take_along_axis(counts[:, 0, :], source, axis=1), 0)
    slot_index = source * CAP + earlier + token_pos // N_DP
    slot_index = jnp.where(live_rows, slot_index, SRC_ROWS).reshape(-1).astype(jnp.int32)
    return (seq_lens, slot_index)


def draw_seq_lengths(key, part):
    seq_lens, slot_index = plan_tables(key)
    return seq_lens


def draw_source_slot(key, part):
    seq_lens, slot_index = plan_tables(key)
    return slot_index


def steps_of(own_key, dims, split, least, top_value):
    factor_of = 1.0
    for dim, blocks in split:
        heights = jax.random.uniform(jax.random.fold_in(jax.random.fold_in(own_key, 6), dim), (blocks,), jnp.float32, least / len(split), top_value / len(split))
        factor_of = factor_of * jnp.repeat(jnp.exp(heights), dims[dim] // blocks).reshape((-1,) + (1,) * (len(dims) - 1 - dim))
    return factor_of


def gaussian(key, shape, deviation, bound, cuts=(), kind=jnp.bfloat16):
    entries = jax.random.normal(key, shape, jnp.float32) * deviation
    if len(cuts) > 0:
        entries = steps_of(key, shape, cuts, -0.22, 0.18) * entries
    return jnp.clip(entries, min=-bound, max=bound).astype(kind)


def setup_inputs(seed: int = 0) -> dict:
    seeds = jax.random.split(jax.random.key(seed), 17)
    return {
        "tokens": gaussian(seeds[0], (TOKENS, MODEL_DIMENSION), 1.0, 6.0, ((0, 8),)),
        "cotangent": gaussian(seeds[1], (TOKENS, MODEL_DIMENSION), 1.0, 6.0, ((0, 8),)),
        "seq_lengths": draw_seq_lengths(jax.random.fold_in(seeds[16], 71), 0),
        "source_slot": draw_source_slot(jax.random.fold_in(seeds[16], 71), 0),
        "ln1_gain": jnp.clip(1.0 + 0.1 * jax.random.normal(seeds[4], (MODEL_DIMENSION,), jnp.float32), 0.5, 1.5).astype(jnp.bfloat16),
        "ln1_bias": gaussian(seeds[5], (MODEL_DIMENSION,), 0.2, 1.25),
        "qkv_weight": gaussian(seeds[6], (MODEL_DIMENSION, 3, MODEL_DIMENSION), MODEL_DIMENSION ** -0.5, 0.21875, ((2, 4),)),
        "qv_bias": gaussian(seeds[7], (2, MODEL_DIMENSION), 0.2, 1.25, ((1, 4),)),
        "output_projection_weight": gaussian(seeds[8], (MODEL_DIMENSION, MODEL_DIMENSION), (16 * MODEL_DIMENSION // MAXLEN) ** -0.5, 1.75, ((0, 4),)),
        "out_bias": gaussian(seeds[9], (MODEL_DIMENSION,), 0.2, 1.25),
        "ln2_gain": jnp.clip(1.0 + 0.1 * jax.random.normal(seeds[10], (MODEL_DIMENSION,), jnp.float32), 0.5, 1.5).astype(jnp.bfloat16),
        "ln2_bias": gaussian(seeds[11], (MODEL_DIMENSION,), 0.2, 1.25),
        "fc_weight": gaussian(seeds[12], (MODEL_DIMENSION, FF), MODEL_DIMENSION ** -0.5, 0.21875, ((1, 4),)),
        "fc_bias": gaussian(seeds[13], (FF,), 0.2, 1.25, ((0, 4),)),
        "proj_weight": gaussian(seeds[14], (FF, MODEL_DIMENSION), FF ** -0.5, 0.109375, ((0, 4),)),
        "proj_bias": gaussian(seeds[15], (MODEL_DIMENSION,), 0.2, 1.25),
    }


@jax.custom_vjp
def reduced_precision(v):
    return lax.optimization_barrier(v.astype(jnp.bfloat16)).astype(jnp.float32)

@jax.custom_vjp
def low_back(v):
    return v

def low_keep(v):
    return (reduced_precision(v), None)

def low_pass(kept, grad):
    return (grad,)

def back_keep(v):
    return (v, None)

def back_low(kept, grad):
    return (reduced_precision(grad),)
reduced_precision.defvjp(low_keep, low_pass)
low_back.defvjp(back_keep, back_low)
EPSILON = 1e-05
MASKED = -1000000000.0
FULL_PRECISION = lax.Precision.HIGHEST

def norm_rows(values, norm_gain, norm_shift):
    row_mean = lax.optimization_barrier(jnp.mean(values, axis=-1, keepdims=True))
    centered = values - row_mean
    variance = lax.optimization_barrier(jnp.mean(centered * centered, axis=-1, keepdims=True))
    return centered * lax.rsqrt(variance + EPSILON) * norm_gain + norm_shift

def head_major(values, block_len):
    local_heads = MODEL_DIMENSION // N_MP // HD
    return values.reshape(N_MP, block_len, local_heads, HD).transpose(0, 2, 1, 3).reshape(H, block_len, HD)

def block_layer(row_data, lengths, weights):
    gain_one, shift_one, qkv_weight, qv_bias, output_projection_weight, out_bias, gain_two, shift_two, fc_weight, fc_bias, proj_weight, proj_bias = weights
    block_len = row_data.shape[0]
    group_span_width = MODEL_DIMENSION // N_MP
    local_heads = group_span_width // HD
    unit_width = FF // N_MP
    normed = reduced_precision(norm_rows(row_data, gain_one, shift_one))
    copies = low_back(jnp.broadcast_to(normed, (N_MP, block_len, MODEL_DIMENSION)))
    grouped = qkv_weight.reshape(MODEL_DIMENSION, 3, N_MP, group_span_width)
    projected = jnp.einsum('gbd,dcgp->cgbp', copies, grouped, precision=FULL_PRECISION)
    queries = projected[0] + qv_bias[0].reshape(N_MP, 1, group_span_width)
    keys_all = projected[1]
    values_all = projected[2] + qv_bias[1].reshape(N_MP, 1, group_span_width)
    queries = low_back(reduced_precision(head_major(queries, block_len)))
    keys_all = low_back(reduced_precision(head_major(keys_all, block_len)))
    values_all = low_back(reduced_precision(head_major(values_all, block_len)))
    scores = low_back(jnp.einsum('hqd,hkd->hqk', queries, keys_all, precision=FULL_PRECISION) * HD ** (-0.5))
    positions = jnp.arange(block_len).astype(jnp.int32)
    segment = (positions >= lengths[0]).astype(jnp.int32) + (positions >= lengths[0] + lengths[1]).astype(jnp.int32)
    allowed = (positions[None, :] <= positions[:, None]) & (segment[None, :] == segment[:, None])
    scores = jnp.where(allowed[None], scores, MASKED)
    row_top = lax.optimization_barrier(jnp.max(scores, axis=-1, keepdims=True))
    exponent = jnp.exp(scores - row_top)
    probabilities = reduced_precision(exponent / lax.optimization_barrier(jnp.sum(exponent, axis=-1, keepdims=True)))
    attention_result = jnp.einsum('hqk,hkd->hqd', probabilities, values_all, precision=FULL_PRECISION)
    attention_result = attention_result.reshape(N_MP, local_heads, block_len, HD).transpose(0, 2, 1, 3).reshape(N_MP, block_len, group_span_width)
    attention_result = low_back(reduced_precision(attention_result))
    attention_pieces = reduced_precision(jnp.einsum('ymd,ydo->ymo', attention_result, output_projection_weight.reshape(N_MP, group_span_width, MODEL_DIMENSION), precision=FULL_PRECISION))
    attn_out = low_back(lax.optimization_barrier(jnp.sum(attention_pieces, axis=0)) + out_bias)
    middle = row_data + attn_out
    normed_two = reduced_precision(norm_rows(middle, gain_two, shift_two))
    copies_two = low_back(jnp.broadcast_to(normed_two, (N_MP, block_len, MODEL_DIMENSION)))
    hidden = jnp.einsum('gbd,dgf->gbf', copies_two, fc_weight.reshape(MODEL_DIMENSION, N_MP, unit_width), precision=FULL_PRECISION) + fc_bias.reshape(N_MP, 1, unit_width)
    hidden = low_back(hidden)
    active = reduced_precision(jax.nn.gelu(hidden, approximate=True))
    mlp_terms = reduced_precision(jnp.einsum('gbf,gfe->gbe', active, proj_weight.reshape(N_MP, unit_width, MODEL_DIMENSION), precision=FULL_PRECISION))
    return middle + (lax.optimization_barrier(jnp.sum(mlp_terms, axis=0)) + proj_bias)

def packed_index(source_slot):
    position = jnp.arange(N_DP * PACK).astype(jnp.int32)
    device = position // PACK
    source = source_slot // CAP
    within = source_slot % CAP
    gathered = source * SRC_ROWS + device * CAP + within
    return jnp.where(source_slot == SRC_ROWS, TOKENS, gathered).astype(jnp.int32)

def reference(tokens, cotangent, seq_lengths, source_slot, ln1_gain, ln1_bias, qkv_weight, qv_bias, output_projection_weight, out_bias, ln2_gain, ln2_bias, fc_weight, fc_bias, proj_weight, proj_bias):
    parameters = tuple((item.astype(jnp.float32) for item in (ln1_gain, ln1_bias, qkv_weight, qv_bias, output_projection_weight, out_bias, ln2_gain, ln2_bias, fc_weight, fc_bias, proj_weight, proj_bias)))
    flat_rows = tokens.astype(jnp.float32)
    gather_index = packed_index(source_slot)

    def forward(source_rows, weights):
        padded = jnp.concatenate([source_rows, jnp.zeros((1, MODEL_DIMENSION), jnp.float32)], axis=0)
        packed = jnp.take(padded, gather_index, axis=0).reshape(BLOCKS, BLOCK, MODEL_DIMENSION)

        def one_block(block_item):
            return jax.checkpoint(block_layer)(block_item[0], block_item[1], weights)
        results = lax.map(one_block, (packed, seq_lengths))
        holder = jnp.zeros((TOKENS + 1, MODEL_DIMENSION), jnp.float32).at[gather_index].add(results.reshape(N_DP * PACK, MODEL_DIMENSION))
        return holder[:TOKENS]
    outcome, pullback = jax.vjp(forward, flat_rows, parameters)
    grad_rows, grad_params = pullback(cotangent.astype(jnp.float32))
    g_gain_one, g_shift_one, g_qkv, g_qv, g_out, g_out_bias, g_gain_two, g_shift_two, g_fc, g_fc_bias, g_proj, g_proj_bias = grad_params
    return (outcome.astype(jnp.bfloat16), grad_rows.astype(jnp.bfloat16), g_gain_one, g_shift_one, g_qkv, g_qv, g_out, g_out_bias, g_gain_two, g_shift_two, g_fc, g_fc_bias, g_proj, g_proj_bias)
```

```python
import functools

import jax
import jax.numpy as jnp
from jax import lax
from jax.experimental import pallas as pl
from jax.experimental.pallas import tpu as pltpu
from jax.sharding import PartitionSpec as P

MESH = pl.DeviceIdType.MESH
BF = jnp.bfloat16
F32 = jnp.float32
HD = 64
EPSILON = 1e-05
NEG = -1e30
LOG2E = 1.4426950408889634
TILE = 256
WINDOW = 1024
CHUNKS = 4
LANES = 128
VMEM_LIMIT = 60 * 2**20


class Plan:
    def __init__(self, n, members, rows, width, heads):
        self.n, self.members, self.rows, self.width, self.heads = n, members, rows, width, heads
        self.slots = rows // n
        self.group = max(1, (16 * members) // self.slots)
        self.share = self.group * self.slots // members
        self.groups = n // self.group
        self.chunk = rows // CHUNKS
        self.own = self.chunk // members
        self.take = max(16, self.share // CHUNKS)
        self.split = self.share // self.take
        self.in_chunk = self.own // self.take
        self.pad = -(-heads * HD // LANES) * LANES

    def work_index(self, slot_ids):
        source, slot = slot_ids // self.slots, slot_ids % self.slots
        grp = source // self.group
        inside = (source % self.group) * self.slots + slot
        owner, row = inside // self.share, inside % self.share
        chunk = (grp // self.in_chunk) * self.split + row // self.take
        place = (owner % 2) * (self.members // 2) + owner // 2
        index = chunk * self.chunk + place * self.own + (grp % self.in_chunk) * self.take + row % self.take
        return jnp.where(slot_ids >= self.rows, -1, index).astype(jnp.int32)


def nn(a, b):
    return lax.dot_general(a, b, (((1,), (0,)), ((), ())), preferred_element_type=F32)


def nt(a, b):
    return lax.dot_general(a, b, (((1,), (1,)), ((), ())), preferred_element_type=F32)


def tn(a, b):
    return lax.dot_general(a, b, (((0,), (0,)), ((), ())), preferred_element_type=F32)


def rows_at(start, count, step=16):
    if not isinstance(start, int):
        start = pl.multiple_of(start, step)
    return pl.ds(start, count)


class Place:
    def __init__(self, plan):
        self.plan = plan
        self.d = lax.axis_index("dp")
        self.m = lax.axis_index("mp")
        self.core = lax.rem(self.m, 2)
        self.side = self.m // 2
        self.mate = self.m + 1 - 2 * self.core
        self.across = lax.rem(self.m + 2, plan.members)
        self.spot = self.core * 2 + self.side

    def spot_of(self, core_flip, side_flip):
        core = 1 - self.core if core_flip else self.core
        side = 1 - self.side if side_flip else self.side
        return core * 2 + side

    def member(self, core_flip, side_flip):
        core = 1 - self.core if core_flip else self.core
        side = 1 - self.side if side_flip else self.side
        return side * 2 + core


def send(src, dst, sems, index, device):
    copy = pltpu.make_async_remote_copy(
        src_ref=src,
        dst_ref=dst,
        send_sem=sems[0].at[index],
        recv_sem=sems[1].at[index],
        device_id=device,
        device_id_type=MESH,
    )
    copy.start()
    return copy


def landed(dst, sems, index, device):
    pltpu.make_async_remote_copy(
        src_ref=dst,
        dst_ref=dst,
        send_sem=sems[0].at[index],
        recv_sem=sems[1].at[index],
        device_id=device,
        device_id_type=MESH,
    ).wait_recv()


def left(src, sems, index, device):
    pltpu.make_async_remote_copy(
        src_ref=src,
        dst_ref=src,
        send_sem=sems[0].at[index],
        recv_sem=sems[1].at[index],
        device_id=device,
        device_id_type=MESH,
    ).wait_send()


def entry_barrier(plan, at):
    barrier = pltpu.get_barrier_semaphore()

    def signal(j, carry):
        pl.semaphore_signal(
            barrier, inc=1, device_id={"dp": lax.rem(at.d + j, plan.n)}, device_id_type=MESH
        )
        return carry

    lax.fori_loop(1, plan.n, signal, 0)
    pl.semaphore_signal(barrier, inc=1, device_id={"mp": at.mate}, device_id_type=MESH)
    pl.semaphore_signal(barrier, inc=1, device_id={"mp": at.across}, device_id_type=MESH)
    pl.semaphore_wait(barrier, plan.n + 1)


class Gather:
    def __init__(self, at, buf, sems):
        self.at, self.buf, self.sems, self.copies = at, buf, sems, []

    def rows(self, c, core_flip=False, side_flip=False):
        plan = self.at.plan
        start = c * plan.chunk + self.at.spot_of(core_flip, side_flip) * plan.own
        return self.buf.at[rows_at(start, plan.own)]

    def start(self, c):
        mine = self.rows(c)
        self.copies.append(send(mine, mine, self.sems, (c, 1), {"mp": self.at.across}))
        self.copies.append(send(mine, mine, self.sems, (c, 0), {"mp": self.at.mate}))

    def forward(self, c):
        theirs = self.rows(c, side_flip=True)
        landed(theirs, self.sems, (c, 1), {"mp": self.at.across})
        self.copies.append(send(theirs, theirs, self.sems, (c, 2), {"mp": self.at.mate}))

    def finish(self, c):
        landed(self.rows(c, core_flip=True), self.sems, (c, 0), {"mp": self.at.mate})
        landed(self.rows(c, core_flip=True, side_flip=True), self.sems, (c, 2), {"mp": self.at.mate})

    def drain(self):
        for copy in self.copies:
            copy.wait_send()


class Scatter:
    def __init__(self, at, term, near, stage, far, sems):
        self.at, self.term, self.near, self.stage, self.far, self.sems = at, term, near, stage, far, sems
        self.copies = []

    def start(self, c):
        plan, at = self.at.plan, self.at
        start = c * plan.chunk + (1 - at.core) * (2 * plan.own)
        src = self.term.at[rows_at(start, 2 * plan.own)]
        dst = self.near.at[rows_at(c * 2 * plan.own, 2 * plan.own)]
        self.copies.append(send(src, dst, self.sems, (c, 0), {"mp": at.mate}))

    def middle(self, c):
        plan, at = self.at.plan, self.at
        landed(
            self.near.at[rows_at(c * 2 * plan.own, 2 * plan.own)], self.sems, (c, 0), {"mp": at.mate}
        )
        mine = self.term[rows_at(c * plan.chunk + at.spot_of(False, True) * plan.own, plan.own), :]
        other = self.near[rows_at(c * 2 * plan.own + (1 - at.side) * plan.own, plan.own), :]
        where = rows_at(c * plan.own, plan.own)
        self.stage[where, :] = (mine.astype(F32) + other.astype(F32)).astype(BF)
        self.copies.append(
            send(self.stage.at[where], self.far.at[where], self.sems, (c, 1), {"mp": at.across})
        )

    def finish(self, c):
        plan, at = self.at.plan, self.at
        where = rows_at(c * plan.own, plan.own)
        landed(self.far.at[where], self.sems, (c, 1), {"mp": at.across})
        mine = self.term[rows_at(c * plan.chunk + at.spot * plan.own, plan.own), :]
        other = self.near[rows_at(c * 2 * plan.own + at.side * plan.own, plan.own), :]
        return mine.astype(F32) + other.astype(F32) + self.far[where, :].astype(F32)

    def drain(self):
        for copy in self.copies:
            copy.wait_send()


class Incoming:
    def __init__(self, at, source, sems, landing):
        plan = at.plan
        self.at, self.source, self.sems, self.landing = at, source, sems, landing
        self.offset = lax.rem(at.m * plan.share, plan.slots)
        self.sends = None
        if plan.group > 1:
            self.sends = lax.rem(at.d, plan.group) == (at.m * plan.share) // plan.slots

    def guarded(self, run):
        if self.sends is None:
            run()
        else:
            pl.when(self.sends)(run)

    def mine(self, part):
        plan, at = self.at.plan, self.at
        grp = at.d // plan.group
        return (grp // plan.in_chunk) * plan.split + part, lax.rem(grp, plan.in_chunk)

    def piece(self, k, part):
        plan = self.at.plan
        start = k * plan.slots + self.offset + part * plan.take
        return self.source.at[rows_at(start, plan.take)]

    def start(self):
        plan, at = self.at.plan, self.at

        def run():
            for part in range(plan.split):
                c, gi = self.mine(part)

                def one(j, carry, part=part, c=c, gi=gi):
                    k = lax.rem(at.d + j, plan.n)
                    pltpu.make_async_remote_copy(
                        src_ref=self.piece(k, part),
                        dst_ref=self.landing(c, gi),
                        send_sem=self.sems[0].at[part, j],
                        recv_sem=self.sems[1].at[c, gi],
                        device_id={"dp": k},
                        device_id_type=MESH,
                    ).start()
                    return carry

                lax.fori_loop(1, plan.n, one, 0)
                pltpu.make_async_copy(
                    self.piece(at.d, part), self.landing(c, gi), self.sems[1].at[c, gi]
                ).start()

        self.guarded(run)

    def wait(self, c):
        plan, at = self.at.plan, self.at

        def one(gi, carry):
            landed(self.landing(c, gi), (self.sems[1], self.sems[1]), (c, gi), {"dp": at.d})
            return carry

        lax.fori_loop(0, plan.in_chunk, one, 0)

    def drain(self):
        plan, at = self.at.plan, self.at

        def run():
            for part in range(plan.split):

                def one(j, carry, part=part):
                    k = lax.rem(at.d + j, plan.n)
                    left(self.piece(k, part), (self.sems[0], self.sems[0]), (part, j), {"dp": k})
                    return carry

                lax.fori_loop(1, plan.n, one, 0)

        self.guarded(run)


class Outgoing:
    def __init__(self, at, rows_ref, out, sems, local_sem, share_sems):
        plan = at.plan
        self.at, self.rows_ref, self.out = at, rows_ref, out
        self.sems, self.local_sem, self.share_sems = sems, local_sem, share_sems

    def holds(self, member):
        plan = self.at.plan
        if plan.group == 1:
            return None
        return lax.rem(self.at.d, plan.group) == (member * plan.share) // plan.slots

    def guarded(self, member, run):
        if self.at.plan.group == 1:
            run()
        else:
            pl.when(self.holds(member))(run)

    def place(self, k, part, member):
        plan = self.at.plan
        start = k * plan.slots + lax.rem(member * plan.share, plan.slots) + part * plan.take
        return self.out.at[rows_at(start, plan.take)]

    def each(self, c, remote, local):
        plan, at = self.at.plan, self.at
        part = c % plan.split

        def one(gi, carry):
            grp = (c // plan.split) * plan.in_chunk + gi
            dest = grp * plan.group + (at.m * plan.share) // plan.slots
            src = self.rows_ref.at[rows_at(c * plan.own + gi * plan.take, plan.take)]
            dst = self.place(at.d, part, at.m)
            pl.when(dest != at.d)(lambda: remote(gi, part, src, dst, dest))
            pl.when(dest == at.d)(lambda: local(gi, part, src, dst))
            return carry

        lax.fori_loop(0, plan.in_chunk, one, 0)

    def copy(self, c, gi, part, src, dst, dest):
        return pltpu.make_async_remote_copy(
            src_ref=src,
            dst_ref=dst,
            send_sem=self.sems[0].at[c, gi],
            recv_sem=self.sems[1].at[part, self.at.d],
            device_id={"dp": dest},
            device_id_type=MESH,
        )

    def start(self, c):
        def local(gi, part, src, dst):
            pltpu.make_async_copy(src, dst, self.local_sem.at[part]).start()

        self.each(c, lambda gi, part, src, dst, dest: self.copy(c, gi, part, src, dst, dest).start(), local)

    def drain(self):
        for c in range(CHUNKS):
            self.each(
                c,
                lambda gi, part, src, dst, dest: self.copy(c, gi, part, src, dst, dest).wait_send(),
                lambda gi, part, src, dst: None,
            )

    def loop(self, part, run):
        lax.fori_loop(0, self.at.plan.n, lambda k, carry: (run(k), carry)[1], 0)

    def share(self, part):
        at = self.at

        def run():
            def one(k):
                here = self.place(k, part, at.m)

                def remote():
                    landed(here, (self.sems[1], self.sems[1]), (part, k), {"dp": at.d})

                def local():
                    pltpu.make_async_copy(here, here, self.local_sem.at[part]).wait()

                pl.when(k != at.d)(remote)
                pl.when(k == at.d)(local)
                send(here, here, self.share_sems, (1, part, k), {"mp": at.across})
                send(here, here, self.share_sems, (0, part, k), {"mp": at.mate})

            self.loop(part, one)

        self.guarded(at.m, run)

    def forward(self, part):
        at = self.at

        def run():
            def one(k):
                there = self.place(k, part, at.across)
                landed(there, self.share_sems, (1, part, k), {"mp": at.across})
                send(there, there, self.share_sems, (2, part, k), {"mp": at.mate})

            self.loop(part, one)

        self.guarded(at.across, run)

    def finish(self, part):
        at = self.at
        corner = at.member(True, True)

        def near():
            self.loop(
                part,
                lambda k: landed(
                    self.place(k, part, at.mate), self.share_sems, (0, part, k), {"mp": at.mate}
                ),
            )

        def far():
            self.loop(
                part,
                lambda k: landed(
                    self.place(k, part, corner), self.share_sems, (2, part, k), {"mp": at.mate}
                ),
            )

        def sent():
            def one(k):
                here = self.place(k, part, at.m)
                left(here, self.share_sems, (1, part, k), {"mp": at.across})
                left(here, self.share_sems, (0, part, k), {"mp": at.mate})

            self.loop(part, one)

        def passed():
            self.loop(
                part,
                lambda k: left(
                    self.place(k, part, at.across), self.share_sems, (2, part, k), {"mp": at.mate}
                ),
            )

        self.guarded(at.mate, near)
        self.guarded(corner, far)
        self.guarded(at.m, sent)
        self.guarded(at.across, passed)


def halvings(rows, n):
    steps, bit, size = [], 1, rows
    while bit < n:
        if size % 32 == 0:
            size //= 2
            steps.append((bit, True, size))
        else:
            steps.append((bit, False, size))
        bit *= 2
    return steps


class Total:
    def __init__(self, at, first, out, landing, base, sems, sem_base):
        self.at, self.out, self.landing, self.sems = at, out, landing, sems
        self.jobs = []
        offset, room, index = 0, base, sem_base
        trail = []
        source, origin = first, 0
        steps = halvings(first.shape[0], at.plan.n)
        for number, (bit, halve, size) in enumerate(steps):
            high = lax.rem(at.d // bit, 2)
            partner = {"dp": at.d + (1 - 2 * high) * bit}
            keep = give = 0
            if halve:
                keep, give = high * size, (1 - high) * size
                trail.append((offset, offset + keep, size, partner))
                offset = offset + keep
            last = offset if number + 1 == len(steps) else None
            self.jobs.append(
                self.exchange(source, origin + give, origin + keep, size, room, index, partner, last)
            )
            source, origin = landing, room
            room, index = room + size, index + 1
        for before, keep, size, partner in reversed(trail):
            self.jobs.append(self.spread(keep, 2 * before + size - keep, size, index, partner))
            index += 1
        self.next = 0
        self.pending = None

    def exchange(self, source, give, keep, size, room, index, partner, last):
        def start():
            return send(
                source.at[rows_at(give, size)],
                self.landing.at[rows_at(room, size)],
                self.sems,
                index,
                partner,
            )

        def end(copy):
            copy.wait()
            step = 96 if size % 96 == 0 else 16

            def one(i, carry):
                here = rows_at(keep + i * step, step)
                there = rows_at(room + i * step, step)
                value = (source[here, :].astype(F32) + self.landing[there, :].astype(F32)).astype(BF)
                if last is None:
                    self.landing[there, :] = value
                else:
                    self.out[rows_at(last + i * step, step), :] = value
                return carry

            lax.fori_loop(0, size // step, one, 0)

        return start, end

    def spread(self, keep, other, size, index, partner):
        def start():
            here = self.out.at[rows_at(keep, size)]
            return send(here, here, self.sems, index, partner)

        def end(copy):
            copy.wait_send()
            landed(self.out.at[rows_at(other, size)], self.sems, index, partner)

        return start, end

    def step(self):
        if self.pending is not None:
            self.pending[0](self.pending[1])
            self.pending = None
        if self.next < len(self.jobs):
            start, end = self.jobs[self.next]
            self.next += 1
            self.pending = (end, start())
        return self.pending is not None


def landing_rows(rows, n):
    return sum(size for _, _, size in halvings(rows, n))


def total_sems(rows, n):
    steps = halvings(rows, n)
    return len(steps) + sum(1 for _, halve, _ in steps if halve)


def normal_rows(x):
    centered = x - jnp.mean(x, axis=-1, keepdims=True)
    inv = lax.rsqrt(jnp.mean(centered * centered, axis=-1, keepdims=True) + EPSILON)
    return centered * inv, inv


def norm_back(grad, normal, inv, gain):
    scaled = grad * gain
    return inv * (
        scaled
        - jnp.mean(scaled, axis=-1, keepdims=True)
        - normal * jnp.mean(scaled * normal, axis=-1, keepdims=True)
    )


def pick(index_col, count):
    lanes = lax.broadcasted_iota(jnp.int32, (index_col.shape[0], count), 1)
    return jnp.where(lanes == index_col, 1.0, 0.0).astype(BF)


def pick_rows(index_row, first, count):
    lines = lax.broadcasted_iota(jnp.int32, (count, index_row.shape[1]), 0) + first
    return jnp.where(lines == index_row, 1.0, 0.0).astype(BF)


def head_lanes(x, odd):
    lane = lax.broadcasted_iota(jnp.int32, x.shape, 1)
    return jnp.where((lane >= HD) == odd, x, jnp.zeros_like(x))


V_LN1G, V_LN1B, V_OUTB, V_LN2G, V_LN2B, V_PROJB, V_FCB, V_QKVB = range(8)
G_LN1G, G_LN1B, G_LN2G, G_LN2B, G_OUTB, G_PROJB, G_FCB, G_QKVB = range(8)
SHARED = 6


def forward_kernel(
    plan,
    tokens,
    cotangent,
    wcol,
    wrow,
    first_key,
    vec,
    wqkv,
    wo,
    wfc,
    wproj,
    n1f,
    qkv_p,
    k_t,
    att_t,
    lse,
    att_w,
    datf,
    dmid,
    own_x,
    mid,
    mlp_term,
    grads,
    gvec,
    live,
    cotf,
    qkv_w,
    v_t,
    term,
    n2f,
    act,
    dhid,
    near_a,
    stage_a,
    far_a,
    near_b,
    stage_b,
    far_b,
    tok_s,
    tok_r,
    cot_s,
    cot_r,
    ag_s,
    ag_r,
    rs_s,
    rs_r,
):
    at = Place(plan)
    rows, width, pad = plan.rows, plan.width, plan.pad
    chunk, own = plan.chunk, plan.own
    entry_barrier(plan, at)
    tok = Incoming(
        at,
        tokens,
        (tok_s, tok_r),
        lambda c, gi: own_x.at[rows_at(c * own + gi * plan.take, plan.take)],
    )
    cot = Incoming(
        at,
        cotangent,
        (cot_s, cot_r),
        lambda c, gi: cotf.at[rows_at(c * chunk + at.spot * own + gi * plan.take, plan.take)],
    )
    tok.start()
    cot.start()
    gather = [
        Gather(at, buf, (ag_s.at[i], ag_r.at[i])) for i, buf in enumerate((n1f, cotf, n2f, datf))
    ]
    norm1_all, cot_all, norm2_all, dattn_all = gather
    attn_sum = Scatter(at, term, near_a, stage_a, far_a, (rs_s.at[0], rs_r.at[0]))
    back_sum = Scatter(at, term, near_b, stage_b, far_b, (rs_s.at[1], rs_r.at[1]))

    def row(i):
        return vec[i : i + 1, :]

    att_t[...] = jnp.zeros_like(att_t)
    gvec[...] = jnp.zeros_like(gvec)
    for c in range(CHUNKS):
        lines = lax.broadcasted_iota(jnp.int32, (own, rows), 0) + (c * chunk + at.spot * own)
        found = jnp.where(lines == wrow[...], 1.0, 0.0)
        live[c * own : (c + 1) * own, :] = jnp.max(found, axis=1, keepdims=True)
    for c in range(CHUNKS + 1):
        if c < CHUNKS:
            tok.wait(c)
            normal, _ = normal_rows(own_x[c * own : (c + 1) * own, :].astype(F32))
            n1f[rows_at(c * chunk + at.spot * own, own), :] = (
                normal * row(V_LN1G) + row(V_LN1B)
            ).astype(BF)
            norm1_all.start(c)
        if c >= 1:
            norm1_all.forward(c - 1)
    for c in range(CHUNKS):
        norm1_all.finish(c)

        def project(i, carry, c=c):
            here = rows_at(c * chunk + i * TILE, TILE, TILE)
            qkv_w[here, :] = (nn(n1f[here, :], wqkv[...]) + row(V_QKVB)).astype(BF)
            return carry

        lax.fori_loop(0, chunk // TILE, project, 0)
    for c in range(CHUNKS):
        cot.wait(c)
        here = rows_at(c * chunk + at.spot * own, own)
        named = live[c * own : (c + 1) * own, :] > 0.5
        cotf[here, :] = jnp.where(named, cotf[here, :].astype(F32), 0.0).astype(BF)
        cot_all.start(c)

    def to_packed(i, carry):
        here = rows_at(i * TILE, TILE, TILE)
        moved = nn(pick(wcol[here, :], rows), qkv_w[...])
        qkv_p[here, :] = moved.astype(BF)
        k_t[:, here] = moved[:, pad : 2 * pad].T.astype(BF)
        v_t[:, here] = moved[:, 2 * pad :].T.astype(BF)
        return carry

    lax.fori_loop(0, rows // TILE, to_packed, 0)
    for c in range(CHUNKS):
        cot_all.forward(c)

    def attend(q0, k0, keys):
        q_here = rows_at(q0, TILE, TILE)
        k_here = rows_at(k0, keys, TILE)
        first = first_key[0:1, q_here]
        key = k0 + lax.broadcasted_iota(jnp.int32, (keys, TILE), 0)
        query = q0 + lax.broadcasted_iota(jnp.int32, (keys, TILE), 1)
        seen = (key >= first) & (key <= query)
        for h in range(plan.heads):
            pair = pl.ds((h // 2) * LANES, LANES)
            qh = head_lanes(qkv_p[q_here, pair], h % 2 == 1)
            kh = qkv_p[k_here, pl.ds(pad + (h // 2) * LANES, LANES)]
            scores = jnp.where(seen, nt(kh, qh), NEG)
            top = jnp.max(scores, axis=0, keepdims=True)
            expo = jnp.exp2((scores - top) * LOG2E)
            total = jnp.sum(expo, axis=0, keepdims=True)
            out = nn(v_t[h * HD : (h + 1) * HD, k_here], expo.astype(BF))
            att_t[h * HD : (h + 1) * HD, q_here] = (out * (1.0 / total)).astype(BF)
            lse[h : h + 1, q_here] = top * LOG2E + jnp.log2(total)

    reach = min(rows, WINDOW + TILE)
    for i in range(reach // TILE - 1):
        attend(i * TILE, 0, (i + 1) * TILE)

    def attend_far(i, carry):
        attend(i * TILE, (i + 1) * TILE - reach, reach)
        return carry

    lax.fori_loop(reach // TILE - 1, rows // TILE, attend_far, 0)

    for c in range(CHUNKS):

        def combine(i, carry, c=c):
            start = c * chunk + i * TILE
            here = rows_at(start, TILE, TILE)
            moved = nt(pick_rows(wrow[...], start, TILE), att_t[...]).astype(BF)
            att_w[here, :] = moved
            term[here, :] = nn(moved, wo[...]).astype(BF)
            return carry

        lax.fori_loop(0, chunk // TILE, combine, 0)
        attn_sum.start(c)
        if c >= 1:
            attn_sum.middle(c - 1)
    attn_sum.middle(CHUNKS - 1)
    for c in range(CHUNKS):
        mine = slice(c * own, (c + 1) * own)
        middle = own_x[mine, :].astype(F32) + (attn_sum.finish(c) + row(V_OUTB))
        mid[mine, :] = middle
        normal, _ = normal_rows(middle)
        n2f[rows_at(c * chunk + at.spot * own, own), :] = (
            normal * row(V_LN2G) + row(V_LN2B)
        ).astype(BF)
        norm2_all.start(c)
        if c >= 1:
            norm2_all.forward(c - 1)
    norm2_all.forward(CHUNKS - 1)
    attn_sum.drain()
    for c in range(CHUNKS):
        norm2_all.finish(c)
        cot_all.finish(c)

        def feed(i, carry, c=c):
            here = rows_at(c * chunk + i * TILE, TILE, TILE)
            v = nn(n2f[here, :], wfc[...]) + row(V_FCB)
            scale = 0.7978845608028654
            square = v * v
            t = jnp.tanh(scale * v * (1.0 + 0.044715 * square))
            half = 0.5 * (1.0 + t)
            active = (v * half).astype(BF)
            slope = half + 0.5 * v * (1.0 - t * t) * (scale * (1.0 + 3.0 * 0.044715 * square))
            act[here, :] = active
            mlp_term[here, :] = nn(active, wproj[...]).astype(BF)
            low = (nt(cotf[here, :], wproj[...]) * slope).astype(BF)
            dhid[here, :] = low
            gvec[G_FCB : G_FCB + 1, :] += jnp.sum(low.astype(F32), axis=0, keepdims=True)
            term[here, :] = nt(low, wfc[...]).astype(BF)
            return carry

        lax.fori_loop(0, chunk // TILE, feed, 0)
        back_sum.start(c)
        if c >= 1:
            back_sum.middle(c - 1)
    back_sum.middle(CHUNKS - 1)

    def proj_grad(i, carry):
        here = rows_at(i * TILE, TILE, TILE)
        grads[here, :] = tn(act[:, here], cotf[...]).astype(BF)
        return carry

    lax.fori_loop(0, width // TILE, proj_grad, 0)
    for c in range(CHUNKS):
        mine = slice(c * own, (c + 1) * own)
        grad2 = back_sum.finish(c)
        normal, inv = normal_rows(mid[mine, :])
        dres = cotf[rows_at(c * chunk + at.spot * own, own), :].astype(F32)
        grad_mid = dres + norm_back(grad2, normal, inv, row(V_LN2G))
        low = grad_mid.astype(BF)
        dmid[mine, :] = grad_mid
        datf[rows_at(c * chunk + at.spot * own, own), :] = low
        dattn_all.start(c)
        for line, value in (
            (G_LN2G, grad2 * normal),
            (G_LN2B, grad2),
            (G_OUTB, low.astype(F32)),
            (G_PROJB, dres),
        ):
            gvec[line : line + 1, :] += jnp.sum(value, axis=0, keepdims=True)
        if c >= 1:
            dattn_all.forward(c - 1)
    dattn_all.forward(CHUNKS - 1)

    def fc_grad(i, carry):
        here = rows_at(i * TILE, TILE, TILE)
        there = rows_at(width + i * TILE, TILE, TILE)
        grads[there, :] = tn(n2f[:, here], dhid[...]).astype(BF)
        return carry

    lax.fori_loop(0, width // TILE, fc_grad, 0)
    for c in range(CHUNKS):
        dattn_all.finish(c)
    tok.drain()
    cot.drain()
    for each in gather:
        each.drain()
    back_sum.drain()


def backward_kernel(
    plan,
    wcol,
    wrow,
    first_key,
    vec,
    wqkv,
    wo,
    n1f,
    qkv_p,
    k_t,
    att_t,
    lse,
    att_w,
    datf,
    dmid,
    own_x,
    mid,
    mlp_term,
    grads,
    gvec,
    live,
    block_out,
    input_grad,
    mlp_total,
    out_total,
    qkv_total,
    vec_total,
    dout_w,
    dout_p,
    delta,
    out_part,
    qkv_part,
    dq_acc,
    dq_t,
    dv_p,
    dqkv_w,
    term,
    result,
    dx,
    near_a,
    stage_a,
    far_a,
    near_b,
    stage_b,
    far_b,
    landing,
    vec_s,
    vec_r,
    rs_s,
    rs_r,
    back_s,
    back_r,
    back_l,
    share_s,
    share_r,
    sum_s,
    sum_r,
    vec_ss,
    vec_sr,
):
    at = Place(plan)
    rows, width, pad = plan.rows, plan.width, plan.pad
    chunk, own = plan.chunk, plan.own
    entry_barrier(plan, at)
    dk_p = dout_w

    def row(i):
        return vec[i : i + 1, :]

    mlp_sum = Scatter(at, mlp_term, near_a, stage_a, far_a, (rs_s.at[0], rs_r.at[0]))
    norm_sum = Scatter(at, term, near_b, stage_b, far_b, (rs_s.at[1], rs_r.at[1]))
    out_way, grad_way = (
        Outgoing(
            at,
            ref,
            out,
            (back_s.at[i], back_r.at[i]),
            back_l.at[i],
            (share_s.at[i], share_r.at[i]),
        )
        for i, (ref, out) in enumerate(((result, block_out), (dx, input_grad)))
    )
    totals, room, index = [], 0, 0
    half = width
    for first, out in (
        (grads.at[0:half], mlp_total.at[0:half]),
        (grads.at[half : 2 * half], mlp_total.at[half : 2 * half]),
        (out_part, out_total),
        (qkv_part, qkv_total),
    ):
        totals.append(Total(at, first, out, landing, room, (sum_s, sum_r), index))
        room += landing_rows(first.shape[0], plan.n)
        index += total_sems(first.shape[0], plan.n)
    proj_sum, fc_sum, wo_sum, qkv_sum = totals

    for c in range(CHUNKS):
        mlp_sum.start(c)
    proj_sum.step()
    fc_sum.step()
    for c in range(CHUNKS):
        mlp_sum.middle(c)

    def back_out(i, carry):
        here = rows_at(i * TILE, TILE, TILE)
        dout_w[here, :] = nt(datf[here, :], wo[...]).astype(BF)
        return carry

    lax.fori_loop(0, rows // TILE, back_out, 0)

    def to_packed(i, carry):
        here = rows_at(i * TILE, TILE, TILE)
        moved = nn(pick(wcol[here, :], rows), dout_w[...])
        dout_p[here, :] = moved.astype(BF)
        flipped = moved.T
        both = flipped * att_t[:, here].astype(F32)
        for h in range(plan.heads):
            delta[h : h + 1, here] = jnp.sum(both[h * HD : (h + 1) * HD, :], axis=0, keepdims=True)
        return carry

    lax.fori_loop(0, rows // TILE, to_packed, 0)
    out_part[...] = tn(att_w[...], datf[...]).astype(BF)
    wo_sum.step()

    for c in range(CHUNKS):
        mine = slice(c * own, (c + 1) * own)
        outcome = mid[mine, :] + (mlp_sum.finish(c) + row(V_PROJB))
        result[mine, :] = jnp.where(live[mine, :] > 0.5, outcome, 0.0).astype(BF)
        out_way.start(c)

    dq_acc[...] = jnp.zeros_like(dq_acc)

    def attend_back(k0, queries):
        k_here = rows_at(k0, TILE, TILE)
        q_here = rows_at(k0, queries, TILE)
        first = first_key[0:1, q_here]
        key = k0 + lax.broadcasted_iota(jnp.int32, (TILE, queries), 0)
        query = k0 + lax.broadcasted_iota(jnp.int32, (TILE, queries), 1)
        seen = (key >= first) & (key <= query)
        parts = []
        for h in range(plan.heads):
            lanes = (h // 2) * LANES
            q_all = qkv_p[q_here, pl.ds(lanes, LANES)]
            do_all = dout_p[q_here, pl.ds(lanes, LANES)]
            kh = head_lanes(qkv_p[k_here, pl.ds(pad + lanes, LANES)], h % 2 == 1)
            vh = head_lanes(qkv_p[k_here, pl.ds(2 * pad + lanes, LANES)], h % 2 == 1)
            expo = jnp.exp2(nt(kh, q_all) * LOG2E - lse[h : h + 1, q_here])
            prob = jnp.where(seen, expo, 0.0)
            slope = prob * (nt(vh, do_all) - delta[h : h + 1, q_here])
            low = slope.astype(BF)
            dv = nn(prob.astype(BF), do_all)
            dk = nn(low, q_all)
            dq_acc[h * HD : (h + 1) * HD, q_here] += nn(k_t[h * HD : (h + 1) * HD, k_here], low)
            parts.append((dk, dv))
        for h in range(0, plan.heads, 2):
            lanes = pl.ds((h // 2) * LANES, LANES)
            for i, ref in enumerate((dk_p, dv_p)):
                value = head_lanes(parts[h][i], False)
                if h + 1 < plan.heads:
                    value = value + head_lanes(parts[h + 1][i], True)
                ref[k_here, lanes] = value.astype(BF)

    reach = min(rows, WINDOW + TILE)
    full = (rows - reach) // TILE + 1

    def attend_full(i, carry):
        attend_back(i * TILE, reach)
        return carry

    lax.fori_loop(0, full // 2, attend_full, 0)
    proj_sum.step()
    fc_sum.step()
    for part in range(plan.split):
        out_way.share(part)
    lax.fori_loop(full // 2, full, attend_full, 0)
    proj_sum.step()
    fc_sum.step()
    wo_sum.step()
    for part in range(plan.split):
        out_way.forward(part)
    for i in range(full, rows // TILE):
        attend_back(i * TILE, rows - i * TILE)
    proj_sum.step()
    fc_sum.step()
    wo_sum.step()
    dq_t[...] = dq_acc[...].astype(BF)
    for c in range(CHUNKS):

        def back_project(i, carry, c=c):
            start = c * chunk + i * TILE
            here = rows_at(start, TILE, TILE)
            hot = pick_rows(wrow[...], start, TILE)
            dq = nt(hot, dq_t[...])
            dk = nn(hot, dk_p[...])
            dv = nn(hot, dv_p[...])
            for j, value in enumerate((dq, dk, dv)):
                dqkv_w[here, j * pad : (j + 1) * pad] = value.astype(BF)
            sums = [jnp.sum(value, axis=0, keepdims=True) for value in (dq, dk, dv)]
            vec_s[0, G_QKVB : G_QKVB + 1, :] += jnp.concatenate(sums, axis=1)
            term[here, :] = nt(dqkv_w[here, :], wqkv[...]).astype(BF)
            return carry

        if c == 0:
            vec_s[0, :, :] = gvec[...]
        lax.fori_loop(0, chunk // TILE, back_project, 0)
        norm_sum.start(c)
        if c >= 1:
            norm_sum.middle(c - 1)
    norm_sum.middle(CHUNKS - 1)

    def qkv_grad(i, carry):
        here = rows_at(i * TILE, TILE, TILE)
        qkv_part[here, :] = tn(n1f[:, here], dqkv_w[...]).astype(BF)
        return carry

    lax.fori_loop(0, width // TILE, qkv_grad, 0)
    qkv_sum.step()
    proj_sum.step()
    fc_sum.step()
    wo_sum.step()
    for c in range(CHUNKS):
        mine = slice(c * own, (c + 1) * own)
        grad1 = norm_sum.finish(c)
        normal, inv = normal_rows(own_x[mine, :].astype(F32))
        dx[mine, :] = (dmid[mine, :] + norm_back(grad1, normal, inv, row(V_LN1G))).astype(BF)
        grad_way.start(c)
        for line, value in ((G_LN1G, grad1 * normal), (G_LN1B, grad1)):
            vec_s[0, line : line + 1, :] += jnp.sum(value, axis=0, keepdims=True)
        if c % 2 == 1:
            qkv_sum.step()

    hops = [({"mp": at.mate}, True), ({"mp": at.across}, True)]
    bit = 1
    while bit < plan.n:
        high = lax.rem(at.d // bit, 2)
        hops.append(({"dp": at.d + (1 - 2 * high) * bit}, False))
        bit *= 2
    line = lax.broadcasted_iota(jnp.int32, (8, width), 0)
    vec_copies = []

    def vec_step(i):
        device, shared = hops[i]
        copy = send(vec_s.at[i], vec_r.at[i], (vec_ss, vec_sr), i, device)
        return copy, shared

    def vec_end(i, copy, shared):
        copy.wait()
        new = vec_r[i, :, :]
        if shared:
            new = jnp.where(line < SHARED, new, 0.0)
        value = vec_s[i, :, :] + new
        if i + 1 < len(hops):
            vec_s[i + 1, :, :] = value
        else:
            vec_total[...] = value

    state = vec_step(0)
    more = []
    for part in range(plan.split):
        more.append(functools.partial(grad_way.share, part))
    for part in range(plan.split):
        more.append(functools.partial(grad_way.forward, part))
    at_hop = 0
    for job in more:
        job()
        if at_hop < len(hops):
            vec_end(at_hop, *state)
            at_hop += 1
            if at_hop < len(hops):
                state = vec_step(at_hop)
        for each in totals:
            each.step()
    while at_hop < len(hops):
        vec_end(at_hop, *state)
        at_hop += 1
        if at_hop < len(hops):
            state = vec_step(at_hop)
    while any([each.step() for each in totals]):
        pass
    for part in range(plan.split):
        out_way.finish(part)
        grad_way.finish(part)
    out_way.drain()
    grad_way.drain()
    mlp_sum.drain()
    norm_sum.drain()


def body(
    tokens,
    cotangent,
    seq_lengths,
    source_slot,
    ln1_gain,
    ln1_bias,
    qkv_weight,
    qv_bias,
    output_projection_weight,
    out_bias,
    ln2_gain,
    ln2_bias,
    fc_weight,
    fc_bias,
    proj_weight,
    proj_bias,
):
    rows, width = tokens.shape
    span = qkv_weight.shape[2]
    n, members = lax.axis_size("dp"), lax.axis_size("mp")
    plan = Plan(n, members, rows, width, span // HD)
    pad = plan.pad
    hidden = fc_weight.shape[1]

    windex = plan.work_index(source_slot)
    wcol, wrow = windex[:, None], windex[None, :]
    position = jnp.arange(rows, dtype=jnp.int32)
    l0, l1 = seq_lengths[0, 0], seq_lengths[0, 0] + seq_lengths[0, 1]
    first_key = jnp.where(position >= l1, l1, jnp.where(position >= l0, l0, 0))[None, :].astype(jnp.int32)

    def widen(x):
        return jnp.pad(x, [(0, 0)] * (x.ndim - 1) + [(0, pad - span)])

    scale = jnp.array([HD**-0.5, 1.0, 1.0], BF)
    wqkv = widen(qkv_weight * scale[None, :, None]).reshape(width, 3 * pad)
    wo = jnp.pad(output_projection_weight, [(0, pad - span), (0, 0)])
    qkv_bias = widen(
        jnp.stack([qv_bias[0].astype(F32) * HD**-0.5, jnp.zeros_like(qv_bias[0], F32), qv_bias[1].astype(F32)])
    ).reshape(3 * pad)
    vec = jnp.stack(
        [
            v.astype(F32)
            for v in (ln1_gain, ln1_bias, out_bias, ln2_gain, ln2_bias, proj_bias, fc_bias, qkv_bias)
        ]
    )
    vm = pl.BlockSpec(memory_space=pltpu.VMEM)
    hbm = pl.BlockSpec(memory_space=pl.ANY)
    shape = jax.ShapeDtypeStruct
    quarter = rows // members
    dma = pltpu.SemaphoreType.DMA
    (
        n1f,
        qkv_p,
        k_t,
        att_t,
        lse,
        att_w,
        datf,
        dmid,
        own_x,
        mid,
        mlp_term,
        grads,
        gvec,
        live,
    ) = pl.pallas_call(
        functools.partial(forward_kernel, plan),
        out_shape=(
            shape((rows, width), BF),
            shape((rows, 3 * pad), BF),
            shape((pad, rows), BF),
            shape((pad, rows), BF),
            shape((8, rows), F32),
            shape((rows, pad), BF),
            shape((rows, width), BF),
            shape((quarter, width), F32),
            shape((quarter, width), BF),
            shape((quarter, width), F32),
            shape((rows, width), BF),
            shape((2 * width, width), BF),
            shape((8, width), F32),
            shape((quarter, 1), F32),
        ),
        in_specs=[hbm, hbm] + [vm] * 8,
        out_specs=(vm,) * 14,
        scratch_shapes=[
            pltpu.VMEM((rows, width), BF),
            pltpu.VMEM((rows, 3 * pad), BF),
            pltpu.VMEM((pad, rows), BF),
            pltpu.VMEM((rows, width), BF),
            pltpu.VMEM((rows, width), BF),
            pltpu.VMEM((rows, hidden), BF),
            pltpu.VMEM((rows, hidden), BF),
        ]
        + [
            pltpu.VMEM((2 * quarter, width), BF),
            pltpu.VMEM((quarter, width), BF),
            pltpu.VMEM((quarter, width), BF),
        ]
        * 2
        + [
            dma((plan.split, n)),
            dma((CHUNKS, plan.in_chunk)),
            dma((plan.split, n)),
            dma((CHUNKS, plan.in_chunk)),
            dma((4, CHUNKS, 3)),
            dma((4, CHUNKS, 3)),
            dma((2, CHUNKS, 2)),
            dma((2, CHUNKS, 2)),
        ],
        compiler_params=pltpu.CompilerParams(
            collective_id=0, has_side_effects=True, vmem_limit_bytes=VMEM_LIMIT
        ),
        name="forward",
    )(tokens, cotangent, wcol, wrow, first_key, vec, wqkv, wo, fc_weight, proj_weight)

    parts = (width, width, pad, width)
    landing = sum(landing_rows(r, n) for r in parts)
    sems = sum(total_sems(r, n) for r in parts)
    hops = 2 + (n - 1).bit_length()
    block_out, input_grad, mlp_total, out_total, qkv_total, vec_total = pl.pallas_call(
        functools.partial(backward_kernel, plan),
        out_shape=(
            shape((rows, width), BF),
            shape((rows, width), BF),
            shape((2 * width, width), BF),
            shape((pad, width), BF),
            shape((width, 3 * pad), BF),
            shape((8, width), F32),
        ),
        in_specs=[vm] * 20,
        out_specs=(hbm, hbm, vm, vm, vm, vm),
        scratch_shapes=[
            pltpu.VMEM((rows, pad), BF),
            pltpu.VMEM((rows, pad), BF),
            pltpu.VMEM((8, rows), F32),
            pltpu.VMEM((pad, width), BF),
            pltpu.VMEM((width, 3 * pad), BF),
            pltpu.VMEM((pad, rows), F32),
            pltpu.VMEM((pad, rows), BF),
            pltpu.VMEM((rows, pad), BF),
            pltpu.VMEM((rows, 3 * pad), BF),
            pltpu.VMEM((rows, width), BF),
            pltpu.VMEM((quarter, width), BF),
            pltpu.VMEM((quarter, width), BF),
        ]
        + [
            pltpu.VMEM((2 * quarter, width), BF),
            pltpu.VMEM((quarter, width), BF),
            pltpu.VMEM((quarter, width), BF),
        ]
        * 2
        + [
            pltpu.VMEM((landing, width), BF),
            pltpu.VMEM((hops, 8, width), F32),
            pltpu.VMEM((hops, 8, width), F32),
            dma((2, CHUNKS, 2)),
            dma((2, CHUNKS, 2)),
            dma((2, CHUNKS, plan.in_chunk)),
            dma((2, plan.split, n)),
            dma((2, plan.split)),
            dma((2, 3, plan.split, n)),
            dma((2, 3, plan.split, n)),
            dma((sems,)),
            dma((sems,)),
            dma((hops,)),
            dma((hops,)),
        ],
        compiler_params=pltpu.CompilerParams(
            collective_id=1, has_side_effects=True, vmem_limit_bytes=VMEM_LIMIT
        ),
        name="backward",
    )(
        wcol,
        wrow,
        first_key,
        vec,
        wqkv,
        wo,
        n1f,
        qkv_p,
        k_t,
        att_t,
        lse,
        att_w,
        datf,
        dmid,
        own_x,
        mid,
        mlp_term,
        grads,
        gvec,
        live,
    )
    qkv_grad = qkv_total.reshape(width, 3, pad)[:, :, :span].astype(F32) * scale.astype(F32)[None, :, None]
    qkv_sums = vec_total[G_QKVB].reshape(3, pad)[:, :span]
    return (
        block_out,
        input_grad,
        vec_total[G_LN1G],
        vec_total[G_LN1B],
        qkv_grad,
        jnp.stack([qkv_sums[0] * HD**-0.5, qkv_sums[2]]),
        out_total[:span].astype(F32),
        vec_total[G_OUTB],
        vec_total[G_LN2G],
        vec_total[G_LN2B],
        mlp_total[width:].astype(F32),
        vec_total[G_FCB],
        mlp_total[:width].astype(F32),
        vec_total[G_PROJB],
    )


def solution(mesh):
    return jax.shard_map(
        body,
        mesh=mesh,
        in_specs=(
            P("dp", None),
            P("dp", None),
            P("dp", None),
            P("dp"),
            P(),
            P(),
            P(None, None, "mp"),
            P(None, "mp"),
            P("mp", None),
            P(),
            P(),
            P(),
            P(None, "mp"),
            P("mp"),
            P("mp", None),
            P(),
        ),
        out_specs=(
            P("dp", None),
            P("dp", None),
            P(),
            P(),
            P(None, None, "mp"),
            P(None, "mp"),
            P("mp", None),
            P(),
            P(),
            P(),
            P(None, "mp"),
            P("mp"),
            P("mp", None),
            P(),
        ),
        check_vma=False,
    )
```

```python
import functools

import jax
import jax.numpy as jnp
from jax import lax
from jax.experimental import pallas as pl
from jax.experimental.pallas import tpu as pltpu
from jax.sharding import PartitionSpec as P

MESH = pl.DeviceIdType.MESH
BF = jnp.bfloat16
F32 = jnp.float32
HD = 64
EPSILON = 1e-05
NEG = -1e30
LOG2E = 1.4426950408889634
TILE = 256
HALVES = 2
CHUNKS = 4
LANES = 128
VMEM_LIMIT = 60 * 2**20


class Plan:
    def __init__(self, n, members, rows, width, heads):
        self.n, self.members, self.rows, self.width, self.heads = n, members, rows, width, heads
        self.slots = rows // n
        self.group = max(1, (16 * members) // self.slots)
        self.share = self.group * self.slots // members
        self.groups = n // self.group
        self.chunk = rows // CHUNKS
        self.own = self.chunk // members
        self.take = max(16, self.share // CHUNKS)
        self.split = self.share // self.take
        self.in_chunk = self.own // self.take
        self.seq = rows // 2
        self.half = self.seq // HALVES
        self.part = self.half // 2
        self.pad = -(-heads * HD // LANES) * LANES

    def work_index(self, slot_ids):
        source, slot = slot_ids // self.slots, slot_ids % self.slots
        grp = source // self.group
        inside = (source % self.group) * self.slots + slot
        owner, row = inside // self.share, inside % self.share
        chunk = (grp // self.in_chunk) * self.split + row // self.take
        place = (owner % 2) * (self.members // 2) + owner // 2
        index = chunk * self.chunk + place * self.own + (grp % self.in_chunk) * self.take + row % self.take
        return jnp.where(slot_ids >= self.rows, -1, index).astype(jnp.int32)


def nn(a, b):
    return lax.dot_general(a, b, (((1,), (0,)), ((), ())), preferred_element_type=F32)


def nt(a, b):
    return lax.dot_general(a, b, (((1,), (1,)), ((), ())), preferred_element_type=F32)


def tn(a, b):
    return lax.dot_general(a, b, (((0,), (0,)), ((), ())), preferred_element_type=F32)


def rows_at(start, count, step=16):
    if not isinstance(start, int):
        start = pl.multiple_of(start, step)
    return pl.ds(start, count)


class Place:
    def __init__(self, plan):
        self.plan = plan
        self.d = lax.axis_index("dp")
        self.m = lax.axis_index("mp")
        self.core = lax.rem(self.m, 2)
        self.side = self.m // 2
        self.mate = self.m + 1 - 2 * self.core
        self.across = lax.rem(self.m + 2, plan.members)
        self.spot = self.core * 2 + self.side

    def mine(self, c, flip=False):
        core = 1 - self.core if flip else self.core
        return (2 * c + core) * self.plan.part

    def spot_of(self, core_flip, side_flip):
        core = 1 - self.core if core_flip else self.core
        side = 1 - self.side if side_flip else self.side
        return core * 2 + side

    def member(self, core_flip, side_flip):
        core = 1 - self.core if core_flip else self.core
        side = 1 - self.side if side_flip else self.side
        return side * 2 + core


def send(src, dst, sems, index, device):
    copy = pltpu.make_async_remote_copy(
        src_ref=src,
        dst_ref=dst,
        send_sem=sems[0].at[index],
        recv_sem=sems[1].at[index],
        device_id=device,
        device_id_type=MESH,
    )
    copy.start()
    return copy


def landed(dst, sems, index, device):
    pltpu.make_async_remote_copy(
        src_ref=dst,
        dst_ref=dst,
        send_sem=sems[0].at[index],
        recv_sem=sems[1].at[index],
        device_id=device,
        device_id_type=MESH,
    ).wait_recv()


def left(src, sems, index, device):
    pltpu.make_async_remote_copy(
        src_ref=src,
        dst_ref=src,
        send_sem=sems[0].at[index],
        recv_sem=sems[1].at[index],
        device_id=device,
        device_id_type=MESH,
    ).wait_send()


def entry_barrier(plan, at):
    barrier = pltpu.get_barrier_semaphore()

    def signal(j, carry):
        pl.semaphore_signal(
            barrier, inc=1, device_id={"dp": lax.rem(at.d + j, plan.n)}, device_id_type=MESH
        )
        return carry

    lax.fori_loop(1, plan.n, signal, 0)
    pl.semaphore_signal(barrier, inc=1, device_id={"mp": at.mate}, device_id_type=MESH)
    pl.semaphore_signal(barrier, inc=1, device_id={"mp": at.across}, device_id_type=MESH)
    pl.semaphore_wait(barrier, plan.n + 1)


class Gather:
    def __init__(self, at, buf, sems):
        self.at, self.buf, self.sems, self.copies = at, buf, sems, []

    def rows(self, c, core_flip=False, side_flip=False):
        plan = self.at.plan
        start = c * plan.chunk + self.at.spot_of(core_flip, side_flip) * plan.own
        return self.buf.at[rows_at(start, plan.own)]

    def start(self, c):
        mine = self.rows(c)
        self.copies.append(send(mine, mine, self.sems, (c, 1), {"mp": self.at.across}))
        self.copies.append(send(mine, mine, self.sems, (c, 0), {"mp": self.at.mate}))

    def forward(self, c):
        theirs = self.rows(c, side_flip=True)
        landed(theirs, self.sems, (c, 1), {"mp": self.at.across})
        self.copies.append(send(theirs, theirs, self.sems, (c, 2), {"mp": self.at.mate}))

    def finish(self, c):
        landed(self.rows(c, core_flip=True), self.sems, (c, 0), {"mp": self.at.mate})
        landed(self.rows(c, core_flip=True, side_flip=True), self.sems, (c, 2), {"mp": self.at.mate})

    def drain(self):
        for copy in self.copies:
            copy.wait_send()
        self.copies = []


class MateGather:
    def __init__(self, at, buf, sems):
        self.at, self.buf, self.sems, self.copies = at, buf, sems, []

    def mine(self, c):
        return rows_at(self.at.mine(c), self.at.plan.part)

    def start(self, c):
        here = self.buf.at[self.mine(c)]
        self.copies.append(send(here, here, self.sems, c, {"mp": self.at.mate}))

    def finish(self, c):
        there = self.buf.at[rows_at(self.at.mine(c, True), self.at.plan.part)]
        landed(there, self.sems, c, {"mp": self.at.mate})

    def drain(self):
        for copy in self.copies:
            copy.wait_send()
        self.copies = []


class MateSum:
    def __init__(self, at, term, land, sems):
        self.at, self.term, self.land, self.sems, self.copies = at, term, land, sems, []

    def start(self, c):
        plan, at = self.at.plan, self.at
        src = self.term.at[rows_at(at.mine(c, True), plan.part)]
        dst = self.land.at[rows_at(c * plan.part, plan.part)]
        self.copies.append(send(src, dst, self.sems, c, {"mp": at.mate}))

    def finish(self, c):
        plan, at = self.at.plan, self.at
        where = rows_at(c * plan.part, plan.part)
        landed(self.land.at[where], self.sems, c, {"mp": at.mate})
        mine = self.term[rows_at(at.mine(c), plan.part), :]
        return mine.astype(F32) + self.land[where, :].astype(F32)

    def drain(self):
        for copy in self.copies:
            copy.wait_send()
        self.copies = []


class AcrossSum:
    def __init__(self, at, part, far, out, sems):
        self.at, self.part, self.far, self.out, self.sems, self.copies = at, part, far, out, sems, []

    def start(self, c):
        plan, at = self.at.plan, self.at
        src = self.part.at[rows_at((2 * c + 1 - at.side) * plan.own, plan.own)]
        dst = self.far.at[rows_at(c * plan.own, plan.own)]
        self.copies.append(send(src, dst, self.sems, c, {"mp": at.across}))

    def finish(self, c):
        plan, at = self.at.plan, self.at
        where = rows_at(c * plan.own, plan.own)
        landed(self.far.at[where], self.sems, c, {"mp": at.across})
        mine = self.part[rows_at((2 * c + at.side) * plan.own, plan.own), :]
        self.out[where, :] = (mine.astype(F32) + self.far[where, :].astype(F32)).astype(BF)

    def drain(self):
        for copy in self.copies:
            copy.wait_send()
        self.copies = []


class Incoming:
    def __init__(self, at, source, sems, landing):
        plan = at.plan
        self.at, self.source, self.sems, self.landing = at, source, sems, landing
        self.offset = lax.rem(at.m * plan.share, plan.slots)
        self.sends = None
        if plan.group > 1:
            self.sends = lax.rem(at.d, plan.group) == (at.m * plan.share) // plan.slots

    def guarded(self, run):
        if self.sends is None:
            run()
        else:
            pl.when(self.sends)(run)

    def mine(self, part):
        plan, at = self.at.plan, self.at
        grp = at.d // plan.group
        return (grp // plan.in_chunk) * plan.split + part, lax.rem(grp, plan.in_chunk)

    def piece(self, k, part):
        plan = self.at.plan
        start = k * plan.slots + self.offset + part * plan.take
        return self.source.at[rows_at(start, plan.take)]

    def start(self, part):
        plan, at = self.at.plan, self.at
        c, gi = self.mine(part)

        def one(j, carry):
            k = lax.rem(at.d + j, plan.n)
            pltpu.make_async_remote_copy(
                src_ref=self.piece(k, part),
                dst_ref=self.landing(c, gi),
                send_sem=self.sems[0].at[part, j],
                recv_sem=self.sems[1].at[c, gi],
                device_id={"dp": k},
                device_id_type=MESH,
            ).start()
            return carry

        def run():
            lax.fori_loop(1, plan.n, one, 0)
            pltpu.make_async_copy(
                self.piece(at.d, part), self.landing(c, gi), self.sems[1].at[c, gi]
            ).start()

        self.guarded(run)

    def wait(self, c):
        plan, at = self.at.plan, self.at

        def one(gi, carry):
            landed(self.landing(c, gi), (self.sems[1], self.sems[1]), (c, gi), {"dp": at.d})
            return carry

        lax.fori_loop(0, plan.in_chunk, one, 0)

    def drain(self):
        plan, at = self.at.plan, self.at

        def run():
            for part in range(plan.split):

                def one(j, carry, part=part):
                    k = lax.rem(at.d + j, plan.n)
                    left(self.piece(k, part), (self.sems[0], self.sems[0]), (part, j), {"dp": k})
                    return carry

                lax.fori_loop(1, plan.n, one, 0)

        self.guarded(run)


class Outgoing:
    def __init__(self, at, rows_ref, out, sems, local_sem, share_sems):
        plan = at.plan
        self.at, self.rows_ref, self.out = at, rows_ref, out
        self.sems, self.local_sem, self.share_sems = sems, local_sem, share_sems

    def holds(self, member):
        plan = self.at.plan
        if plan.group == 1:
            return None
        return lax.rem(self.at.d, plan.group) == (member * plan.share) // plan.slots

    def guarded(self, member, run):
        if self.at.plan.group == 1:
            run()
        else:
            pl.when(self.holds(member))(run)

    def place(self, k, part, member):
        plan = self.at.plan
        start = k * plan.slots + lax.rem(member * plan.share, plan.slots) + part * plan.take
        return self.out.at[rows_at(start, plan.take)]

    def each(self, c, remote, local):
        plan, at = self.at.plan, self.at
        part = c % plan.split

        def one(gi, carry):
            grp = (c // plan.split) * plan.in_chunk + gi
            dest = grp * plan.group + (at.m * plan.share) // plan.slots
            src = self.rows_ref.at[rows_at(c * plan.own + gi * plan.take, plan.take)]
            dst = self.place(at.d, part, at.m)
            pl.when(dest != at.d)(lambda: remote(gi, part, src, dst, dest))
            pl.when(dest == at.d)(lambda: local(gi, part, src, dst))
            return carry

        lax.fori_loop(0, plan.in_chunk, one, 0)

    def copy(self, c, gi, part, src, dst, dest):
        return pltpu.make_async_remote_copy(
            src_ref=src,
            dst_ref=dst,
            send_sem=self.sems[0].at[c, gi],
            recv_sem=self.sems[1].at[part, self.at.d],
            device_id={"dp": dest},
            device_id_type=MESH,
        )

    def start(self, c):
        def local(gi, part, src, dst):
            pltpu.make_async_copy(src, dst, self.local_sem.at[part]).start()

        self.each(c, lambda gi, part, src, dst, dest: self.copy(c, gi, part, src, dst, dest).start(), local)

    def drain(self):
        for c in range(CHUNKS):
            self.each(
                c,
                lambda gi, part, src, dst, dest: self.copy(c, gi, part, src, dst, dest).wait_send(),
                lambda gi, part, src, dst: None,
            )

    def loop(self, part, run):
        lax.fori_loop(0, self.at.plan.n, lambda k, carry: (run(k), carry)[1], 0)

    def share(self, part):
        at = self.at

        def run():
            def one(k):
                here = self.place(k, part, at.m)

                def remote():
                    landed(here, (self.sems[1], self.sems[1]), (part, k), {"dp": at.d})

                def local():
                    pltpu.make_async_copy(here, here, self.local_sem.at[part]).wait()

                pl.when(k != at.d)(remote)
                pl.when(k == at.d)(local)
                send(here, here, self.share_sems, (1, part, k), {"mp": at.across})
                send(here, here, self.share_sems, (0, part, k), {"mp": at.mate})

            self.loop(part, one)

        self.guarded(at.m, run)

    def forward(self, part):
        at = self.at

        def run():
            def one(k):
                there = self.place(k, part, at.across)
                landed(there, self.share_sems, (1, part, k), {"mp": at.across})
                send(there, there, self.share_sems, (2, part, k), {"mp": at.mate})

            self.loop(part, one)

        self.guarded(at.across, run)

    def finish(self, part):
        at = self.at
        corner = at.member(True, True)

        def near():
            self.loop(
                part,
                lambda k: landed(
                    self.place(k, part, at.mate), self.share_sems, (0, part, k), {"mp": at.mate}
                ),
            )

        def far():
            self.loop(
                part,
                lambda k: landed(
                    self.place(k, part, corner), self.share_sems, (2, part, k), {"mp": at.mate}
                ),
            )

        def sent():
            def one(k):
                here = self.place(k, part, at.m)
                left(here, self.share_sems, (1, part, k), {"mp": at.across})
                left(here, self.share_sems, (0, part, k), {"mp": at.mate})

            self.loop(part, one)

        def passed():
            self.loop(
                part,
                lambda k: left(
                    self.place(k, part, at.across), self.share_sems, (2, part, k), {"mp": at.mate}
                ),
            )

        self.guarded(at.mate, near)
        self.guarded(corner, far)
        self.guarded(at.m, sent)
        self.guarded(at.across, passed)


def halvings(rows, n, order):
    steps, size = [], rows
    bits = [1 << i for i in range((n - 1).bit_length())]
    for i in order:
        bits.insert(0, bits.pop(i))
    for bit in bits:
        if size % 32 == 0:
            size //= 2
            steps.append((bit, True, size))
        else:
            steps.append((bit, False, size))
    return steps


def trail_of(at, rows, order):
    offset, trail, size = 0, [], rows
    for bit, halve, size in halvings(rows, at.plan.n, order):
        if halve:
            high = lax.rem(at.d // bit, 2)
            partner = {"dp": at.d + (1 - 2 * high) * bit}
            trail.append((offset, offset + high * size, size, partner))
            offset = offset + high * size
    return offset, size, trail


class Steps:
    def __init__(self, *runs):
        self.runs, self.next = list(runs), 0

    def step(self):
        if self.next < len(self.runs):
            self.next += 1
            self.runs[self.next - 1]()

    def finish(self):
        while self.next < len(self.runs):
            self.step()


class Stepped:
    def __init__(self):
        self.jobs, self.next, self.pending = [], 0, None

    def step(self):
        if self.pending is not None:
            self.pending[0](self.pending[1])
            self.pending = None
        if self.next < len(self.jobs):
            start, end = self.jobs[self.next]
            self.next += 1
            self.pending = (end, start())

    def finish(self):
        while self.pending is not None or self.next < len(self.jobs):
            self.step()

    def spread(self, buf, keep, other, size, sems, index, partner, source=None, before_end=None):
        def start():
            here = buf.at[rows_at(keep, size)]
            return send(here if source is None else source, here, sems, index, partner)

        def end(copy):
            copy.wait_send()
            landed(buf.at[rows_at(other, size)], sems, index, partner)
            if before_end is not None:
                before_end()

        self.jobs.append((start, end))


class Weights(Stepped):
    def __init__(self, at, source, dst, sems, index, order=()):
        super().__init__()
        rows = source.shape[0]
        offset, size, trail = trail_of(at, rows, order)
        slice_rows = rows_at(offset, size)
        across = {"mp": at.across}

        def start():
            return send(source.at[slice_rows], dst.at[slice_rows], sems, index, across)

        def end(copy):
            copy.wait_send()
            landed(dst.at[slice_rows], sems, index, across)

        self.jobs.append((start, end))
        for i, (before, keep, length, partner) in enumerate(reversed(trail)):
            self.spread(dst, keep, 2 * before + length - keep, length, sems, index + 1 + i, partner)


class Total(Stepped):
    def __init__(self, at, first, origins, out, landing, base, sems, index, order, early):
        super().__init__()
        self.at, self.landing = at, landing
        rows, n = out.shape[0], at.plan.n
        steps = halvings(rows, n, order)
        room = sum(size for _, _, size in steps)
        sources = [(first, origin) for origin in origins]
        if early:
            self.cross(sources, base, rows, (sems, index))
            sources, index, base = [(landing, base)], index + 1, base + rows
        lands = [base + i * room for i in range(len(sources))]
        for bit, halve, size in steps:
            high = lax.rem(at.d // bit, 2)
            partner = {"dp": at.d + (1 - 2 * high) * bit}
            keep = high * size if halve else 0
            give = (1 - high) * size if halve else 0
            self.exchange(sources, give, keep, size, list(lands), (sems, index), partner)
            index += len(sources)
            sources = [(landing, land) for land in lands]
            lands = [land + size for land in lands]
        offset, size, trail = trail_of(at, rows, order)
        if not early:
            self.cross(sources, base + 2 * room, size, (sems, index))
            sources, index = [(landing, base + 2 * room)], index + 1
        done = landing.at[rows_at(sources[0][1], size)]
        local = pltpu.make_async_copy(done, out.at[rows_at(offset, size)], sems[0].at[index])
        self.jobs[-1] = (self.jobs[-1][0], self.then(self.jobs[-1][1], local.start))
        index += 1
        for i, (before, keep, length, partner) in enumerate(reversed(trail)):
            source, settle = (done, local.wait) if i == 0 else (None, None)
            self.spread(
                out, keep, 2 * before + length - keep, length, sems, index + i, partner, source, settle
            )

    def then(self, end, more):
        def both(copy):
            end(copy)
            more()

        return both

    def add(self, first, origin, land, size):
        step = 96 if size % 96 == 0 else (32 if size % 32 == 0 else 16)

        def one(i, carry):
            here = rows_at(origin + i * step, step)
            there = rows_at(land + i * step, step)
            value = first[here, :].astype(F32) + self.landing[there, :].astype(F32)
            self.landing[there, :] = value.astype(BF)
            return carry

        lax.fori_loop(0, size // step, one, 0)

    def exchange(self, sources, give, keep, size, lands, sems, partner):
        sems, index = sems

        def start():
            return [
                send(
                    ref.at[rows_at(origin + give, size)],
                    self.landing.at[rows_at(land, size)],
                    sems,
                    index + i,
                    partner,
                )
                for i, ((ref, origin), land) in enumerate(zip(sources, lands))
            ]

        def end(copies):
            for copy, (ref, origin), land in zip(copies, sources, lands):
                copy.wait()
                self.add(ref, origin + keep, land, size)

        self.jobs.append((start, end))

    def cross(self, sources, land, size, sems):
        sems, index = sems
        (mine, mine_at), (theirs, theirs_at) = sources

        def start():
            return send(
                theirs.at[rows_at(theirs_at, size)],
                self.landing.at[rows_at(land, size)],
                sems,
                index,
                {"mp": self.at.across},
            )

        def end(copy):
            copy.wait()
            self.add(mine, mine_at, land, size)

        self.jobs.append((start, end))


def total_room(rows, n, early):
    steps = halvings(rows, n, ())
    size, spreads = steps[-1][2], sum(1 for _, halve, _ in steps if halve)
    room, groups = sum(step[2] for step in steps), 1 if early else 2
    return groups * room + (rows if early else size), groups * len(steps) + 2 + spreads


def weight_sems(rows, n):
    return 1 + sum(1 for _, halve, _ in halvings(rows, n, ()) if halve)


def normal_rows(x):
    centered = x - jnp.mean(x, axis=-1, keepdims=True)
    inv = lax.rsqrt(jnp.mean(centered * centered, axis=-1, keepdims=True) + EPSILON)
    return centered * inv, inv


def norm_back(grad, normal, inv, gain):
    scaled = grad * gain
    return inv * (
        scaled
        - jnp.mean(scaled, axis=-1, keepdims=True)
        - normal * jnp.mean(scaled * normal, axis=-1, keepdims=True)
    )


def pick(index_col, count):
    lanes = lax.broadcasted_iota(jnp.int32, (index_col.shape[0], count), 1)
    return jnp.where(lanes == index_col, 1.0, 0.0).astype(BF)


def pick_rows(index_row, first, count):
    lines = lax.broadcasted_iota(jnp.int32, (count, index_row.shape[1]), 0) + first
    return jnp.where(lines == index_row, 1.0, 0.0).astype(BF)


def head_lanes(x, odd):
    lane = lax.broadcasted_iota(jnp.int32, x.shape, 1)
    return jnp.where((lane >= HD) == odd, x, jnp.zeros_like(x))


V_LN1G, V_LN1B, V_OUTB, V_LN2G, V_LN2B, V_PROJB, V_FCB, V_QKVB = range(8)
G_LN1G, G_LN1B, G_LN2G, G_LN2B, G_OUTB, G_PROJB, G_FCB, G_QKVB, G_FCB2, G_QKVB2 = range(10)
SHARED = 6
MOVES = (("a", ()), ("f", ()), ("p", (1,)))
TOTALS = (
    ("P", "P", 0, (), False),
    ("Q", "P", 1, (1,), False),
    ("F", "F", 0, (), True),
    ("G", "F", 1, (), True),
    ("A", "A", 0, (1,), True),
    ("B", "A", 1, (), True),
)
SCHEDULE = (
    "pfa0p1f2030112a23p34567",
    "",
    "",
    "f",
    "ap",
    "",
    "454645756f6a",
    "7",
    "",
    "",
    "7",
    "",
    "",
    "fp",
    "",
    "",
    "",
    "",
    "",
    "",
    "",
    "",
    "PQ",
    "",
    "",
    "F",
    "",
    "PQ",
    "",
    "F",
    "GP",
    "",
    "QFijGFklivPjGrFsktluFPGrsAFPtuGPBAQGivQBijABjkAk",
    "GlBQlArrBsAsQtBtuvvuvAB",
)
TAIL = 2
GLINES = 16
GELU = 0.7978845608028654
CUBE = 0.044715


class VecTotal(Stepped):
    def __init__(self, hops, given, taken, out, sems):
        super().__init__()
        line = lax.broadcasted_iota(jnp.int32, (8, out.shape[1]), 0)
        for i, device in enumerate(hops):

            def start(i=i, device=device):
                return send(given.at[i], taken.at[i], sems, i + 1, device)

            def end(copy, i=i):
                copy.wait()
                low, high = taken[i, 0:8, :], taken[i, 8:16, :]
                if i == 0:
                    low, high = jnp.where(line < SHARED, low, 0.0), jnp.zeros_like(high)
                elif i == 1:
                    low = jnp.concatenate([low[0:SHARED, :], high[0:2, :]], axis=0)
                    high = jnp.zeros_like(high)
                if i + 1 < len(hops):
                    given[i + 1, 0:8, :] = given[i, 0:8, :] + low
                    given[i + 1, 8:16, :] = given[i, 8:16, :] + high
                else:
                    out[...] = given[i, 0:8, :] + low

            self.jobs.append((start, end))


def block_kernel(
    plan,
    tokens,
    cotangent,
    wrow,
    vec,
    wattn,
    wfc,
    wproj,
    block_out,
    input_grad,
    proj_total,
    fc_total,
    attn_total,
    vec_total,
    vec2,
    weights2,
    act,
    dhid,
    own_x,
    n1,
    cot_p,
    n2,
    dattn,
    qkv,
    v_t,
    att_t,
    lse,
    delta,
    term,
    land_a,
    land_b,
    land_c,
    mid,
    dout,
    dq_acc,
    grads,
    landing,
    res,
    far,
    going,
    vec_s,
    vec_r,
    tok_s,
    tok_r,
    cot_s,
    cot_r,
    ag_s,
    ag_r,
    mate_s,
    mate_r,
    sum_s,
    sum_r,
    weight_s,
    weight_r,
    across_s,
    across_r,
    back_s,
    back_r,
    back_l,
    share_s,
    share_r,
    total_s,
    total_r,
    vec_ss,
    vec_sr,
):
    at = Place(plan)
    rows, width, pad, seq = plan.rows, plan.width, plan.pad, plan.seq
    chunk, own, part_rows = plan.chunk, plan.own, plan.part
    n = plan.n
    entry_barrier(plan, at)
    tokbuf, cotbuf, dqkv, grads2 = act, dhid, act, dhid
    mlp_term = grads.at[2 * width : 2 * width + seq]
    span = plan.heads * HD

    def here_in(buf):
        return lambda c, gi: buf.at[rows_at(c * chunk + at.spot * own + gi * plan.take, plan.take)]

    tok = Incoming(at, tokens, (tok_s, tok_r), here_in(tokbuf))
    cot = Incoming(at, cotangent, (cot_s, cot_r), here_in(cotbuf))
    tok_all = Gather(at, tokbuf, (ag_s.at[0], ag_r.at[0]))
    cot_all = Gather(at, cotbuf, (ag_s.at[1], ag_r.at[1]))
    n1_mate, cot_mate, n2_mate, dattn_mate, res_mate, dx_mate = (
        MateGather(at, buf, (mate_s.at[i], mate_r.at[i]))
        for i, buf in enumerate((n1, cot_p, n2, dattn, res, res))
    )
    attn_sum, back_sum, mlp_sum, norm_sum = (
        MateSum(at, ref, land, (sum_s.at[i], sum_r.at[i]))
        for i, (ref, land) in enumerate(
            ((term, land_a), (term, land_b), (mlp_term, land_c), (term, land_a))
        )
    )
    weights = (wattn, wfc, wproj)
    pieces = {}
    for i, (name, order) in enumerate(MOVES):
        pieces[name] = Weights(
            at,
            weights[i],
            weights2.at[i * width : (i + 1) * width],
            (weight_s, weight_r),
            i * weight_sems(width, n),
            order,
        )

    def weight(gi, i, start=0, stop=width):
        if gi:
            return weights2[i * width + start : i * width + stop, :]
        return weights[i][start:stop, :]

    vec_g = (vec, vec2)
    ways, sums = [], []
    for i, out in enumerate((block_out, input_grad)):
        rows_out = going.at[i]
        sums.append(AcrossSum(at, (cot_p, n2)[i], far.at[i], rows_out, (across_s.at[i], across_r.at[i])))
        ways.append(
            Outgoing(
                at,
                rows_out,
                out,
                (back_s.at[i], back_r.at[i]),
                back_l.at[i],
                (share_s.at[i], share_r.at[i]),
            )
        )
    out_across, dx_across = sums
    out_way, grad_way = ways
    outs = {"P": proj_total, "F": fc_total, "A": attn_total}
    room, index, half = 0, 0, width // 2
    for name, kind, which, order, early in TOTALS:
        first, at_row = {"P": (grads, 0), "F": (grads, 2 * width), "A": (grads2, 0)}[kind]
        pieces[name] = Total(
            at,
            first,
            [at_row + gi * width + which * half for gi in range(2)],
            outs[kind].at[which * half : (which + 1) * half],
            landing,
            room,
            (total_s, total_r),
            index,
            order,
            early,
        )
        more, sems = total_room(half, n, early)
        room, index = room + more, index + sems

    def incoming(way, every, c):
        def first():
            if c < plan.split:
                way.start(c)

        def second():
            way.wait(c)
            every.start(c)

        return Steps(first, second, lambda: every.forward(c), lambda: every.finish(c))

    def outgoing(across, way, c):
        part_of = c - (CHUNKS - plan.split)

        def second():
            across.finish(c)
            way.start(c)

        def when_part(run):
            return lambda: run(part_of) if part_of >= 0 else None

        return Steps(
            lambda: across.start(c),
            second,
            when_part(way.share),
            when_part(way.forward),
            when_part(way.finish),
        )

    for c in range(CHUNKS):
        pieces["0123"[c]] = incoming(tok, tok_all, c)
        pieces["4567"[c]] = incoming(cot, cot_all, c)
        pieces["ijkl"[c]] = outgoing(out_across, out_way, c)
        pieces["rstu"[c]] = outgoing(dx_across, grad_way, c)

    hops = [{"mp": at.mate}, {"mp": at.across}]
    bit = 1
    while bit < n:
        high = lax.rem(at.d // bit, 2)
        hops.append({"dp": at.d + (1 - 2 * high) * bit})
        bit *= 2
    vec_total_sum = VecTotal(hops, vec_s, vec_r, vec_total, (vec_ss, vec_sr))
    pieces["v"] = vec_total_sum
    schedule = iter(SCHEDULE)

    def go():
        for name in next(schedule):
            pieces[name].step()

    def need(names):
        for name in names:
            pieces[name].finish()

    def row(i):
        return vec[i : i + 1, :]

    def add_line(line, value):
        vec_s[0, line : line + 1, :] += jnp.sum(value, axis=0, keepdims=True)

    def pack(c, buf):
        line = wrow[0:1, rows_at(at.mine(c), part_rows, LANES)].astype(F32)
        col = jnp.broadcast_to(line, (8, part_rows)).T[:, 0:1].astype(jnp.int32)
        return nn(pick(col, rows), buf[...])

    for c in range(CHUNKS):
        pieces["0123"[c]].step()
    pieces["a"].step()
    bias_copy = send(vec, vec2, (vec_ss, vec_sr), 0, {"mp": at.across})
    vec_s[0, :, :] = jnp.zeros((GLINES, width), F32)
    dq_acc[...] = jnp.zeros_like(dq_acc)
    qkv[...] = jnp.zeros_like(qkv)
    dout[...] = jnp.zeros_like(dout)
    go()
    need("0123")
    for c in range(HALVES):
        packed = pack(c, tokbuf)
        own_x[c * part_rows : (c + 1) * part_rows, :] = packed.astype(BF)
        normal, _ = normal_rows(packed)
        n1[rows_at(at.mine(c), part_rows), :] = (normal * row(V_LN1G) + row(V_LN1B)).astype(BF)
        n1_mate.start(c)
    go()
    for c in range(HALVES):
        n1_mate.finish(c)

    def project(gi):
        def one(i, carry):
            here = rows_at(i * TILE, TILE, TILE)
            there = rows_at(gi * seq + i * TILE, TILE, TILE)
            for j in range(3):
                made = nt(n1[here, :], weight(gi, 0, j * span, (j + 1) * span))
                made = made + vec_g[gi][V_QKVB : V_QKVB + 1, j * pad : j * pad + span]
                qkv[there, j * pad : j * pad + span] = made.astype(BF)
            turned = qkv[there, 2 * pad :].astype(F32).T.astype(BF)
            v_t[gi * span : (gi + 1) * span, here] = turned[0:span, :]
            return carry

        lax.fori_loop(0, seq // TILE, one, 0)

    key_line = lax.broadcasted_iota(jnp.int32, (TILE, TILE), 0)
    query_line = lax.broadcasted_iota(jnp.int32, (TILE, TILE), 1)
    seen = key_line <= query_line

    def attend(gi, i):
        q0, base = i * TILE, gi * seq
        cols = slice(q0, q0 + TILE)
        for h in range(plan.heads):
            lanes = (h // 2) * LANES
            q_lanes = slice(lanes, lanes + LANES)
            k_lanes = slice(pad + lanes, pad + lanes + LANES)
            vh = v_t.at[gi * span + h * HD : gi * span + (h + 1) * HD]
            qh = head_lanes(qkv[base + q0 : base + q0 + TILE, q_lanes], h % 2 == 1)
            near = jnp.where(seen, nt(qkv[base + q0 : base + q0 + TILE, k_lanes], qh), NEG)
            top = jnp.max(near, axis=0, keepdims=True)
            if i:
                old = nt(qkv[base : base + q0, k_lanes], qh)
                top = jnp.maximum(top, jnp.max(old, axis=0, keepdims=True))
            expo = jnp.exp2((near - top) * LOG2E)
            total = jnp.sum(expo, axis=0, keepdims=True)
            out = nn(vh[:, cols], expo.astype(BF))
            if i:
                expo = jnp.exp2((old - top) * LOG2E)
                total = total + jnp.sum(expo, axis=0, keepdims=True)
                out = out + nn(vh[:, 0:q0], expo.astype(BF))
            line = gi * 4 + h
            att_t[gi * span + h * HD : gi * span + (h + 1) * HD, cols] = (out * (1.0 / total)).astype(BF)
            lse[line : line + 1, cols] = top * LOG2E + jnp.log2(total)

    blocks = seq // TILE

    def merge(c):
        def one(i, carry):
            here = rows_at(c * plan.half + i * TILE, TILE, TILE)
            total = None
            for gi in range(2):
                att = att_t[gi * span : (gi + 1) * span, here].astype(F32).T.astype(BF)
                value = nn(att, weight(gi, 0, 3 * span, 4 * span))
                total = value if total is None else total + value
            term[here, :] = total.astype(BF)
            return carry

        lax.fori_loop(0, plan.half // TILE, one, 0)

    project(0)
    for i in range(blocks):
        go()
        attend(0, i)
    go()
    need("a")
    landed(vec2, (vec_ss, vec_sr), 0, {"mp": at.across})
    project(1)
    for i in range(blocks):
        go()
        attend(1, i)
    go()
    for c in range(HALVES):
        merge(c)
        attn_sum.start(c)
    go()
    need("4567")
    for c in range(HALVES):
        packed = pack(c, cotbuf)
        cot_p[rows_at(at.mine(c), part_rows), :] = packed.astype(BF)
        add_line(G_PROJB, packed)
        cot_mate.start(c)
        middle = own_x[c * part_rows : (c + 1) * part_rows, :].astype(F32) + (
            attn_sum.finish(c) + row(V_OUTB)
        )
        mid[c * part_rows : (c + 1) * part_rows, :] = middle
        normal, _ = normal_rows(middle)
        n2[rows_at(at.mine(c), part_rows), :] = (normal * row(V_LN2G) + row(V_LN2B)).astype(BF)
        n2_mate.start(c)
    attn_sum.drain()
    go()
    need("fp")
    tok_all.drain()
    cot_all.drain()
    for c in range(HALVES):
        n2_mate.finish(c)
        cot_mate.finish(c)

        def feed(i, carry, c=c):
            here = rows_at(c * plan.half + i * TILE, TILE, TILE)
            up, down = None, None
            for gi in range(2):
                there = rows_at(gi * seq + c * plan.half + i * TILE, TILE, TILE)
                v = nn(n2[here, :], weight(gi, 1)) + vec_g[gi][V_FCB : V_FCB + 1, :]
                square = v * v
                t = jnp.tanh(GELU * v * (1.0 + CUBE * square))
                halved = 0.5 * (1.0 + t)
                active = (v * halved).astype(BF)
                slope = halved + 0.5 * v * (1.0 - t * t) * (GELU * (1.0 + 3.0 * CUBE * square))
                act[there, :] = active
                more = nn(active, weight(gi, 2))
                up = more if up is None else up + more
                low = (nt(cot_p[here, :], weight(gi, 2)) * slope).astype(BF)
                dhid[there, :] = low
                add_line((G_FCB, G_FCB2)[gi], low.astype(F32))
                more = nt(low, weight(gi, 1))
                down = more if down is None else down + more
            mlp_term[here, :] = up.astype(BF)
            term[here, :] = down.astype(BF)
            return carry

        lax.fori_loop(0, plan.half // TILE, feed, 0)
        back_sum.start(c)
        mlp_sum.start(c)
        go()

    def weight_grad(left_ref, left_row, right_ref, right_row, dst, place):
        def one(i, carry):
            cols = rows_at(i * TILE, TILE, TILE)
            value = tn(left_ref[left_row : left_row + seq, cols], right_ref[right_row : right_row + seq, :])
            dst[rows_at(place + i * TILE, TILE, TILE), :] = value.astype(BF)
            return carry

        lax.fori_loop(0, width // TILE, one, 0)

    for gi in range(2):
        weight_grad(act, gi * seq, cot_p, 0, grads, gi * width)
    for name in "PQ":
        pieces[name].step()
    go()
    for c in range(HALVES):
        mine = slice(c * part_rows, (c + 1) * part_rows)
        where = rows_at(at.mine(c), part_rows)
        grad2 = back_sum.finish(c)
        middle = mid[mine, :]
        res[where, :] = (middle + (mlp_sum.finish(c) + row(V_PROJB))).astype(BF)
        res_mate.start(c)
        normal, inv = normal_rows(middle)
        grad_mid = cot_p[where, :].astype(F32) + norm_back(grad2, normal, inv, row(V_LN2G))
        low = grad_mid.astype(BF)
        mid[mine, :] = grad_mid
        dattn[where, :] = low
        dattn_mate.start(c)
        add_line(G_LN2G, grad2 * normal)
        add_line(G_LN2B, grad2)
        add_line(G_OUTB, low.astype(F32))
    mlp_sum.drain()
    go()
    for gi in range(2):
        weight_grad(n2, 0, dhid, gi * seq, grads, (2 + gi) * width)
    for name in "FG":
        pieces[name].step()
    back_sum.drain()
    go()

    def unpack(c, part):
        start = c * chunk + at.core * (2 * own)
        part[c * 2 * own : (c + 1) * 2 * own, :] = nn(
            pick_rows(wrow[...], start, 2 * own), res[...]
        ).astype(BF)

    cot_mate.drain()
    for c in range(HALVES):
        res_mate.finish(c)
    for c in range(CHUNKS):
        unpack(c, cot_p)
        pieces["ijkl"[c]].step()
    go()
    for c in range(HALVES):
        dattn_mate.finish(c)
    for gi in range(2):

        def back_out(i, carry, gi=gi):
            here = rows_at(i * TILE, TILE, TILE)
            there = rows_at(gi * seq + i * TILE, TILE, TILE)
            low = nt(dattn[here, :], weight(gi, 0, 3 * span, 4 * span)).astype(BF)
            dout[there, 0:span] = low
            turned = dout[there, :].astype(F32).T
            both = turned[0:span, :] * att_t[gi * span : (gi + 1) * span, here].astype(F32)
            for h in range(plan.heads):
                line = gi * 4 + h
                delta[line : line + 1, here] = jnp.sum(both[h * HD : (h + 1) * HD, :], axis=0, keepdims=True)
            return carry

        lax.fori_loop(0, seq // TILE, back_out, 0)
        grads2[gi * width + 3 * span : gi * width + 4 * span, :] = nn(
            att_t[gi * span : (gi + 1) * span, :], dattn[...]
        ).astype(BF)

    def attend_back(gi, i):
        k0, base = i * TILE, gi * seq
        k_rows = slice(base + k0, base + k0 + TILE)
        parts = []
        for h in range(plan.heads):
            lanes = (h // 2) * LANES
            q_lanes = slice(lanes, lanes + LANES)
            kh = head_lanes(qkv[k_rows, pad + lanes : pad + lanes + LANES], h % 2 == 1)
            vh = head_lanes(qkv[k_rows, 2 * pad + lanes : 2 * pad + lanes + LANES], h % 2 == 1)
            if h % 2 == 0:
                turned = qkv[k_rows, pad + lanes : pad + lanes + LANES].astype(F32).T.astype(BF)
            kt = turned[(h % 2) * HD : (h % 2 + 1) * HD, :]
            line = gi * 4 + h
            dk = dv = None
            for q0, q1 in ((k0, k0 + TILE), (k0 + TILE, seq)):
                if q0 == q1:
                    continue
                q_all = qkv[base + q0 : base + q1, q_lanes]
                do_all = dout[base + q0 : base + q1, q_lanes]
                prob = jnp.exp2(nt(kh, q_all) * LOG2E - lse[line : line + 1, q0:q1])
                if q0 == k0:
                    prob = jnp.where(seen, prob, 0.0)
                low = (prob * (nt(vh, do_all) - delta[line : line + 1, q0:q1])).astype(BF)
                more_v, more_k = nn(prob.astype(BF), do_all), nn(low, q_all)
                dv = more_v if dv is None else dv + more_v
                dk = more_k if dk is None else dk + more_k
                dq_acc[gi * span + h * HD : gi * span + (h + 1) * HD, q0:q1] += nn(kt, low)
            parts.append((dk, dv))
        for h in range(0, plan.heads, 2):
            lanes = (h // 2) * LANES
            for j in range(2):
                value = head_lanes(parts[h][j], False)
                if h + 1 < plan.heads:
                    value = value + head_lanes(parts[h + 1][j], True)
                start = (1 + j) * pad + lanes
                dqkv[k_rows, start : start + LANES] = value.astype(BF)

    for gi in range(2):
        for i in range(blocks):
            go()
            attend_back(gi, i)
    go()
    for c in range(HALVES):

        def back_project(i, carry, c=c):
            here = rows_at(c * plan.half + i * TILE, TILE, TILE)
            total = None
            for gi in range(2):
                there = rows_at(gi * seq + c * plan.half + i * TILE, TILE, TILE)
                turned = jnp.concatenate(
                    [dq_acc[gi * span : (gi + 1) * span, here], jnp.zeros((pad - span, TILE), F32)], axis=0
                )
                dqkv[there, 0:pad] = turned.T.astype(BF)
                add_line((G_QKVB, G_QKVB2)[gi], dqkv[there, :].astype(F32))
                for j in range(3):
                    more = nn(dqkv[there, j * pad : j * pad + span], weight(gi, 0, j * span, (j + 1) * span))
                    total = more if total is None else total + more
            term[here, :] = total.astype(BF)
            return carry

        lax.fori_loop(0, plan.half // TILE, back_project, 0)
        norm_sum.start(c)
    go()
    for c in range(HALVES):
        mine = slice(c * part_rows, (c + 1) * part_rows)
        grad1 = norm_sum.finish(c)
        normal, inv = normal_rows(own_x[mine, :].astype(F32))
        dx = mid[mine, :] + norm_back(grad1, normal, inv, row(V_LN1G))
        if c == 0:
            res_mate.drain()
        res[rows_at(at.mine(c), part_rows), :] = dx.astype(BF)
        dx_mate.start(c)
        add_line(G_LN1G, grad1 * normal)
        add_line(G_LN1B, grad1)
    bias_copy.wait_send()
    pieces["v"].step()
    go()
    n2_mate.drain()
    for c in range(HALVES):
        dx_mate.finish(c)
    for c in range(CHUNKS):
        unpack(c, n2)
        pieces["rstu"[c]].step()
    go()
    for gi in range(2):
        for j in range(3):
            row0 = gi * width + j * span
            grads2[row0 : row0 + span, :] = tn(
                dqkv[gi * seq : (gi + 1) * seq, j * pad : j * pad + span], n1[...]
            ).astype(BF)
    for name in "AB":
        pieces[name].step()
    for _ in range(TAIL):
        go()
    need(pieces)
    out_way.drain()
    grad_way.drain()
    tok.drain()
    cot.drain()
    for each in (n1_mate, out_across, dattn_mate, dx_mate, norm_sum, dx_across):
        each.drain()


def body(
    tokens,
    cotangent,
    seq_lengths,
    source_slot,
    ln1_gain,
    ln1_bias,
    qkv_weight,
    qv_bias,
    output_projection_weight,
    out_bias,
    ln2_gain,
    ln2_bias,
    fc_weight,
    fc_bias,
    proj_weight,
    proj_bias,
):
    rows, width = tokens.shape
    span = qkv_weight.shape[2]
    n, members = lax.axis_size("dp"), lax.axis_size("mp")
    plan = Plan(n, members, rows, width, span // HD)
    pad, seq = plan.pad, plan.seq

    side = lax.axis_index("mp") // 2
    start = jnp.where(side == 0, 0, seq_lengths[0, 0])
    length = jnp.where(side == 0, seq_lengths[0, 0], seq_lengths[0, 1])
    windex = plan.work_index(source_slot)
    windex = lax.dynamic_slice(jnp.pad(windex, (0, seq), constant_values=-1), (start,), (seq,))
    windex = jnp.where(jnp.arange(seq) < length, windex, -1)
    wrow = windex[None, :]

    scale = jnp.array([HD**-0.5, 1.0, 1.0], BF)
    turned = (qkv_weight * scale[None, :, None]).transpose(1, 2, 0).reshape(3 * span, width)
    wattn = jnp.concatenate([turned, output_projection_weight], axis=0)
    qkv_bias = jnp.stack(
        [qv_bias[0].astype(F32) * HD**-0.5, jnp.zeros_like(qv_bias[0], F32), qv_bias[1].astype(F32)]
    )
    qkv_bias = jnp.pad(qkv_bias, [(0, 0), (0, pad - span)]).reshape(3 * pad)
    vec = jnp.stack(
        [
            v.astype(F32)
            for v in (ln1_gain, ln1_bias, out_bias, ln2_gain, ln2_bias, proj_bias, fc_bias, qkv_bias)
        ]
    )
    vm = pl.BlockSpec(memory_space=pltpu.VMEM)
    hbm = pl.BlockSpec(memory_space=pl.ANY)
    shape = jax.ShapeDtypeStruct
    quarter = rows // members
    dma = pltpu.SemaphoreType.DMA
    rooms = [total_room(width // 2, n, entry[4]) for entry in TOTALS]
    landing, sems = (sum(room[i] for room in rooms) for i in range(2))
    moves = 3 * weight_sems(width, n)
    hops = 2 + (n - 1).bit_length()

    def vmem(*dims, dtype=BF):
        return pltpu.VMEM(dims, dtype)

    block_out, input_grad, proj_total, fc_total, attn_total, vec_total = pl.pallas_call(
        functools.partial(block_kernel, plan),
        out_shape=(
            shape((rows, width), BF),
            shape((rows, width), BF),
            shape((width, width), BF),
            shape((width, width), BF),
            shape((width, width), BF),
            shape((8, width), F32),
        ),
        in_specs=[hbm, hbm] + [vm] * 5,
        out_specs=(hbm,) * 5 + (vm,),
        scratch_shapes=[
            vmem(8, width, dtype=F32),
            vmem(3 * width, width),
            vmem(rows, width),
            vmem(rows, width),
            vmem(quarter, width),
            vmem(seq, width),
            vmem(seq, width),
            vmem(seq, width),
            vmem(seq, width),
            vmem(2 * seq, 3 * pad),
            vmem(2 * span, seq),
            vmem(2 * span, seq),
            vmem(8, seq, dtype=F32),
            vmem(8, seq, dtype=F32),
            vmem(seq, width),
            vmem(seq // 2, width),
            vmem(seq // 2, width),
            vmem(seq // 2, width),
            vmem(seq // 2, width, dtype=F32),
            vmem(2 * seq, pad),
            vmem(2 * span, seq, dtype=F32),
            vmem(4 * width, width),
            vmem(landing, width),
            vmem(seq, width),
            vmem(2, quarter, width),
            vmem(2, quarter, width),
            vmem(hops, GLINES, width, dtype=F32),
            vmem(hops, GLINES, width, dtype=F32),
            dma((plan.split, n)),
            dma((CHUNKS, plan.in_chunk)),
            dma((plan.split, n)),
            dma((CHUNKS, plan.in_chunk)),
            dma((2, CHUNKS, 3)),
            dma((2, CHUNKS, 3)),
            dma((6, HALVES)),
            dma((6, HALVES)),
            dma((4, HALVES)),
            dma((4, HALVES)),
            dma((moves,)),
            dma((moves,)),
            dma((2, CHUNKS)),
            dma((2, CHUNKS)),
            dma((2, CHUNKS, plan.in_chunk)),
            dma((2, plan.split, n)),
            dma((2, plan.split)),
            dma((2, 3, plan.split, n)),
            dma((2, 3, plan.split, n)),
            dma((sems,)),
            dma((sems,)),
            dma((hops + 1,)),
            dma((hops + 1,)),
        ],
        compiler_params=pltpu.CompilerParams(
            collective_id=0, has_side_effects=True, vmem_limit_bytes=VMEM_LIMIT
        ),
        name="block",
    )(tokens, cotangent, wrow, vec, wattn, fc_weight, proj_weight)
    qkv_grad = attn_total[: 3 * span].reshape(3, span, width).transpose(2, 0, 1).astype(F32)
    qkv_grad = qkv_grad * scale.astype(F32)[None, :, None]
    qkv_sums = vec_total[G_QKVB].reshape(3, pad)[:, :span]
    return (
        block_out,
        input_grad,
        vec_total[G_LN1G],
        vec_total[G_LN1B],
        qkv_grad,
        jnp.stack([qkv_sums[0] * HD**-0.5, qkv_sums[2]]),
        attn_total[3 * span :].astype(F32),
        vec_total[G_OUTB],
        vec_total[G_LN2G],
        vec_total[G_LN2B],
        fc_total.astype(F32),
        vec_total[G_FCB],
        proj_total.astype(F32),
        vec_total[G_PROJB],
    )


def solution(mesh):
    return jax.shard_map(
        body,
        mesh=mesh,
        in_specs=(
            P("dp", None),
            P("dp", None),
            P("dp", None),
            P("dp"),
            P(),
            P(),
            P(None, None, "mp"),
            P(None, "mp"),
            P("mp", None),
            P(),
            P(),
            P(),
            P(None, "mp"),
            P("mp"),
            P("mp", None),
            P(),
        ),
        out_specs=(
            P("dp", None),
            P("dp", None),
            P(),
            P(),
            P(None, None, "mp"),
            P(None, "mp"),
            P("mp", None),
            P(),
            P(),
            P(),
            P(None, "mp"),
            P("mp"),
            P("mp", None),
            P(),
        ),
        check_vma=False,
    )
```

```python
import functools

import jax
import jax.numpy as jnp
from jax import lax
from jax.experimental import pallas as pl
from jax.experimental.pallas import tpu as pltpu
from jax.sharding import PartitionSpec as P

MESH = pl.DeviceIdType.MESH
BF = jnp.bfloat16
F32 = jnp.float32
HD = 64
EPSILON = 1e-05
NEG = -1e30
LOG2E = 1.4426950408889634
TILE = 256
HALVES = 2
COPIES = 4
CHUNKS = 4
LANES = 128
VMEM_LIMIT = 60 * 2**20


class Plan:
    def __init__(self, n, members, rows, width, heads):
        self.n, self.members, self.rows, self.width, self.heads = n, members, rows, width, heads
        self.slots = rows // n
        self.group = max(1, (16 * members) // self.slots)
        self.share = self.group * self.slots // members
        self.groups = n // self.group
        self.chunk = rows // CHUNKS
        self.own = self.chunk // members
        self.take = max(16, self.share // CHUNKS)
        self.split = self.share // self.take
        self.in_chunk = self.own // self.take
        self.seq = rows // 2
        self.half = self.seq // HALVES
        self.part = self.half // 2
        self.pad = -(-heads * HD // LANES) * LANES

    def work_index(self, slot_ids):
        source, slot = over(slot_ids, self.slots), under(slot_ids, self.slots)
        grp = over(source, self.group)
        inside = under(source, self.group) * self.slots + slot
        owner, row = over(inside, self.share), under(inside, self.share)
        chunk = over(grp, self.in_chunk) * self.split + over(row, self.take)
        place = under(owner, 2) * (self.members // 2) + over(owner, 2)
        return (
            chunk * self.chunk
            + place * self.own
            + under(grp, self.in_chunk) * self.take
            + under(row, self.take)
        )


def over(x, size):
    return lax.shift_right_logical(x, jnp.full_like(x, size.bit_length() - 1))


def under(x, size):
    return x & (size - 1)


def nn(a, b):
    return lax.dot_general(a, b, (((1,), (0,)), ((), ())), preferred_element_type=F32)


def nt(a, b):
    return lax.dot_general(a, b, (((1,), (1,)), ((), ())), preferred_element_type=F32)


def tn(a, b):
    return lax.dot_general(a, b, (((0,), (0,)), ((), ())), preferred_element_type=F32)


def rows_at(start, count, step=16):
    if not isinstance(start, int):
        start = pl.multiple_of(start, step)
    return pl.ds(start, count)


class Place:
    def __init__(self, plan):
        self.plan = plan
        self.d = lax.axis_index("dp")
        self.m = lax.axis_index("mp")
        self.core = lax.rem(self.m, 2)
        self.side = self.m // 2
        self.mate = self.m + 1 - 2 * self.core
        self.across = lax.rem(self.m + 2, plan.members)
        self.spot = self.core * 2 + self.side

    def mine(self, c, flip=False):
        core = 1 - self.core if flip else self.core
        return (2 * c + core) * self.plan.part

    def spot_of(self, core_flip, side_flip):
        core = 1 - self.core if core_flip else self.core
        side = 1 - self.side if side_flip else self.side
        return core * 2 + side

    def member(self, core_flip, side_flip):
        core = 1 - self.core if core_flip else self.core
        side = 1 - self.side if side_flip else self.side
        return side * 2 + core


def send(src, dst, sems, index, device):
    copy = pltpu.make_async_remote_copy(
        src_ref=src,
        dst_ref=dst,
        send_sem=sems[0].at[index],
        recv_sem=sems[1].at[index],
        device_id=device,
        device_id_type=MESH,
    )
    copy.start()
    return copy


def landed(dst, sems, index, device):
    pltpu.make_async_remote_copy(
        src_ref=dst,
        dst_ref=dst,
        send_sem=sems[0].at[index],
        recv_sem=sems[1].at[index],
        device_id=device,
        device_id_type=MESH,
    ).wait_recv()


def left(src, sems, index, device):
    pltpu.make_async_remote_copy(
        src_ref=src,
        dst_ref=src,
        send_sem=sems[0].at[index],
        recv_sem=sems[1].at[index],
        device_id=device,
        device_id_type=MESH,
    ).wait_send()


def entry_barrier(plan, at):
    barrier = pltpu.get_barrier_semaphore()

    def signal(j, carry):
        pl.semaphore_signal(
            barrier, inc=1, device_id={"dp": lax.rem(at.d + j, plan.n)}, device_id_type=MESH
        )
        return carry

    lax.fori_loop(1, plan.n, signal, 0)
    pl.semaphore_signal(barrier, inc=1, device_id={"mp": at.mate}, device_id_type=MESH)
    pl.semaphore_signal(barrier, inc=1, device_id={"mp": at.across}, device_id_type=MESH)
    pl.semaphore_wait(barrier, plan.n + 1)


class Gather:
    def __init__(self, at, buf, sems):
        self.at, self.buf, self.sems, self.copies = at, buf, sems, []

    def rows(self, c, core_flip=False, side_flip=False):
        plan = self.at.plan
        start = c * plan.chunk + self.at.spot_of(core_flip, side_flip) * plan.own
        return self.buf.at[rows_at(start, plan.own)]

    def start(self, c):
        mine = self.rows(c)
        self.copies.append(send(mine, mine, self.sems, (c, 1), {"mp": self.at.across}))
        self.copies.append(send(mine, mine, self.sems, (c, 0), {"mp": self.at.mate}))

    def forward(self, c):
        theirs = self.rows(c, side_flip=True)
        landed(theirs, self.sems, (c, 1), {"mp": self.at.across})
        self.copies.append(send(theirs, theirs, self.sems, (c, 2), {"mp": self.at.mate}))

    def finish(self, c):
        landed(self.rows(c, core_flip=True), self.sems, (c, 0), {"mp": self.at.mate})
        landed(self.rows(c, core_flip=True, side_flip=True), self.sems, (c, 2), {"mp": self.at.mate})

    def drain(self):
        for copy in self.copies:
            copy.wait_send()
        self.copies = []


class MateGather:
    def __init__(self, at, buf, sems):
        self.at, self.buf, self.sems, self.copies = at, buf, sems, []

    def mine(self, c):
        return rows_at(self.at.mine(c), self.at.plan.part)

    def start(self, c):
        here = self.buf.at[self.mine(c)]
        self.copies.append(send(here, here, self.sems, c, {"mp": self.at.mate}))

    def finish(self, c):
        there = self.buf.at[rows_at(self.at.mine(c, True), self.at.plan.part)]
        landed(there, self.sems, c, {"mp": self.at.mate})

    def drain(self):
        for copy in self.copies:
            copy.wait_send()
        self.copies = []


class MateSum:
    def __init__(self, at, term, land, sems):
        self.at, self.term, self.land, self.sems, self.copies = at, term, land, sems, []

    def start(self, c):
        plan, at = self.at.plan, self.at
        src = self.term.at[rows_at(at.mine(c, True), plan.part)]
        dst = self.land.at[rows_at(c * plan.part, plan.part)]
        self.copies.append(send(src, dst, self.sems, c, {"mp": at.mate}))

    def finish(self, c):
        plan, at = self.at.plan, self.at
        where = rows_at(c * plan.part, plan.part)
        landed(self.land.at[where], self.sems, c, {"mp": at.mate})
        mine = self.term[rows_at(at.mine(c), plan.part), :]
        return mine.astype(F32) + self.land[where, :].astype(F32)

    def drain(self):
        for copy in self.copies:
            copy.wait_send()
        self.copies = []


class AcrossSum:
    def __init__(self, at, part, far, out, sems):
        self.at, self.part, self.far, self.out, self.sems, self.copies = at, part, far, out, sems, []

    def start(self, c):
        plan, at = self.at.plan, self.at
        src = self.part.at[rows_at((2 * c + 1 - at.side) * plan.own, plan.own)]
        dst = self.far.at[rows_at(c * plan.own, plan.own)]
        self.copies.append(send(src, dst, self.sems, c, {"mp": at.across}))

    def finish(self, c):
        plan, at = self.at.plan, self.at
        where = rows_at(c * plan.own, plan.own)
        landed(self.far.at[where], self.sems, c, {"mp": at.across})
        mine = self.part[rows_at((2 * c + at.side) * plan.own, plan.own), :]
        self.out[where, :] = (mine.astype(F32) + self.far[where, :].astype(F32)).astype(BF)

    def drain(self):
        for copy in self.copies:
            copy.wait_send()
        self.copies = []


class Incoming:
    def __init__(self, at, source, sems, landing):
        plan = at.plan
        self.at, self.source, self.sems, self.landing = at, source, sems, landing
        self.offset = lax.rem(at.m * plan.share, plan.slots)
        self.sends = None
        if plan.group > 1:
            self.sends = lax.rem(at.d, plan.group) == (at.m * plan.share) // plan.slots

    def guarded(self, run):
        if self.sends is None:
            run()
        else:
            pl.when(self.sends)(run)

    def mine(self, part):
        plan, at = self.at.plan, self.at
        grp = at.d // plan.group
        return (grp // plan.in_chunk) * plan.split + part, lax.rem(grp, plan.in_chunk)

    def piece(self, k, part):
        plan = self.at.plan
        start = k * plan.slots + self.offset + part * plan.take
        return self.source.at[rows_at(start, plan.take)]

    def start(self, part):
        plan, at = self.at.plan, self.at
        c, gi = self.mine(part)

        def one(j, carry):
            k = lax.rem(at.d + j, plan.n)
            pltpu.make_async_remote_copy(
                src_ref=self.piece(k, part),
                dst_ref=self.landing(c, gi),
                send_sem=self.sems[0].at[part, j],
                recv_sem=self.sems[1].at[c, gi],
                device_id={"dp": k},
                device_id_type=MESH,
            ).start()
            return carry

        def run():
            lax.fori_loop(1, plan.n, one, 0)
            pltpu.make_async_copy(
                self.piece(at.d, part), self.landing(c, gi), self.sems[1].at[c, gi]
            ).start()

        self.guarded(run)

    def wait(self, c):
        plan, at = self.at.plan, self.at

        def one(gi, carry):
            landed(self.landing(c, gi), (self.sems[1], self.sems[1]), (c, gi), {"dp": at.d})
            return carry

        lax.fori_loop(0, plan.in_chunk, one, 0)

    def drain(self):
        plan, at = self.at.plan, self.at

        def run():
            for part in range(plan.split):

                def one(j, carry, part=part):
                    k = lax.rem(at.d + j, plan.n)
                    left(self.piece(k, part), (self.sems[0], self.sems[0]), (part, j), {"dp": k})
                    return carry

                lax.fori_loop(1, plan.n, one, 0)

        self.guarded(run)


class Outgoing:
    def __init__(self, at, rows_ref, out, sems, local_sem, share_sems):
        plan = at.plan
        self.at, self.rows_ref, self.out = at, rows_ref, out
        self.sems, self.local_sem, self.share_sems = sems, local_sem, share_sems

    def holds(self, member):
        plan = self.at.plan
        if plan.group == 1:
            return None
        return lax.rem(self.at.d, plan.group) == (member * plan.share) // plan.slots

    def guarded(self, member, run):
        if self.at.plan.group == 1:
            run()
        else:
            pl.when(self.holds(member))(run)

    def place(self, k, part, member):
        plan = self.at.plan
        start = k * plan.slots + lax.rem(member * plan.share, plan.slots) + part * plan.take
        return self.out.at[rows_at(start, plan.take)]

    def each(self, c, remote, local):
        plan, at = self.at.plan, self.at
        part = c % plan.split

        def one(gi, carry):
            grp = (c // plan.split) * plan.in_chunk + gi
            dest = grp * plan.group + (at.m * plan.share) // plan.slots
            src = self.rows_ref.at[rows_at(c * plan.own + gi * plan.take, plan.take)]
            dst = self.place(at.d, part, at.m)
            pl.when(dest != at.d)(lambda: remote(gi, part, src, dst, dest))
            pl.when(dest == at.d)(lambda: local(gi, part, src, dst))
            return carry

        lax.fori_loop(0, plan.in_chunk, one, 0)

    def copy(self, c, gi, part, src, dst, dest):
        return pltpu.make_async_remote_copy(
            src_ref=src,
            dst_ref=dst,
            send_sem=self.sems[0].at[c, gi],
            recv_sem=self.sems[1].at[part, self.at.d],
            device_id={"dp": dest},
            device_id_type=MESH,
        )

    def start(self, c):
        def local(gi, part, src, dst):
            pltpu.make_async_copy(src, dst, self.local_sem.at[part]).start()

        self.each(c, lambda gi, part, src, dst, dest: self.copy(c, gi, part, src, dst, dest).start(), local)

    def drain(self):
        for c in range(CHUNKS):
            self.each(
                c,
                lambda gi, part, src, dst, dest: self.copy(c, gi, part, src, dst, dest).wait_send(),
                lambda gi, part, src, dst: None,
            )

    def loop(self, part, run):
        lax.fori_loop(0, self.at.plan.n, lambda k, carry: (run(k), carry)[1], 0)

    def share(self, part):
        at = self.at

        def run():
            def one(k):
                here = self.place(k, part, at.m)

                def remote():
                    landed(here, (self.sems[1], self.sems[1]), (part, k), {"dp": at.d})

                def local():
                    pltpu.make_async_copy(here, here, self.local_sem.at[part]).wait()

                pl.when(k != at.d)(remote)
                pl.when(k == at.d)(local)
                send(here, here, self.share_sems, (1, part, k), {"mp": at.across})
                send(here, here, self.share_sems, (0, part, k), {"mp": at.mate})

            self.loop(part, one)

        self.guarded(at.m, run)

    def forward(self, part):
        at = self.at

        def run():
            def one(k):
                there = self.place(k, part, at.across)
                landed(there, self.share_sems, (1, part, k), {"mp": at.across})
                send(there, there, self.share_sems, (2, part, k), {"mp": at.mate})

            self.loop(part, one)

        self.guarded(at.across, run)

    def finish(self, part):
        at = self.at
        corner = at.member(True, True)

        def near():
            self.loop(
                part,
                lambda k: landed(
                    self.place(k, part, at.mate), self.share_sems, (0, part, k), {"mp": at.mate}
                ),
            )

        def far():
            self.loop(
                part,
                lambda k: landed(
                    self.place(k, part, corner), self.share_sems, (2, part, k), {"mp": at.mate}
                ),
            )

        def sent():
            def one(k):
                here = self.place(k, part, at.m)
                left(here, self.share_sems, (1, part, k), {"mp": at.across})
                left(here, self.share_sems, (0, part, k), {"mp": at.mate})

            self.loop(part, one)

        def passed():
            self.loop(
                part,
                lambda k: left(
                    self.place(k, part, at.across), self.share_sems, (2, part, k), {"mp": at.mate}
                ),
            )

        self.guarded(at.mate, near)
        self.guarded(corner, far)
        self.guarded(at.m, sent)
        self.guarded(at.across, passed)


def halvings(rows, n, order):
    steps, size = [], rows
    bits = [1 << i for i in range((n - 1).bit_length())]
    for i in order:
        bits.insert(0, bits.pop(i))
    for bit in bits:
        if size % 32 == 0:
            size //= 2
            steps.append((bit, True, size))
        else:
            steps.append((bit, False, size))
    return steps


def trail_of(at, rows, order):
    offset, trail, size = 0, [], rows
    for bit, halve, size in halvings(rows, at.plan.n, order):
        if halve:
            high = lax.rem(at.d // bit, 2)
            partner = {"dp": at.d + (1 - 2 * high) * bit}
            trail.append((offset, offset + high * size, size, partner))
            offset = offset + high * size
    return offset, size, trail


class Steps:
    def __init__(self, *runs):
        self.runs, self.next = list(runs), 0

    def step(self):
        if self.next < len(self.runs):
            self.next += 1
            self.runs[self.next - 1]()

    def finish(self):
        while self.next < len(self.runs):
            self.step()


class Stepped:
    def __init__(self):
        self.jobs, self.next, self.pending = [], 0, None

    def step(self):
        if self.pending is not None:
            self.pending[0](self.pending[1])
            self.pending = None
        if self.next < len(self.jobs):
            start, end = self.jobs[self.next]
            self.next += 1
            self.pending = (end, start())

    def finish(self):
        while self.pending is not None or self.next < len(self.jobs):
            self.step()

    def spread(self, buf, keep, other, size, sems, index, partner, source=None, before_end=None):
        def start():
            here = buf.at[rows_at(keep, size)]
            return send(here if source is None else source, here, sems, index, partner)

        def end(copy):
            copy.wait_send()
            landed(buf.at[rows_at(other, size)], sems, index, partner)
            if before_end is not None:
                before_end()

        self.jobs.append((start, end))


class Weights(Stepped):
    def __init__(self, at, source, dst, sems, index, bits):
        super().__init__()
        offset, trail, size = 0, [], source.shape[0]
        for bit in bits:
            if bit < at.plan.n:
                size //= 2
                high = lax.rem(at.d // bit, 2)
                partner = {"dp": at.d + (1 - 2 * high) * bit}
                trail.append((offset, offset + high * size, size, partner))
                offset = offset + high * size
        slice_rows = rows_at(offset, size)
        across = {"mp": at.across}

        def start():
            return send(source.at[slice_rows], dst.at[slice_rows], sems, index, across)

        def end(copy):
            copy.wait_send()
            landed(dst.at[slice_rows], sems, index, across)

        self.jobs.append((start, end))
        for i, (before, keep, length, partner) in enumerate(reversed(trail)):
            self.spread(dst, keep, 2 * before + length - keep, length, sems, index + 1 + i, partner)


class Total(Stepped):
    def __init__(self, at, first, origins, out, landing, base, sems, index, order, early):
        super().__init__()
        self.at, self.landing = at, landing
        rows, n = out.shape[0], at.plan.n
        steps = halvings(rows, n, order)
        room = sum(size for _, _, size in steps)
        sources = [(first, origin) for origin in origins]
        if early:
            self.cross(sources, base, rows, (sems, index))
            sources, index, base = [(landing, base)], index + 1, base + rows
        lands = [base + i * room for i in range(len(sources))]
        for bit, halve, size in steps:
            high = lax.rem(at.d // bit, 2)
            partner = {"dp": at.d + (1 - 2 * high) * bit}
            keep = high * size if halve else 0
            give = (1 - high) * size if halve else 0
            self.exchange(sources, give, keep, size, list(lands), (sems, index), partner)
            index += len(sources)
            sources = [(landing, land) for land in lands]
            lands = [land + size for land in lands]
        offset, size, trail = trail_of(at, rows, order)
        if not early:
            self.cross(sources, base + 2 * room, size, (sems, index))
            sources, index = [(landing, base + 2 * room)], index + 1
        done = landing.at[rows_at(sources[0][1], size)]
        local = pltpu.make_async_copy(done, out.at[rows_at(offset, size)], sems[0].at[index])
        self.jobs[-1] = (self.jobs[-1][0], self.then(self.jobs[-1][1], local.start))
        index += 1
        for i, (before, keep, length, partner) in enumerate(reversed(trail)):
            source, settle = (done, local.wait) if i == 0 else (None, None)
            self.spread(
                out, keep, 2 * before + length - keep, length, sems, index + i, partner, source, settle
            )

    def then(self, end, more):
        def both(copy):
            end(copy)
            more()

        return both

    def add(self, first, origin, land, size):
        step = 96 if size % 96 == 0 else (32 if size % 32 == 0 else 16)

        def one(i, carry):
            here = rows_at(origin + i * step, step)
            there = rows_at(land + i * step, step)
            value = first[here, :].astype(F32) + self.landing[there, :].astype(F32)
            self.landing[there, :] = value.astype(BF)
            return carry

        lax.fori_loop(0, size // step, one, 0)

    def exchange(self, sources, give, keep, size, lands, sems, partner):
        sems, index = sems

        def start():
            return [
                send(
                    ref.at[rows_at(origin + give, size)],
                    self.landing.at[rows_at(land, size)],
                    sems,
                    index + i,
                    partner,
                )
                for i, ((ref, origin), land) in enumerate(zip(sources, lands))
            ]

        def end(copies):
            for copy, (ref, origin), land in zip(copies, sources, lands):
                copy.wait()
                self.add(ref, origin + keep, land, size)

        self.jobs.append((start, end))

    def cross(self, sources, land, size, sems):
        sems, index = sems
        (mine, mine_at), (theirs, theirs_at) = sources

        def start():
            return send(
                theirs.at[rows_at(theirs_at, size)],
                self.landing.at[rows_at(land, size)],
                sems,
                index,
                {"mp": self.at.across},
            )

        def end(copy):
            copy.wait()
            self.add(mine, mine_at, land, size)

        self.jobs.append((start, end))


def total_room(rows, n, early):
    steps = halvings(rows, n, ())
    size, spreads = steps[-1][2], sum(1 for _, halve, _ in steps if halve)
    room, groups = sum(step[2] for step in steps), 1 if early else 2
    return groups * room + (rows if early else size), groups * len(steps) + 2 + spreads


def normal_rows(x):
    centered = x - jnp.mean(x, axis=-1, keepdims=True)
    inv = lax.rsqrt(jnp.mean(centered * centered, axis=-1, keepdims=True) + EPSILON)
    return centered * inv, inv


def norm_back(grad, normal, inv, gain):
    scaled = grad * gain
    return inv * (
        scaled
        - jnp.mean(scaled, axis=-1, keepdims=True)
        - normal * jnp.mean(scaled * normal, axis=-1, keepdims=True)
    )


def pick(index_col, count):
    lanes = lax.broadcasted_iota(jnp.int32, (index_col.shape[0], count), 1)
    return jnp.where(lanes == index_col, 1.0, 0.0).astype(BF)


def pick_rows(index_row, first, count):
    lines = lax.broadcasted_iota(jnp.int32, (count, index_row.shape[1]), 0) + first
    return jnp.where(lines == index_row, 1.0, 0.0).astype(BF)


def head_lanes(x, odd):
    lane = lax.broadcasted_iota(jnp.int32, x.shape, 1)
    return jnp.where((lane >= HD) == odd, x, jnp.zeros_like(x))


V_LN1G, V_LN1B, V_OUTB, V_LN2G, V_LN2B, V_PROJB, V_FCB, V_QKVB = range(8)
G_LN1G, G_LN1B, G_LN2G, G_LN2B, G_OUTB, G_PROJB, G_FCB, G_QKVB, G_FCB2, G_QKVB2 = range(10)
SHARED = 6
MOVES = (
    ("a", 0, 0, 256, (1, 2)),
    ("b", 0, 256, 512, (1, 2, 4)),
    ("c", 0, 512, 768, (1, 2)),
    ("f", 1, 0, 384, (1, 2)),
    ("g", 1, 384, 768, (2, 1)),
    ("p", 2, 0, 256, (2, 1, 4)),
    ("q", 2, 256, 512, (1, 2)),
    ("x", 2, 512, 768, (1, 2, 4)),
)
TOTALS = (
    ("F", "F", 0, 256, (), False),
    ("G", "F", 256, 512, (), False),
    ("H", "F", 512, 768, (), True),
    ("A", "A", 0, 256, (), True),
    ("B", "A", 256, 512, (1,), True),
    ("C", "A", 512, 768, (), True),
    ("P", "P", 0, 256, (1,), False),
    ("Q", "P", 256, 512, (), True),
    ("X", "P", 512, 768, (), False),
)
SCHEDULE = (
    "ab04567c1020a13fgpqx12bca2343",
    "5fgbcp",
    "6",
    "q",
    "x",
    "",
    "7g4fp4bq",
    "5",
    "x",
    "",
    "5",
    "6f",
    "gp67x7",
    "qpx",
    "",
    "",
    "",
    "",
    "",
    "",
    "PQX",
    "",
    "",
    "X",
    "FH",
    "",
    "Xi",
    "",
    "FjG",
    "Pk",
    "F",
    "GQvXl",
    "HPFriQsjtkHuvGXlAFXrQABFstXCAPHiuFQiBjCAjBPQkvGH",
    "kCPAlBQHlGrCrHPsAsBtGtCAuvBvCuGBC",
)
TAIL = 2
GLINES = 16
GELU = 0.7978845608028654
CUBE = 0.044715


class VecTotal(Stepped):
    def __init__(self, hops, given, taken, out, sems):
        super().__init__()
        line = lax.broadcasted_iota(jnp.int32, (8, out.shape[1]), 0)
        for i, device in enumerate(hops):

            def start(i=i, device=device):
                return send(given.at[i], taken.at[i], sems, i + 1, device)

            def end(copy, i=i):
                copy.wait()
                low, high = taken[i, 0:8, :], taken[i, 8:16, :]
                if i == 0:
                    low, high = jnp.where(line < SHARED, low, 0.0), jnp.zeros_like(high)
                elif i == 1:
                    low = jnp.concatenate([low[0:SHARED, :], high[0:2, :]], axis=0)
                    high = jnp.zeros_like(high)
                if i + 1 < len(hops):
                    given[i + 1, 0:8, :] = given[i, 0:8, :] + low
                    given[i + 1, 8:16, :] = given[i, 8:16, :] + high
                else:
                    out[...] = given[i, 0:8, :] + low

            self.jobs.append((start, end))


def block_kernel(
    plan,
    tokens,
    cotangent,
    slot_row,
    lengths,
    vec_in,
    qv_in,
    wqkv_in,
    wo_in,
    wfc,
    wproj,
    block_out,
    input_grad,
    proj_total,
    fc_total,
    attn_total,
    vec_total,
    vec,
    wrow,
    wattn,
    vec2,
    weights2,
    act,
    dhid,
    own_x,
    n1,
    cot_p,
    n2,
    dattn,
    qkv,
    v_t,
    att_t,
    lse,
    delta,
    term,
    land_a,
    land_b,
    land_c,
    mid,
    dout,
    dq_acc,
    grads,
    landing,
    res,
    far,
    going,
    vec_s,
    vec_r,
    tok_s,
    tok_r,
    cot_s,
    cot_r,
    ag_s,
    ag_r,
    mate_s,
    mate_r,
    sum_s,
    sum_r,
    weight_s,
    weight_r,
    across_s,
    across_r,
    back_s,
    back_r,
    back_l,
    share_s,
    share_r,
    total_s,
    total_r,
    vec_ss,
    vec_sr,
    local,
):
    at = Place(plan)
    rows, width, pad, seq = plan.rows, plan.width, plan.pad, plan.seq
    chunk, own, part_rows = plan.chunk, plan.own, plan.part
    n = plan.n
    span = plan.heads * HD
    fetch = [
        pltpu.make_async_copy(wqkv_in, wattn.at[0 : 3 * span], local.at[0]),
        pltpu.make_async_copy(wo_in, wattn.at[3 * span : 4 * span], local.at[1]),
    ]
    for copy in fetch:
        copy.start()
    vec[...] = vec_in[...]
    vec[V_QKVB : V_QKVB + 1, 0:span] = qv_in[0:1, :].astype(F32)
    vec[V_QKVB : V_QKVB + 1, 2 * pad : 2 * pad + span] = qv_in[1:2, :].astype(F32)
    entry_barrier(plan, at)
    tokbuf, cotbuf, dqkv, grads2 = act, dhid, act, dhid
    mlp_term = grads.at[2 * width : 2 * width + seq]

    def here_in(buf):
        return lambda c, gi: buf.at[rows_at(c * chunk + at.spot * own + gi * plan.take, plan.take)]

    tok = Incoming(at, tokens, (tok_s, tok_r), here_in(tokbuf))
    cot = Incoming(at, cotangent, (cot_s, cot_r), here_in(cotbuf))
    tok_all = Gather(at, tokbuf, (ag_s.at[0], ag_r.at[0]))
    cot_all = Gather(at, cotbuf, (ag_s.at[1], ag_r.at[1]))
    n1_mate, cot_mate, n2_mate, dattn_mate, res_mate, dx_mate = (
        MateGather(at, buf, (mate_s.at[i], mate_r.at[i]))
        for i, buf in enumerate((n1, cot_p, n2, dattn, res, res))
    )
    attn_sum, back_sum, mlp_sum, norm_sum = (
        MateSum(at, ref, land, (sum_s.at[i], sum_r.at[i]))
        for i, (ref, land) in enumerate(
            ((term, land_a), (term, land_b), (mlp_term, land_c), (term, land_a))
        )
    )
    weights = (wattn, wfc, wproj)
    pieces = {}
    for i, (name, which, start, stop, bits) in enumerate(MOVES):
        pieces[name] = Weights(
            at,
            weights[which].at[start:stop],
            weights2.at[which * width + start : which * width + stop],
            (weight_s.at[i], weight_r.at[i]),
            0,
            bits,
        )

    def weight(gi, i, start=0, stop=width):
        if gi:
            return weights2[i * width + start : i * width + stop, :]
        return weights[i][start:stop, :]

    vec_g = (vec, vec2)
    ways, sums = [], []
    for i, out in enumerate((block_out, input_grad)):
        rows_out = going.at[i]
        sums.append(AcrossSum(at, (cot_p, n2)[i], far.at[i], rows_out, (across_s.at[i], across_r.at[i])))
        ways.append(
            Outgoing(
                at,
                rows_out,
                out,
                (back_s.at[i], back_r.at[i]),
                back_l.at[i],
                (share_s.at[i], share_r.at[i]),
            )
        )
    out_across, dx_across = sums
    out_way, grad_way = ways
    outs = {"P": proj_total, "F": fc_total, "A": attn_total}
    room, index = 0, 0
    for name, kind, start, stop, order, early in TOTALS:
        first, at_row = {"P": (grads, 0), "F": (grads, 2 * width), "A": (grads2, 0)}[kind]
        pieces[name] = Total(
            at,
            first,
            [at_row + gi * width + start for gi in range(2)],
            outs[kind].at[start:stop],
            landing,
            room,
            (total_s, total_r),
            index,
            order,
            early,
        )
        more, sems = total_room(stop - start, n, early)
        room, index = room + more, index + sems

    def incoming(way, every, c):
        def first():
            if c < plan.split:
                way.start(c)

        def second():
            way.wait(c)
            every.start(c)

        return Steps(first, second, lambda: every.forward(c), lambda: every.finish(c))

    def outgoing(across, way, c):
        part_of = c - (CHUNKS - plan.split)

        def second():
            across.finish(c)
            way.start(c)

        def when_part(run):
            return lambda: run(part_of) if part_of >= 0 else None

        return Steps(
            lambda: across.start(c),
            second,
            when_part(way.share),
            when_part(way.forward),
            when_part(way.finish),
        )

    for c in range(CHUNKS):
        pieces["0123"[c]] = incoming(tok, tok_all, c)
        pieces["4567"[c]] = incoming(cot, cot_all, c)
        pieces["ijkl"[c]] = outgoing(out_across, out_way, c)
        pieces["rstu"[c]] = outgoing(dx_across, grad_way, c)

    hops = [{"mp": at.mate}, {"mp": at.across}]
    bit = 1
    while bit < n:
        high = lax.rem(at.d // bit, 2)
        hops.append({"dp": at.d + (1 - 2 * high) * bit})
        bit *= 2
    vec_total_sum = VecTotal(hops, vec_s, vec_r, vec_total, (vec_ss, vec_sr))
    pieces["v"] = vec_total_sum
    schedule = iter(SCHEDULE)

    def go():
        for name in next(schedule):
            pieces[name].step()

    def need(names):
        for name in names:
            pieces[name].finish()

    def begin(table, kind):
        for entry in table:
            if entry[1] == kind:
                pieces[entry[0]].step()

    def names_of(table, *kinds):
        return [entry[0] for entry in table if entry[1] in kinds]

    def row(i):
        return vec[i : i + 1, :]

    def add_line(line, value):
        vec_s[0, line : line + 1, :] += jnp.sum(value, axis=0, keepdims=True)

    def pack(c, buf):
        line = wrow[0:1, rows_at(at.mine(c), part_rows, LANES)].astype(F32)
        col = jnp.broadcast_to(line, (8, part_rows)).T[:, 0:1].astype(jnp.int32)
        return nn(pick(col, rows), buf[...])

    for c in range(CHUNKS):
        pieces["0123"[c]].step()
    for copy in fetch:
        copy.wait()
    begin(MOVES, 0)
    bias_copy = send(vec, vec2, (vec_ss, vec_sr), 0, {"mp": at.across})
    vec_s[0, :, :] = jnp.zeros((GLINES, width), F32)
    dq_acc[...] = jnp.zeros_like(dq_acc)
    qkv[...] = jnp.zeros_like(qkv)
    dout[...] = jnp.zeros_like(dout)
    line = slot_row[...]
    index = jnp.where(line < rows, plan.work_index(line) + 1, 0)
    digits = jnp.concatenate(
        [over(index, 64).astype(F32), under(index, 64).astype(F32), jnp.zeros((14, rows), F32)], axis=0
    ).astype(BF)
    begins = jnp.where(at.side == 0, 0, lengths[0, 0])
    count = jnp.where(at.side == 0, lengths[0, 0], lengths[0, 1])
    shift = lax.broadcasted_iota(jnp.int32, (rows, seq), 0) - begins
    chosen = jnp.where(shift == lax.broadcasted_iota(jnp.int32, (rows, seq), 1), 1.0, 0.0).astype(BF)
    moved = nn(digits, chosen)
    found = (moved[0:1, :] * 64.0 + moved[1:2, :]).astype(jnp.int32) - 1
    wrow[0:1, :] = jnp.where(lax.broadcasted_iota(jnp.int32, (1, seq), 1) < count, found, -1)
    go()
    need("0123")
    for c in range(HALVES):
        packed = pack(c, tokbuf)
        own_x[c * part_rows : (c + 1) * part_rows, :] = packed.astype(BF)
        normal, _ = normal_rows(packed)
        n1[rows_at(at.mine(c), part_rows), :] = (normal * row(V_LN1G) + row(V_LN1B)).astype(BF)
        n1_mate.start(c)
    go()
    for c in range(HALVES):
        n1_mate.finish(c)

    def project(gi):
        def one(i, carry):
            here = rows_at(i * TILE, TILE, TILE)
            there = rows_at(gi * seq + i * TILE, TILE, TILE)
            for j in range(3):
                made = nt(n1[here, :], weight(gi, 0, j * span, (j + 1) * span))
                made = made + vec_g[gi][V_QKVB : V_QKVB + 1, j * pad : j * pad + span]
                if j == 0:
                    made = made * HD**-0.5
                qkv[there, j * pad : j * pad + span] = made.astype(BF)
            turned = qkv[there, 2 * pad :].astype(F32).T.astype(BF)
            v_t[gi * span : (gi + 1) * span, here] = turned[0:span, :]
            return carry

        lax.fori_loop(0, seq // TILE, one, 0)

    key_line = lax.broadcasted_iota(jnp.int32, (TILE, TILE), 0)
    query_line = lax.broadcasted_iota(jnp.int32, (TILE, TILE), 1)
    seen = key_line <= query_line

    def attend(gi, i):
        q0, base = i * TILE, gi * seq
        cols = slice(q0, q0 + TILE)
        for h in range(plan.heads):
            lanes = (h // 2) * LANES
            q_lanes = slice(lanes, lanes + LANES)
            k_lanes = slice(pad + lanes, pad + lanes + LANES)
            vh = v_t.at[gi * span + h * HD : gi * span + (h + 1) * HD]
            qh = head_lanes(qkv[base + q0 : base + q0 + TILE, q_lanes], h % 2 == 1)
            near = jnp.where(seen, nt(qkv[base + q0 : base + q0 + TILE, k_lanes], qh), NEG)
            top = jnp.max(near, axis=0, keepdims=True)
            if i:
                old = nt(qkv[base : base + q0, k_lanes], qh)
                top = jnp.maximum(top, jnp.max(old, axis=0, keepdims=True))
            expo = jnp.exp2((near - top) * LOG2E)
            total = jnp.sum(expo, axis=0, keepdims=True)
            out = nn(vh[:, cols], expo.astype(BF))
            if i:
                expo = jnp.exp2((old - top) * LOG2E)
                total = total + jnp.sum(expo, axis=0, keepdims=True)
                out = out + nn(vh[:, 0:q0], expo.astype(BF))
            line = gi * 4 + h
            att_t[gi * span + h * HD : gi * span + (h + 1) * HD, cols] = (out * (1.0 / total)).astype(BF)
            lse[line : line + 1, cols] = top * LOG2E + jnp.log2(total)

    blocks = seq // TILE

    def merge(c):
        def one(i, carry):
            here = rows_at(c * plan.half + i * TILE, TILE, TILE)
            total = None
            for gi in range(2):
                att = att_t[gi * span : (gi + 1) * span, here].astype(F32).T.astype(BF)
                value = nn(att, weight(gi, 0, 3 * span, 4 * span))
                total = value if total is None else total + value
            term[here, :] = total.astype(BF)
            return carry

        lax.fori_loop(0, plan.half // TILE, one, 0)

    project(0)
    for i in range(blocks):
        go()
        attend(0, i)
    go()
    need(names_of(MOVES, 0))
    landed(vec2, (vec_ss, vec_sr), 0, {"mp": at.across})
    project(1)
    for i in range(blocks):
        go()
        attend(1, i)
    go()
    for c in range(HALVES):
        merge(c)
        attn_sum.start(c)
    go()
    need("4567")
    for c in range(HALVES):
        packed = pack(c, cotbuf)
        cot_p[rows_at(at.mine(c), part_rows), :] = packed.astype(BF)
        add_line(G_PROJB, packed)
        cot_mate.start(c)
        middle = own_x[c * part_rows : (c + 1) * part_rows, :].astype(F32) + (
            attn_sum.finish(c) + row(V_OUTB)
        )
        mid[c * part_rows : (c + 1) * part_rows, :] = middle
        normal, _ = normal_rows(middle)
        n2[rows_at(at.mine(c), part_rows), :] = (normal * row(V_LN2G) + row(V_LN2B)).astype(BF)
        n2_mate.start(c)
    attn_sum.drain()
    go()
    need(names_of(MOVES, 1, 2))
    tok_all.drain()
    cot_all.drain()
    for c in range(HALVES):
        n2_mate.finish(c)
        cot_mate.finish(c)

        def feed(i, carry, c=c):
            here = rows_at(c * plan.half + i * TILE, TILE, TILE)
            up, down = None, None
            for gi in range(2):
                there = rows_at(gi * seq + c * plan.half + i * TILE, TILE, TILE)
                v = nn(n2[here, :], weight(gi, 1)) + vec_g[gi][V_FCB : V_FCB + 1, :]
                square = v * v
                t = jnp.tanh(GELU * v * (1.0 + CUBE * square))
                halved = 0.5 * (1.0 + t)
                active = (v * halved).astype(BF)
                slope = halved + 0.5 * v * (1.0 - t * t) * (GELU * (1.0 + 3.0 * CUBE * square))
                act[there, :] = active
                more = nn(active, weight(gi, 2))
                up = more if up is None else up + more
                low = (nt(cot_p[here, :], weight(gi, 2)) * slope).astype(BF)
                dhid[there, :] = low
                add_line((G_FCB, G_FCB2)[gi], low.astype(F32))
                more = nt(low, weight(gi, 1))
                down = more if down is None else down + more
            mlp_term[here, :] = up.astype(BF)
            term[here, :] = down.astype(BF)
            return carry

        lax.fori_loop(0, plan.half // TILE, feed, 0)
        back_sum.start(c)
        mlp_sum.start(c)
        go()

    def weight_grad(left_ref, left_row, right_ref, right_row, dst, place):
        def one(i, carry):
            cols = rows_at(i * TILE, TILE, TILE)
            value = tn(left_ref[left_row : left_row + seq, cols], right_ref[right_row : right_row + seq, :])
            dst[rows_at(place + i * TILE, TILE, TILE), :] = value.astype(BF)
            return carry

        lax.fori_loop(0, width // TILE, one, 0)

    for gi in range(2):
        weight_grad(act, gi * seq, cot_p, 0, grads, gi * width)
    begin(TOTALS, "P")
    go()
    for c in range(HALVES):
        mine = slice(c * part_rows, (c + 1) * part_rows)
        where = rows_at(at.mine(c), part_rows)
        grad2 = back_sum.finish(c)
        middle = mid[mine, :]
        res[where, :] = (middle + (mlp_sum.finish(c) + row(V_PROJB))).astype(BF)
        res_mate.start(c)
        normal, inv = normal_rows(middle)
        grad_mid = cot_p[where, :].astype(F32) + norm_back(grad2, normal, inv, row(V_LN2G))
        low = grad_mid.astype(BF)
        mid[mine, :] = grad_mid
        dattn[where, :] = low
        dattn_mate.start(c)
        add_line(G_LN2G, grad2 * normal)
        add_line(G_LN2B, grad2)
        add_line(G_OUTB, low.astype(F32))
    mlp_sum.drain()
    go()
    for gi in range(2):
        weight_grad(n2, 0, dhid, gi * seq, grads, (2 + gi) * width)
    begin(TOTALS, "F")
    back_sum.drain()
    go()

    def unpack(c, part):
        start = c * chunk + at.core * (2 * own)
        part[c * 2 * own : (c + 1) * 2 * own, :] = nn(
            pick_rows(wrow[0:1, :], start, 2 * own), res[...]
        ).astype(BF)

    cot_mate.drain()
    for c in range(HALVES):
        res_mate.finish(c)
    for c in range(CHUNKS):
        unpack(c, cot_p)
        pieces["ijkl"[c]].step()
    go()
    for c in range(HALVES):
        dattn_mate.finish(c)
    for gi in range(2):

        def back_out(i, carry, gi=gi):
            here = rows_at(i * TILE, TILE, TILE)
            there = rows_at(gi * seq + i * TILE, TILE, TILE)
            low = nt(dattn[here, :], weight(gi, 0, 3 * span, 4 * span)).astype(BF)
            dout[there, 0:span] = low
            turned = dout[there, :].astype(F32).T
            both = turned[0:span, :] * att_t[gi * span : (gi + 1) * span, here].astype(F32)
            for h in range(plan.heads):
                line = gi * 4 + h
                delta[line : line + 1, here] = jnp.sum(both[h * HD : (h + 1) * HD, :], axis=0, keepdims=True)
            return carry

        lax.fori_loop(0, seq // TILE, back_out, 0)
        grads2[gi * width + 3 * span : gi * width + 4 * span, :] = nn(
            att_t[gi * span : (gi + 1) * span, :], dattn[...]
        ).astype(BF)

    def attend_back(gi, i):
        k0, base = i * TILE, gi * seq
        k_rows = slice(base + k0, base + k0 + TILE)
        parts = []
        for h in range(plan.heads):
            lanes = (h // 2) * LANES
            q_lanes = slice(lanes, lanes + LANES)
            kh = head_lanes(qkv[k_rows, pad + lanes : pad + lanes + LANES], h % 2 == 1)
            vh = head_lanes(qkv[k_rows, 2 * pad + lanes : 2 * pad + lanes + LANES], h % 2 == 1)
            if h % 2 == 0:
                turned = qkv[k_rows, pad + lanes : pad + lanes + LANES].astype(F32).T.astype(BF)
            kt = turned[(h % 2) * HD : (h % 2 + 1) * HD, :]
            line = gi * 4 + h
            dk = dv = None
            for q0, q1 in ((k0, k0 + TILE), (k0 + TILE, seq)):
                if q0 == q1:
                    continue
                q_all = qkv[base + q0 : base + q1, q_lanes]
                do_all = dout[base + q0 : base + q1, q_lanes]
                prob = jnp.exp2(nt(kh, q_all) * LOG2E - lse[line : line + 1, q0:q1])
                if q0 == k0:
                    prob = jnp.where(seen, prob, 0.0)
                low = (prob * (nt(vh, do_all) - delta[line : line + 1, q0:q1])).astype(BF)
                more_v, more_k = nn(prob.astype(BF), do_all), nn(low, q_all)
                dv = more_v if dv is None else dv + more_v
                dk = more_k if dk is None else dk + more_k
                dq_acc[gi * span + h * HD : gi * span + (h + 1) * HD, q0:q1] += nn(kt, low)
            parts.append((dk, dv))
        for h in range(0, plan.heads, 2):
            lanes = (h // 2) * LANES
            for j in range(2):
                value = head_lanes(parts[h][j], False)
                if h + 1 < plan.heads:
                    value = value + head_lanes(parts[h + 1][j], True)
                start = (1 + j) * pad + lanes
                dqkv[k_rows, start : start + LANES] = value.astype(BF)

    for gi in range(2):
        for i in range(blocks):
            go()
            attend_back(gi, i)
    go()
    for c in range(HALVES):

        def back_project(i, carry, c=c):
            here = rows_at(c * plan.half + i * TILE, TILE, TILE)
            total = None
            for gi in range(2):
                there = rows_at(gi * seq + c * plan.half + i * TILE, TILE, TILE)
                turned = jnp.concatenate(
                    [dq_acc[gi * span : (gi + 1) * span, here], jnp.zeros((pad - span, TILE), F32)], axis=0
                )
                dqkv[there, 0:pad] = (turned.T * HD**-0.5).astype(BF)
                add_line((G_QKVB, G_QKVB2)[gi], dqkv[there, :].astype(F32))
                for j in range(3):
                    more = nn(dqkv[there, j * pad : j * pad + span], weight(gi, 0, j * span, (j + 1) * span))
                    total = more if total is None else total + more
            term[here, :] = total.astype(BF)
            return carry

        lax.fori_loop(0, plan.half // TILE, back_project, 0)
        norm_sum.start(c)
    go()
    for c in range(HALVES):
        mine = slice(c * part_rows, (c + 1) * part_rows)
        grad1 = norm_sum.finish(c)
        normal, inv = normal_rows(own_x[mine, :].astype(F32))
        dx = mid[mine, :] + norm_back(grad1, normal, inv, row(V_LN1G))
        if c == 0:
            res_mate.drain()
        res[rows_at(at.mine(c), part_rows), :] = dx.astype(BF)
        dx_mate.start(c)
        add_line(G_LN1G, grad1 * normal)
        add_line(G_LN1B, grad1)
    bias_copy.wait_send()
    pieces["v"].step()
    go()
    n2_mate.drain()
    for c in range(HALVES):
        dx_mate.finish(c)
    for c in range(CHUNKS):
        unpack(c, n2)
        pieces["rstu"[c]].step()
    go()
    for gi in range(2):
        for j in range(3):
            row0 = gi * width + j * span
            grads2[row0 : row0 + span, :] = tn(
                dqkv[gi * seq : (gi + 1) * seq, j * pad : j * pad + span], n1[...]
            ).astype(BF)
    begin(TOTALS, "A")
    for _ in range(TAIL):
        go()
    need(pieces)
    out_way.drain()
    grad_way.drain()
    tok.drain()
    cot.drain()
    for each in (n1_mate, out_across, dattn_mate, dx_mate, norm_sum, dx_across):
        each.drain()


def finish_kernel(rows_a, rows_b, proj, fc, attn, out_a, out_b, proj_f, fc_f, qkv_f, out_f, sems):
    count = rows_a.shape[0] // COPIES
    copies = [
        pltpu.make_async_copy(
            src.at[pl.ds(i * count, count)], dst.at[pl.ds(i * count, count)], sems.at[which, i]
        )
        for which, (src, dst) in enumerate(((rows_a, out_a), (rows_b, out_b)))
        for i in range(COPIES)
    ]
    for copy in copies:
        copy.start()
    split = qkv_f.shape[0]
    proj_f[...] = proj[...].astype(F32)
    fc_f[...] = fc[...].astype(F32)
    qkv_f[...] = attn[0:split, :].astype(F32)
    out_f[...] = attn[split:, :].astype(F32)
    for copy in copies:
        copy.wait()


def body(
    tokens,
    cotangent,
    seq_lengths,
    source_slot,
    ln1_gain,
    ln1_bias,
    qkv_weight,
    qv_bias,
    output_projection_weight,
    out_bias,
    ln2_gain,
    ln2_bias,
    fc_weight,
    fc_bias,
    proj_weight,
    proj_bias,
):
    rows, width = tokens.shape
    span = qkv_weight.shape[2]
    n, members = lax.axis_size("dp"), lax.axis_size("mp")
    plan = Plan(n, members, rows, width, span // HD)
    pad, seq = plan.pad, plan.seq

    vectors = (ln1_gain, ln1_bias, out_bias, ln2_gain, ln2_bias, proj_bias, fc_bias)
    vec = jnp.concatenate(vectors + (jnp.zeros((width,), BF),)).astype(F32).reshape(8, width)
    vm = pl.BlockSpec(memory_space=pltpu.VMEM)
    hbm = pl.BlockSpec(memory_space=pl.ANY)
    shape = jax.ShapeDtypeStruct
    quarter = rows // members
    dma = pltpu.SemaphoreType.DMA
    rooms = [total_room(entry[3] - entry[2], n, entry[5]) for entry in TOTALS]
    landing, sems = (sum(room[i] for room in rooms) for i in range(2))
    hops = 2 + (n - 1).bit_length()

    def vmem(*dims, dtype=BF):
        return pltpu.VMEM(dims, dtype)

    block_out, input_grad, proj_total, fc_total, attn_total, vec_total = pl.pallas_call(
        functools.partial(block_kernel, plan),
        out_shape=(
            shape((rows, width), BF),
            shape((rows, width), BF),
            shape((width, width), BF),
            shape((width, width), BF),
            shape((width, width), BF),
            shape((8, width), F32),
        ),
        in_specs=[hbm, hbm, vm, pl.BlockSpec(memory_space=pltpu.SMEM), vm, vm, hbm, hbm, vm, vm],
        out_specs=(hbm,) * 5 + (vm,),
        scratch_shapes=[
            vmem(8, width, dtype=F32),
            vmem(8, seq, dtype=jnp.int32),
            vmem(width, width),
            vmem(8, width, dtype=F32),
            vmem(3 * width, width),
            vmem(rows, width),
            vmem(rows, width),
            vmem(quarter, width),
            vmem(seq, width),
            vmem(seq, width),
            vmem(seq, width),
            vmem(seq, width),
            vmem(2 * seq, 3 * pad),
            vmem(2 * span, seq),
            vmem(2 * span, seq),
            vmem(8, seq, dtype=F32),
            vmem(8, seq, dtype=F32),
            vmem(seq, width),
            vmem(seq // 2, width),
            vmem(seq // 2, width),
            vmem(seq // 2, width),
            vmem(seq // 2, width, dtype=F32),
            vmem(2 * seq, pad),
            vmem(2 * span, seq, dtype=F32),
            vmem(4 * width, width),
            vmem(landing, width),
            vmem(seq, width),
            vmem(2, quarter, width),
            vmem(2, quarter, width),
            vmem(hops, GLINES, width, dtype=F32),
            vmem(hops, GLINES, width, dtype=F32),
            dma((plan.split, n)),
            dma((CHUNKS, plan.in_chunk)),
            dma((plan.split, n)),
            dma((CHUNKS, plan.in_chunk)),
            dma((2, CHUNKS, 3)),
            dma((2, CHUNKS, 3)),
            dma((6, HALVES)),
            dma((6, HALVES)),
            dma((4, HALVES)),
            dma((4, HALVES)),
            dma((len(MOVES), 4)),
            dma((len(MOVES), 4)),
            dma((2, CHUNKS)),
            dma((2, CHUNKS)),
            dma((2, CHUNKS, plan.in_chunk)),
            dma((2, plan.split, n)),
            dma((2, plan.split)),
            dma((2, 3, plan.split, n)),
            dma((2, 3, plan.split, n)),
            dma((sems,)),
            dma((sems,)),
            dma((hops + 1,)),
            dma((hops + 1,)),
            dma((2,)),
        ],
        compiler_params=pltpu.CompilerParams(
            collective_id=0, has_side_effects=True, vmem_limit_bytes=VMEM_LIMIT
        ),
        name="block",
    )(
        tokens,
        cotangent,
        source_slot.reshape(1, rows),
        seq_lengths,
        vec,
        qv_bias,
        qkv_weight.transpose(1, 2, 0).reshape(3 * span, width),
        output_projection_weight,
        fc_weight,
        proj_weight,
    )
    block_out, input_grad, proj_grad, fc_grad, qkv_grad, out_grad = pl.pallas_call(
        finish_kernel,
        out_shape=(
            shape((rows, width), BF),
            shape((rows, width), BF),
            shape((width, width), F32),
            shape((width, width), F32),
            shape((3 * span, width), F32),
            shape((span, width), F32),
        ),
        in_specs=[hbm, hbm, vm, vm, vm],
        out_specs=(hbm, hbm, vm, vm, vm, vm),
        scratch_shapes=[dma((2, COPIES))],
        compiler_params=pltpu.CompilerParams(vmem_limit_bytes=VMEM_LIMIT // 2),
        name="finish",
    )(block_out, input_grad, proj_total, fc_total, attn_total)
    qkv_sums = vec_total[G_QKVB].reshape(3, pad)[:, :span]
    return (
        block_out,
        input_grad,
        vec_total[G_LN1G],
        vec_total[G_LN1B],
        qkv_grad.reshape(3, span, width).transpose(2, 0, 1),
        jnp.stack([qkv_sums[0], qkv_sums[2]]),
        out_grad,
        vec_total[G_OUTB],
        vec_total[G_LN2G],
        vec_total[G_LN2B],
        fc_grad,
        vec_total[G_FCB],
        proj_grad,
        vec_total[G_PROJB],
    )


def solution(mesh):
    return jax.shard_map(
        body,
        mesh=mesh,
        in_specs=(
            P("dp", None),
            P("dp", None),
            P("dp", None),
            P("dp"),
            P(),
            P(),
            P(None, None, "mp"),
            P(None, "mp"),
            P("mp", None),
            P(),
            P(),
            P(),
            P(None, "mp"),
            P("mp"),
            P("mp", None),
            P(),
        ),
        out_specs=(
            P("dp", None),
            P("dp", None),
            P(),
            P(),
            P(None, None, "mp"),
            P(None, "mp"),
            P("mp", None),
            P(),
            P(),
            P(),
            P(None, "mp"),
            P("mp"),
            P("mp", None),
            P(),
        ),
        check_vma=False,
    )
```

```python
import functools

import jax
import jax.numpy as jnp
from jax import lax
from jax.experimental import pallas as pl
from jax.experimental.pallas import tpu as pltpu
from jax.sharding import PartitionSpec as P

MESH = pl.DeviceIdType.MESH
BF = jnp.bfloat16
F32 = jnp.float32
HD = 64
EPSILON = 1e-05
NEG = -1e30
LOG2E = 1.4426950408889634
TILE = 256
HALVES = 2
STEPS = 4
CHUNKS = 4
LANES = 128
VMEM_LIMIT = 60 * 2**20


class Plan:
    def __init__(self, n, members, rows, width, heads):
        self.n, self.members, self.rows, self.width, self.heads = n, members, rows, width, heads
        self.slots = rows // n
        self.seq = rows // 2
        self.per = self.seq // n
        self.group = max(1, 32 // self.per)
        self.share = self.group * self.per // 2
        self.groups = n // self.group
        self.own = self.seq // (2 * CHUNKS)
        self.take = max(16, self.share // CHUNKS)
        self.split = self.share // self.take
        self.in_chunk = self.own // self.take
        self.half = self.seq // HALVES
        self.part = self.half // 2
        self.pad = -(-heads * HD // LANES) * LANES

    def come_index(self, source, turn):
        grp = over(source, self.group)
        inside = under(source, self.group) * self.per + turn
        core, row = over(inside, self.share), under(inside, self.share)
        chunk = over(grp, self.in_chunk) * self.split + over(row, self.take)
        return (
            (2 * chunk + core) * self.own
            + under(grp, self.in_chunk) * self.take
            + under(row, self.take)
        )

    def source_of(self, core):
        return (core * self.share) // self.per, lax.rem(core * self.share, self.per)


def over(x, size):
    return lax.shift_right_logical(x, jnp.full_like(x, size.bit_length() - 1))


def under(x, size):
    return x & (size - 1)


def nn(a, b):
    return lax.dot_general(a, b, (((1,), (0,)), ((), ())), preferred_element_type=F32)


def nt(a, b):
    return lax.dot_general(a, b, (((1,), (1,)), ((), ())), preferred_element_type=F32)


def tn(a, b):
    return lax.dot_general(a, b, (((0,), (0,)), ((), ())), preferred_element_type=F32)


def rows_at(start, count, step=16):
    if not isinstance(start, int):
        start = pl.multiple_of(start, step)
    return pl.ds(start, count)


class Place:
    def __init__(self, plan):
        self.plan = plan
        self.d = lax.axis_index("dp")
        self.m = lax.axis_index("mp")
        self.core = lax.rem(self.m, 2)
        self.side = self.m // 2
        self.mate = self.m + 1 - 2 * self.core
        self.across = lax.rem(self.m + 2, plan.members)
        self.source, self.offset = plan.source_of(self.core)

    def mine(self, c, flip=False):
        core = 1 - self.core if flip else self.core
        return (2 * c + core) * self.plan.part


def send(src, dst, sems, index, device):
    copy = pltpu.make_async_remote_copy(
        src_ref=src,
        dst_ref=dst,
        send_sem=sems[0].at[index],
        recv_sem=sems[1].at[index],
        device_id=device,
        device_id_type=MESH,
    )
    copy.start()
    return copy


def landed(dst, sems, index, device):
    pltpu.make_async_remote_copy(
        src_ref=dst,
        dst_ref=dst,
        send_sem=sems[0].at[index],
        recv_sem=sems[1].at[index],
        device_id=device,
        device_id_type=MESH,
    ).wait_recv()


def left(src, sems, index, device):
    pltpu.make_async_remote_copy(
        src_ref=src,
        dst_ref=src,
        send_sem=sems[0].at[index],
        recv_sem=sems[1].at[index],
        device_id=device,
        device_id_type=MESH,
    ).wait_send()


def entry_barrier(plan, at):
    barrier = pltpu.get_barrier_semaphore()

    def signal(j, carry):
        pl.semaphore_signal(
            barrier, inc=1, device_id={"dp": lax.rem(at.d + j, plan.n)}, device_id_type=MESH
        )
        return carry

    lax.fori_loop(1, plan.n, signal, 0)
    pl.semaphore_signal(barrier, inc=1, device_id={"mp": at.mate}, device_id_type=MESH)
    pl.semaphore_signal(barrier, inc=1, device_id={"mp": at.across}, device_id_type=MESH)
    pl.semaphore_wait(barrier, plan.n + 1)


class MateGather:
    def __init__(self, at, buf, sems, count):
        self.at, self.buf, self.sems, self.count, self.copies = at, buf, sems, count, []

    def rows(self, c, core):
        return self.buf.at[rows_at((2 * c + core) * self.count, self.count)]

    def start(self, c):
        here = self.rows(c, self.at.core)
        self.copies.append(send(here, here, self.sems, c, {"mp": self.at.mate}))

    def finish(self, c):
        landed(self.rows(c, 1 - self.at.core), self.sems, c, {"mp": self.at.mate})

    def drain(self):
        for copy in self.copies:
            copy.wait_send()
        self.copies = []


class MateSum:
    def __init__(self, at, term, land, sems):
        self.at, self.term, self.land, self.sems, self.copies = at, term, land, sems, []

    def start(self, c):
        plan, at = self.at.plan, self.at
        src = self.term.at[rows_at(at.mine(c, True), plan.part)]
        dst = self.land.at[rows_at(c * plan.part, plan.part)]
        self.copies.append(send(src, dst, self.sems, c, {"mp": at.mate}))

    def finish(self, c):
        plan, at = self.at.plan, self.at
        where = rows_at(c * plan.part, plan.part)
        landed(self.land.at[where], self.sems, c, {"mp": at.mate})
        mine = self.term[rows_at(at.mine(c), plan.part), :]
        return mine.astype(F32) + self.land[where, :].astype(F32)

    def drain(self):
        for copy in self.copies:
            copy.wait_send()
        self.copies = []


class Incoming:
    def __init__(self, at, source, sems, landing):
        plan = at.plan
        self.at, self.source, self.sems, self.landing = at, source, sems, landing
        self.sends = None
        if plan.group > 1:
            self.sends = lax.rem(at.d, plan.group) == at.source

    def guarded(self, run):
        if self.sends is None:
            run()
        else:
            pl.when(self.sends)(run)

    def mine(self, part):
        plan, at = self.at.plan, self.at
        grp = at.d // plan.group
        return (grp // plan.in_chunk) * plan.split + part, lax.rem(grp, plan.in_chunk)

    def piece(self, k, part):
        plan = self.at.plan
        start = k * plan.per + self.at.offset + part * plan.take
        return self.source.at[rows_at(start, plan.take)]

    def start(self, part):
        plan, at = self.at.plan, self.at
        c, gi = self.mine(part)

        def one(j, carry):
            k = lax.rem(at.d + j, plan.n)
            pltpu.make_async_remote_copy(
                src_ref=self.piece(k, part),
                dst_ref=self.landing(c, gi),
                send_sem=self.sems[0].at[part, j],
                recv_sem=self.sems[1].at[c, gi],
                device_id={"dp": k},
                device_id_type=MESH,
            ).start()
            return carry

        def run():
            lax.fori_loop(1, plan.n, one, 0)
            pltpu.make_async_copy(
                self.piece(at.d, part), self.landing(c, gi), self.sems[1].at[c, gi]
            ).start()

        self.guarded(run)

    def wait(self, c):
        plan, at = self.at.plan, self.at

        def one(gi, carry):
            landed(self.landing(c, gi), (self.sems[1], self.sems[1]), (c, gi), {"dp": at.d})
            return carry

        lax.fori_loop(0, plan.in_chunk, one, 0)

    def drain(self):
        plan, at = self.at.plan, self.at

        def run():
            for part in range(plan.split):

                def one(j, carry, part=part):
                    k = lax.rem(at.d + j, plan.n)
                    left(self.piece(k, part), (self.sems[0], self.sems[0]), (part, j), {"dp": k})
                    return carry

                lax.fori_loop(1, plan.n, one, 0)

        self.guarded(run)


class Outgoing:
    def __init__(self, at, rows_ref, out, sems, local_sem, share_sems):
        plan = at.plan
        self.at, self.rows_ref, self.out = at, rows_ref, out
        self.sems, self.local_sem, self.share_sems = sems, local_sem, share_sems

    def holds(self, member):
        plan = self.at.plan
        if plan.group == 1:
            return None
        return lax.rem(self.at.d, plan.group) == plan.source_of(lax.rem(member, 2))[0]

    def guarded(self, member, run):
        if self.at.plan.group == 1:
            run()
        else:
            pl.when(self.holds(member))(run)

    def place(self, k, part, member):
        plan = self.at.plan
        first = (member // 2) * plan.per + plan.source_of(lax.rem(member, 2))[1]
        start = k * plan.slots + first + part * plan.take
        return self.out.at[rows_at(start, plan.take)]

    def each(self, c, remote, local):
        plan, at = self.at.plan, self.at
        part = c % plan.split

        def one(gi, carry):
            grp = (c // plan.split) * plan.in_chunk + gi
            dest = grp * plan.group + at.source
            src = self.rows_ref.at[rows_at(c * plan.own + gi * plan.take, plan.take)]
            dst = self.place(at.d, part, at.m)
            pl.when(dest != at.d)(lambda: remote(gi, part, src, dst, dest))
            pl.when(dest == at.d)(lambda: local(gi, part, src, dst))
            return carry

        lax.fori_loop(0, plan.in_chunk, one, 0)

    def copy(self, c, gi, part, src, dst, dest):
        return pltpu.make_async_remote_copy(
            src_ref=src,
            dst_ref=dst,
            send_sem=self.sems[0].at[c, gi],
            recv_sem=self.sems[1].at[part, self.at.d],
            device_id={"dp": dest},
            device_id_type=MESH,
        )

    def start(self, c):
        def local(gi, part, src, dst):
            pltpu.make_async_copy(src, dst, self.local_sem.at[part]).start()

        self.each(c, lambda gi, part, src, dst, dest: self.copy(c, gi, part, src, dst, dest).start(), local)

    def drain(self):
        for c in range(CHUNKS):
            self.each(
                c,
                lambda gi, part, src, dst, dest: self.copy(c, gi, part, src, dst, dest).wait_send(),
                lambda gi, part, src, dst: None,
            )

    def loop(self, part, run):
        lax.fori_loop(0, self.at.plan.n, lambda k, carry: (run(k), carry)[1], 0)

    def share(self, part):
        at = self.at

        def run():
            def one(k):
                here = self.place(k, part, at.m)

                def remote():
                    landed(here, (self.sems[1], self.sems[1]), (part, k), {"dp": at.d})

                def local():
                    pltpu.make_async_copy(here, here, self.local_sem.at[part]).wait()

                pl.when(k != at.d)(remote)
                pl.when(k == at.d)(local)
                send(here, here, self.share_sems, (1, part, k), {"mp": at.across})
                send(here, here, self.share_sems, (0, part, k), {"mp": at.mate})

            self.loop(part, one)

        self.guarded(at.m, run)

    def forward(self, part):
        at = self.at

        def run():
            def one(k):
                there = self.place(k, part, at.across)
                landed(there, self.share_sems, (1, part, k), {"mp": at.across})
                send(there, there, self.share_sems, (2, part, k), {"mp": at.mate})

            self.loop(part, one)

        self.guarded(at.across, run)

    def finish(self, part):
        at = self.at
        corner = (1 - at.side) * 2 + 1 - at.core

        def near():
            self.loop(
                part,
                lambda k: landed(
                    self.place(k, part, at.mate), self.share_sems, (0, part, k), {"mp": at.mate}
                ),
            )

        def far():
            self.loop(
                part,
                lambda k: landed(
                    self.place(k, part, corner), self.share_sems, (2, part, k), {"mp": at.mate}
                ),
            )

        def sent():
            def one(k):
                here = self.place(k, part, at.m)
                left(here, self.share_sems, (1, part, k), {"mp": at.across})
                left(here, self.share_sems, (0, part, k), {"mp": at.mate})

            self.loop(part, one)

        def passed():
            self.loop(
                part,
                lambda k: left(
                    self.place(k, part, at.across), self.share_sems, (2, part, k), {"mp": at.mate}
                ),
            )

        self.guarded(at.mate, near)
        self.guarded(corner, far)
        self.guarded(at.m, sent)
        self.guarded(at.across, passed)


def halvings(rows, n, order):
    steps, size = [], rows
    bits = [1 << i for i in range((n - 1).bit_length())]
    for i in order:
        bits.insert(0, bits.pop(i))
    for bit in bits:
        if size % 32 == 0:
            size //= 2
            steps.append((bit, True, size))
        else:
            steps.append((bit, False, size))
    return steps


def trail_of(at, rows, order):
    offset, trail, size = 0, [], rows
    for bit, halve, size in halvings(rows, at.plan.n, order):
        if halve:
            high = lax.rem(at.d // bit, 2)
            partner = {"dp": at.d + (1 - 2 * high) * bit}
            trail.append((offset, offset + high * size, size, partner))
            offset = offset + high * size
    return offset, size, trail


class Steps:
    def __init__(self, *runs):
        self.runs, self.next = list(runs), 0

    def step(self):
        if self.next < len(self.runs):
            self.next += 1
            self.runs[self.next - 1]()

    def finish(self):
        while self.next < len(self.runs):
            self.step()


class Stepped:
    def __init__(self):
        self.jobs, self.next, self.pending = [], 0, None

    def step(self):
        if self.pending is not None:
            self.pending[0](self.pending[1])
            self.pending = None
        if self.next < len(self.jobs):
            start, end = self.jobs[self.next]
            self.next += 1
            self.pending = (end, start())

    def finish(self):
        while self.pending is not None or self.next < len(self.jobs):
            self.step()

    def spread(self, buf, keep, other, size, sems, index, partner, source=None, before_end=None):
        def start():
            here = buf.at[rows_at(keep, size)]
            return send(here if source is None else source, here, sems, index, partner)

        def end(copy):
            copy.wait_send()
            landed(buf.at[rows_at(other, size)], sems, index, partner)
            if before_end is not None:
                before_end()

        self.jobs.append((start, end))


class Weights(Stepped):
    def __init__(self, at, source, dst, sems, index, bits):
        super().__init__()
        offset, trail, size = 0, [], source.shape[0]
        for bit in bits:
            if bit < at.plan.n:
                size //= 2
                high = lax.rem(at.d // bit, 2)
                partner = {"dp": at.d + (1 - 2 * high) * bit}
                trail.append((offset, offset + high * size, size, partner))
                offset = offset + high * size
        slice_rows = rows_at(offset, size)
        across = {"mp": at.across}

        def start():
            return send(source.at[slice_rows], dst.at[slice_rows], sems, index, across)

        def end(copy):
            copy.wait_send()
            landed(dst.at[slice_rows], sems, index, across)

        self.jobs.append((start, end))
        for i, (before, keep, length, partner) in enumerate(reversed(trail)):
            self.spread(dst, keep, 2 * before + length - keep, length, sems, index + 1 + i, partner)


class Total(Stepped):
    def __init__(self, at, first, origins, out, landing, base, sems, index, order, early):
        super().__init__()
        self.at, self.landing = at, landing
        rows, n = out.shape[0], at.plan.n
        steps = halvings(rows, n, order)
        room = sum(size for _, _, size in steps)
        sources = [(first, origin) for origin in origins]
        if early:
            self.cross(sources, base, rows, (sems, index))
            sources, index, base = [(landing, base)], index + 1, base + rows
        lands = [base + i * room for i in range(len(sources))]
        for bit, halve, size in steps:
            high = lax.rem(at.d // bit, 2)
            partner = {"dp": at.d + (1 - 2 * high) * bit}
            keep = high * size if halve else 0
            give = (1 - high) * size if halve else 0
            self.exchange(sources, give, keep, size, list(lands), (sems, index), partner)
            index += len(sources)
            sources = [(landing, land) for land in lands]
            lands = [land + size for land in lands]
        offset, size, trail = trail_of(at, rows, order)
        if not early:
            self.cross(sources, base + 2 * room, size, (sems, index))
            sources, index = [(landing, base + 2 * room)], index + 1
        done = landing.at[rows_at(sources[0][1], size)]
        local = pltpu.make_async_copy(done, out.at[rows_at(offset, size)], sems[0].at[index])
        self.jobs[-1] = (self.jobs[-1][0], self.then(self.jobs[-1][1], local.start))
        index += 1
        for i, (before, keep, length, partner) in enumerate(reversed(trail)):
            source, settle = (done, local.wait) if i == 0 else (None, None)
            self.spread(
                out, keep, 2 * before + length - keep, length, sems, index + i, partner, source, settle
            )

    def then(self, end, more):
        def both(copy):
            end(copy)
            more()

        return both

    def add(self, first, origin, land, size):
        step = 96 if size % 96 == 0 else (32 if size % 32 == 0 else 16)

        def one(i, carry):
            here = rows_at(origin + i * step, step)
            there = rows_at(land + i * step, step)
            value = first[here, :].astype(F32) + self.landing[there, :].astype(F32)
            self.landing[there, :] = value.astype(BF)
            return carry

        lax.fori_loop(0, size // step, one, 0)

    def exchange(self, sources, give, keep, size, lands, sems, partner):
        sems, index = sems

        def start():
            return [
                send(
                    ref.at[rows_at(origin + give, size)],
                    self.landing.at[rows_at(land, size)],
                    sems,
                    index + i,
                    partner,
                )
                for i, ((ref, origin), land) in enumerate(zip(sources, lands))
            ]

        def end(copies):
            for copy, (ref, origin), land in zip(copies, sources, lands):
                copy.wait()
                self.add(ref, origin + keep, land, size)

        self.jobs.append((start, end))

    def cross(self, sources, land, size, sems):
        sems, index = sems
        (mine, mine_at), (theirs, theirs_at) = sources

        def start():
            return send(
                theirs.at[rows_at(theirs_at, size)],
                self.landing.at[rows_at(land, size)],
                sems,
                index,
                {"mp": self.at.across},
            )

        def end(copy):
            copy.wait()
            self.add(mine, mine_at, land, size)

        self.jobs.append((start, end))


def total_room(rows, n, early):
    steps = halvings(rows, n, ())
    size, spreads = steps[-1][2], sum(1 for _, halve, _ in steps if halve)
    room, groups = sum(step[2] for step in steps), 1 if early else 2
    return groups * room + (rows if early else size), groups * len(steps) + 2 + spreads


def normal_rows(x):
    centered = x - jnp.mean(x, axis=-1, keepdims=True)
    inv = lax.rsqrt(jnp.mean(centered * centered, axis=-1, keepdims=True) + EPSILON)
    return centered * inv, inv


def norm_back(grad, normal, inv, gain):
    scaled = grad * gain
    return inv * (
        scaled
        - jnp.mean(scaled, axis=-1, keepdims=True)
        - normal * jnp.mean(scaled * normal, axis=-1, keepdims=True)
    )


def pick(index_col, count):
    lanes = lax.broadcasted_iota(jnp.int32, (index_col.shape[0], count), 1)
    return jnp.where(lanes == index_col, 1.0, 0.0).astype(BF)


def pick_rows(index_row, first, count):
    lines = lax.broadcasted_iota(jnp.int32, (count, index_row.shape[1]), 0) + first
    return jnp.where(lines == index_row, 1.0, 0.0).astype(BF)


def head_lanes(x, odd):
    lane = lax.broadcasted_iota(jnp.int32, x.shape, 1)
    return jnp.where((lane >= HD) == odd, x, jnp.zeros_like(x))


V_LN1G, V_LN1B, V_OUTB, V_LN2G, V_LN2B, V_PROJB, V_FCB, V_QKVB = range(8)
G_LN1G, G_LN1B, G_LN2G, G_LN2B, G_OUTB, G_PROJB, G_FCB, G_QKVB, G_FCB2, G_QKVB2 = range(10)
SHARED = 6
MOVES = (
    ("a", 0, 0, 384, (1, 2)),
    ("b", 0, 384, 768, (1,)),
    ("f", 1, 0, 256, ()),
    ("g", 1, 256, 512, (2,)),
    ("h", 1, 512, 768, ()),
    ("p", 2, 0, 384, (2,)),
    ("q", 2, 384, 768, ()),
)
TOTALS = (
    ("F", "F", 0, 256, (), True),
    ("G", "F", 256, 512, (), True),
    ("H", "F", 512, 768, (), True),
    ("A", "A", 0, 256, (1,), True),
    ("B", "A", 256, 512, (), True),
    ("C", "A", 512, 768, (), True),
    ("P", "P", 0, 256, (), True),
    ("Q", "P", 256, 512, (), False),
    ("X", "P", 512, 768, (1,), False),
)
SCHEDULE = (
    "",
    "fghpqa",
    "4567b001f12ag23b3",
    "4h",
    "5",
    "4",
    "",
    "5",
    "ap6",
    "",
    "6",
    "7g",
    "",
    "7",
    "",
    "pq",
    "",
    "",
    "",
    "",
    "",
    "",
    "PQX",
    "",
    "i",
    "",
    "",
    "FPj",
    "k",
    "",
    "GQXl",
    "",
    "FP",
    "HQ",
    "G",
    "FXiPHiGrAsHtBuFBPAGCHABFjPCjGkHFkPAlvQCBlXGFHrAr",
    "GQsCsHBtQAXtCuvBvQuvAXvCBXC",
)
TAIL = 2
GLINES = 16
GELU = 0.7978845608028654
CUBE = 0.044715


class VecTotal(Stepped):
    def __init__(self, hops, given, taken, out, sems):
        super().__init__()
        line = lax.broadcasted_iota(jnp.int32, (8, out.shape[1]), 0)
        for i, device in enumerate(hops):

            def start(i=i, device=device):
                return send(given.at[i], taken.at[i], sems, i + 1, device)

            def end(copy, i=i):
                copy.wait()
                low, high = taken[i, 0:8, :], taken[i, 8:16, :]
                if i == 0:
                    low, high = jnp.where(line < SHARED, low, 0.0), jnp.zeros_like(high)
                elif i == 1:
                    low = jnp.concatenate([low[0:SHARED, :], high[0:2, :]], axis=0)
                    high = jnp.zeros_like(high)
                if i + 1 < len(hops):
                    given[i + 1, 0:8, :] = given[i, 0:8, :] + low
                    given[i + 1, 8:16, :] = given[i, 8:16, :] + high
                else:
                    out[...] = given[i, 0:8, :] + low

            self.jobs.append((start, end))


def block_kernel(
    plan,
    tokens,
    cotangent,
    slot_row,
    lengths,
    vec_in,
    qv_in,
    wqkv_in,
    wo_in,
    wfc,
    wproj,
    block_out,
    input_grad,
    proj_total,
    fc_total,
    attn_total,
    vec_total,
    tab,
    vec,
    tab_out,
    wrow,
    wattn,
    vec2,
    weights2,
    act,
    dhid,
    own_x,
    n1,
    cot_p,
    n2,
    dattn,
    qkv,
    v_t,
    att_t,
    lse,
    delta,
    term,
    land_a,
    land_b,
    land_c,
    mid,
    dout,
    dq_acc,
    grads,
    landing,
    res,
    going,
    vec_s,
    vec_r,
    tok_s,
    tok_r,
    cot_s,
    cot_r,
    ag_s,
    ag_r,
    mate_s,
    mate_r,
    sum_s,
    sum_r,
    weight_s,
    weight_r,
    tab_s,
    tab_r,
    back_s,
    back_r,
    back_l,
    share_s,
    share_r,
    total_s,
    total_r,
    vec_ss,
    vec_sr,
    local,
):
    at = Place(plan)
    rows, width, pad, seq = plan.rows, plan.width, plan.pad, plan.seq
    own, part_rows, per, slots = plan.own, plan.part, plan.per, plan.slots
    n = plan.n
    span = plan.heads * HD
    fetch = [
        pltpu.make_async_copy(wqkv_in, wattn.at[0 : 3 * span], local.at[0]),
        pltpu.make_async_copy(wo_in, wattn.at[3 * span : 4 * span], local.at[1]),
        pltpu.make_async_copy(tokens, act, local.at[2]),
        pltpu.make_async_copy(cotangent, dhid, local.at[3]),
    ]
    for copy in fetch:
        copy.start()
    vec[...] = vec_in[...].astype(F32)
    vec[V_QKVB : V_QKVB + 1, 0:span] = qv_in[0:1, :].astype(F32)
    vec[V_QKVB : V_QKVB + 1, 2 * pad : 2 * pad + span] = qv_in[1:2, :].astype(F32)
    entry_barrier(plan, at)
    dqkv, grads2 = act, dhid
    mlp_term = grads.at[2 * width : 2 * width + seq]
    tok_come, cot_come = grads.at[0:seq], grads.at[seq : 2 * seq]
    tok_stage, cot_stage = term, grads.at[2 * seq : 3 * seq]

    def come(buf):
        return lambda c, gi: buf.at[rows_at((2 * c + at.core) * own + gi * plan.take, plan.take)]

    tok = Incoming(at, tok_stage, (tok_s, tok_r), come(tok_come))
    cot = Incoming(at, cot_stage, (cot_s, cot_r), come(cot_come))
    tok_all = MateGather(at, tok_come, (ag_s.at[0], ag_r.at[0]), own)
    cot_all = MateGather(at, cot_come, (ag_s.at[1], ag_r.at[1]), own)
    n1_mate, cot_mate, n2_mate, dattn_mate, res_mate, dx_mate = (
        MateGather(at, buf, (mate_s.at[i], mate_r.at[i]), part_rows)
        for i, buf in enumerate((n1, cot_p, n2, dattn, res, res))
    )
    attn_sum, back_sum, mlp_sum, norm_sum = (
        MateSum(at, ref, land, (sum_s.at[i], sum_r.at[i]))
        for i, (ref, land) in enumerate(
            ((term, land_a), (term, land_b), (mlp_term, land_c), (term, land_a))
        )
    )
    weights = (wattn, wfc, wproj)
    pieces = {}
    for i, (name, which, start, stop, bits) in enumerate(MOVES):
        pieces[name] = Weights(
            at,
            weights[which].at[start:stop],
            weights2.at[which * width + start : which * width + stop],
            (weight_s.at[i], weight_r.at[i]),
            0,
            bits,
        )

    def weight(gi, i, start=0, stop=width):
        if gi:
            return weights2[i * width + start : i * width + stop, :]
        return weights[i][start:stop, :]

    vec_g = (vec, vec2)
    out_way, grad_way = (
        Outgoing(
            at,
            going.at[i],
            out,
            (back_s.at[i], back_r.at[i]),
            back_l.at[i],
            (share_s.at[i], share_r.at[i]),
        )
        for i, out in enumerate((block_out, input_grad))
    )
    outs = {"P": proj_total, "F": fc_total, "A": attn_total}
    room, index = 0, 0
    for name, kind, start, stop, order, early in TOTALS:
        first, at_row = {"P": (grads, 0), "F": (grads, 2 * width), "A": (grads2, 0)}[kind]
        pieces[name] = Total(
            at,
            first,
            [at_row + gi * width + start for gi in range(2)],
            outs[kind].at[start:stop],
            landing,
            room,
            (total_s, total_r),
            index,
            order,
            early,
        )
        more, sems = total_room(stop - start, n, early)
        room, index = room + more, index + sems

    def incoming(way, every, c):
        def first():
            if c < plan.split:
                way.start(c)

        def second():
            way.wait(c)
            every.start(c)

        return Steps(first, second, lambda: every.finish(c))

    def outgoing(way, c):
        part_of = c - (CHUNKS - plan.split)

        def when_part(run):
            return lambda: run(part_of) if part_of >= 0 else None

        return Steps(
            lambda: way.start(c),
            when_part(way.share),
            when_part(way.forward),
            when_part(way.finish),
        )

    for c in range(CHUNKS):
        pieces["0123"[c]] = incoming(tok, tok_all, c)
        pieces["4567"[c]] = incoming(cot, cot_all, c)
        pieces["ijkl"[c]] = outgoing(out_way, c)
        pieces["rstu"[c]] = outgoing(grad_way, c)

    hops = [{"mp": at.mate}, {"mp": at.across}]
    bit = 1
    while bit < n:
        high = lax.rem(at.d // bit, 2)
        hops.append({"dp": at.d + (1 - 2 * high) * bit})
        bit *= 2
    vec_total_sum = VecTotal(hops, vec_s, vec_r, vec_total, (vec_ss, vec_sr))
    pieces["v"] = vec_total_sum
    schedule = iter(SCHEDULE)

    def go():
        for name in next(schedule, ""):
            pieces[name].step()

    def need(names):
        for name in names:
            pieces[name].finish()

    def begin(table, kind):
        for entry in table:
            if entry[1] == kind:
                pieces[entry[0]].step()

    def names_of(table, *kinds):
        return [entry[0] for entry in table if entry[1] in kinds]

    def row(i):
        return vec[i : i + 1, :]

    def add_line(line, value):
        vec_s[0, line : line + 1, :] += jnp.sum(value, axis=0, keepdims=True)

    def pack(c, buf):
        line = wrow[0:1, rows_at(at.mine(c), part_rows, LANES)].astype(F32)
        col = jnp.broadcast_to(line, (8, part_rows)).T[:, 0:1].astype(jnp.int32)
        return nn(pick(col, seq), buf[...])

    fetch[0].wait()
    fetch[1].wait()
    begin(MOVES, 0)
    bias_copy = send(vec, vec2, (vec_ss, vec_sr), 0, {"mp": at.across})
    go()
    line = slot_row[...]
    index = jnp.where(line < rows, line + 1, 0)
    digits = jnp.concatenate(
        [over(index, 64).astype(F32), under(index, 64).astype(F32), jnp.zeros((14, rows), F32)], axis=0
    ).astype(BF)
    begins = jnp.where(at.side == 0, 0, lengths[0, 0])
    count = jnp.where(at.side == 0, lengths[0, 0], lengths[0, 1])
    shift = lax.broadcasted_iota(jnp.int32, (rows, seq), 0) - begins
    chosen = jnp.where(shift == lax.broadcasted_iota(jnp.int32, (rows, seq), 1), 1.0, 0.0).astype(BF)
    moved = nn(digits, chosen)
    slot = (moved[0:1, :] * 64.0 + moved[1:2, :]).astype(jnp.int32) - 1
    token = lax.broadcasted_iota(jnp.int32, (1, seq), 1)
    named = (token < count) & (slot >= 0)
    slot = jnp.where(named, slot, 0)
    source = jnp.where(named, over(slot, slots), -1)
    wrow[0:1, :] = jnp.where(named, plan.come_index(over(slot, slots), over(token, n)), -1)
    lines = over(lax.broadcasted_iota(jnp.int32, (8 * n, seq), 0), 8)
    told = jnp.where(lines == source, (under(slot, slots) + 1).astype(F32), 0.0).astype(BF)
    turn = over(lax.broadcasted_iota(jnp.int32, (seq, LANES), 0), n)
    turns = jnp.where(turn == lax.broadcasted_iota(jnp.int32, (seq, LANES), 1), 1.0, 0.0).astype(BF)
    tab_out[...] = nn(told, turns)

    def tell(j, carry):
        k = lax.rem(at.d + j, n)
        pltpu.make_async_remote_copy(
            src_ref=tab_out.at[rows_at(k * 8, 8, 8)],
            dst_ref=tab.at[at.side, rows_at(at.d * 8, 8, 8)],
            send_sem=tab_s.at[j],
            recv_sem=tab_r.at[at.d],
            device_id={"dp": k},
            device_id_type=MESH,
        ).start()
        return carry

    lax.fori_loop(1, n, tell, 0)
    tab[at.side, rows_at(at.d * 8, 8, 8), :] = tab_out[rows_at(at.d * 8, 8, 8), :]
    vec_s[0, :, :] = jnp.zeros((GLINES, width), F32)
    dq_acc[...] = jnp.zeros_like(dq_acc)
    qkv[...] = jnp.zeros_like(qkv)
    dout[...] = jnp.zeros_like(dout)

    def hear(j, carry):
        k = lax.rem(at.d + j, n)
        landed(tab.at[at.side, rows_at(k * 8, 8, 8)], (tab_s, tab_r), k, {"dp": k})
        return carry

    lax.fori_loop(1, n, hear, 0)

    def choose(buf, stage):
        def one(k, carry):
            col = tab[at.side, rows_at(k * 8, 8, 8), :].T[0:per, 0:1].astype(jnp.int32) - 1
            rows_of = nn(pick(col, slots), buf[rows_at(k * slots, slots), :])
            stage[rows_at(k * per, per), :] = rows_of.astype(BF)
            return carry

        lax.fori_loop(0, n, one, 0)

    fetch[2].wait()
    choose(act, tok_stage)
    for c in range(CHUNKS):
        pieces["0123"[c]].step()
    go()
    tab_copy = send(tab.at[at.side], tab.at[at.side], (tab_s, tab_r), n, {"mp": at.across})
    fetch[3].wait()
    choose(dhid, cot_stage)
    go()
    need("0123")
    for c in range(HALVES):
        packed = pack(c, tok_come)
        own_x[c * part_rows : (c + 1) * part_rows, :] = packed.astype(BF)
        normal, _ = normal_rows(packed)
        n1[rows_at(at.mine(c), part_rows), :] = (normal * row(V_LN1G) + row(V_LN1B)).astype(BF)
        n1_mate.start(c)
    go()
    for c in range(HALVES):
        n1_mate.finish(c)

    def project(gi):
        def one(i, carry):
            here = rows_at(i * TILE, TILE, TILE)
            there = rows_at(gi * seq + i * TILE, TILE, TILE)
            for j in range(3):
                made = nt(n1[here, :], weight(gi, 0, j * span, (j + 1) * span))
                made = made + vec_g[gi][V_QKVB : V_QKVB + 1, j * pad : j * pad + span]
                if j == 0:
                    made = made * HD**-0.5
                qkv[there, j * pad : j * pad + span] = made.astype(BF)
            turned = qkv[there, 2 * pad :].astype(F32).T.astype(BF)
            v_t[gi * span : (gi + 1) * span, here] = turned[0:span, :]
            return carry

        lax.fori_loop(0, seq // TILE, one, 0)

    key_line = lax.broadcasted_iota(jnp.int32, (TILE, TILE), 0)
    query_line = lax.broadcasted_iota(jnp.int32, (TILE, TILE), 1)
    seen = key_line <= query_line

    def attend(gi, i):
        q0, base = i * TILE, gi * seq
        cols = slice(q0, q0 + TILE)
        for h in range(plan.heads):
            lanes = (h // 2) * LANES
            q_lanes = slice(lanes, lanes + LANES)
            k_lanes = slice(pad + lanes, pad + lanes + LANES)
            vh = v_t.at[gi * span + h * HD : gi * span + (h + 1) * HD]
            qh = head_lanes(qkv[base + q0 : base + q0 + TILE, q_lanes], h % 2 == 1)
            near = jnp.where(seen, nt(qkv[base + q0 : base + q0 + TILE, k_lanes], qh), NEG)
            top = jnp.max(near, axis=0, keepdims=True)
            if i:
                old = nt(qkv[base : base + q0, k_lanes], qh)
                top = jnp.maximum(top, jnp.max(old, axis=0, keepdims=True))
            expo = jnp.exp2((near - top) * LOG2E)
            total = jnp.sum(expo, axis=0, keepdims=True)
            out = nn(vh[:, cols], expo.astype(BF))
            if i:
                expo = jnp.exp2((old - top) * LOG2E)
                total = total + jnp.sum(expo, axis=0, keepdims=True)
                out = out + nn(vh[:, 0:q0], expo.astype(BF))
            line = gi * 4 + h
            att_t[gi * span + h * HD : gi * span + (h + 1) * HD, cols] = (out * (1.0 / total)).astype(BF)
            lse[line : line + 1, cols] = top * LOG2E + jnp.log2(total)

    blocks = seq // TILE

    def merge(c):
        def one(i, carry):
            here = rows_at(c * plan.half + i * TILE, TILE, TILE)
            total = None
            for gi in range(2):
                att = att_t[gi * span : (gi + 1) * span, here].astype(F32).T.astype(BF)
                value = nn(att, weight(gi, 0, 3 * span, 4 * span))
                total = value if total is None else total + value
            term[here, :] = total.astype(BF)
            return carry

        lax.fori_loop(0, plan.half // TILE, one, 0)

    project(0)
    for i in range(blocks):
        go()
        attend(0, i)
    go()
    need(names_of(MOVES, 0))
    landed(vec2, (vec_ss, vec_sr), 0, {"mp": at.across})
    project(1)
    for i in range(blocks):
        go()
        attend(1, i)
    go()
    tok.drain()
    for c in range(HALVES):
        merge(c)
        attn_sum.start(c)
    go()
    need("4567")
    for c in range(HALVES):
        packed = pack(c, cot_come)
        cot_p[rows_at(at.mine(c), part_rows), :] = packed.astype(BF)
        add_line(G_PROJB, packed)
        cot_mate.start(c)
        middle = own_x[c * part_rows : (c + 1) * part_rows, :].astype(F32) + (
            attn_sum.finish(c) + row(V_OUTB)
        )
        mid[c * part_rows : (c + 1) * part_rows, :] = middle
        normal, _ = normal_rows(middle)
        n2[rows_at(at.mine(c), part_rows), :] = (normal * row(V_LN2G) + row(V_LN2B)).astype(BF)
        n2_mate.start(c)
    attn_sum.drain()
    go()
    need(names_of(MOVES, 1, 2))
    tok_all.drain()
    cot_all.drain()
    cot.drain()
    for c in range(HALVES):
        n2_mate.finish(c)
        cot_mate.finish(c)

        def feed(i, carry, c=c):
            here = rows_at(c * plan.half + i * TILE, TILE, TILE)
            up, down = None, None
            for gi in range(2):
                there = rows_at(gi * seq + c * plan.half + i * TILE, TILE, TILE)
                v = nn(n2[here, :], weight(gi, 1)) + vec_g[gi][V_FCB : V_FCB + 1, :]
                square = v * v
                t = jnp.tanh(GELU * v * (1.0 + CUBE * square))
                halved = 0.5 * (1.0 + t)
                active = (v * halved).astype(BF)
                slope = halved + 0.5 * v * (1.0 - t * t) * (GELU * (1.0 + 3.0 * CUBE * square))
                act[there, :] = active
                more = nn(active, weight(gi, 2))
                up = more if up is None else up + more
                low = (nt(cot_p[here, :], weight(gi, 2)) * slope).astype(BF)
                dhid[there, :] = low
                add_line((G_FCB, G_FCB2)[gi], low.astype(F32))
                more = nt(low, weight(gi, 1))
                down = more if down is None else down + more
            mlp_term[here, :] = up.astype(BF)
            term[here, :] = down.astype(BF)
            return carry

        lax.fori_loop(0, plan.half // TILE, feed, 0)
        back_sum.start(c)
        mlp_sum.start(c)
        go()

    def weight_grad(left_ref, left_row, right_ref, right_row, dst, place):
        def one(i, carry):
            cols = rows_at(i * TILE, TILE, TILE)
            value = tn(left_ref[left_row : left_row + seq, cols], right_ref[right_row : right_row + seq, :])
            dst[rows_at(place + i * TILE, TILE, TILE), :] = value.astype(BF)
            return carry

        lax.fori_loop(0, width // TILE, one, 0)

    for gi in range(2):
        weight_grad(act, gi * seq, cot_p, 0, grads, gi * width)
    begin(TOTALS, "P")
    go()
    for c in range(HALVES):
        mine = slice(c * part_rows, (c + 1) * part_rows)
        where = rows_at(at.mine(c), part_rows)
        grad2 = back_sum.finish(c)
        middle = mid[mine, :]
        res[where, :] = (middle + (mlp_sum.finish(c) + row(V_PROJB))).astype(BF)
        res_mate.start(c)
        normal, inv = normal_rows(middle)
        grad_mid = cot_p[where, :].astype(F32) + norm_back(grad2, normal, inv, row(V_LN2G))
        low = grad_mid.astype(BF)
        mid[mine, :] = grad_mid
        dattn[where, :] = low
        dattn_mate.start(c)
        add_line(G_LN2G, grad2 * normal)
        add_line(G_LN2B, grad2)
        add_line(G_OUTB, low.astype(F32))
    mlp_sum.drain()
    go()
    for gi in range(2):
        weight_grad(n2, 0, dhid, gi * seq, grads, (2 + gi) * width)
    begin(TOTALS, "F")
    back_sum.drain()
    go()

    def unpack(c, out):
        start = (2 * c + at.core) * own
        out[c * own : (c + 1) * own, :] = nn(pick_rows(wrow[0:1, :], start, own), res[...]).astype(BF)

    for c in range(HALVES):
        res_mate.finish(c)
    for c in range(CHUNKS):
        unpack(c, going.at[0])
        pieces["ijkl"[c]].step()
    go()
    for c in range(HALVES):
        dattn_mate.finish(c)
    for gi in range(2):

        def back_out(i, carry, gi=gi):
            here = rows_at(i * TILE, TILE, TILE)
            there = rows_at(gi * seq + i * TILE, TILE, TILE)
            low = nt(dattn[here, :], weight(gi, 0, 3 * span, 4 * span)).astype(BF)
            dout[there, 0:span] = low
            turned = dout[there, :].astype(F32).T
            both = turned[0:span, :] * att_t[gi * span : (gi + 1) * span, here].astype(F32)
            for h in range(plan.heads):
                line = gi * 4 + h
                delta[line : line + 1, here] = jnp.sum(both[h * HD : (h + 1) * HD, :], axis=0, keepdims=True)
            return carry

        lax.fori_loop(0, seq // TILE, back_out, 0)
        grads2[gi * width + 3 * span : gi * width + 4 * span, :] = nn(
            att_t[gi * span : (gi + 1) * span, :], dattn[...]
        ).astype(BF)

    def attend_back(gi, i):
        k0, base = i * TILE, gi * seq
        k_rows = slice(base + k0, base + k0 + TILE)
        parts = []
        for h in range(plan.heads):
            lanes = (h // 2) * LANES
            q_lanes = slice(lanes, lanes + LANES)
            kh = head_lanes(qkv[k_rows, pad + lanes : pad + lanes + LANES], h % 2 == 1)
            vh = head_lanes(qkv[k_rows, 2 * pad + lanes : 2 * pad + lanes + LANES], h % 2 == 1)
            if h % 2 == 0:
                turned = qkv[k_rows, pad + lanes : pad + lanes + LANES].astype(F32).T.astype(BF)
            kt = turned[(h % 2) * HD : (h % 2 + 1) * HD, :]
            line = gi * 4 + h
            dk = dv = None
            for q0, q1 in ((k0, k0 + TILE), (k0 + TILE, seq)):
                if q0 == q1:
                    continue
                q_all = qkv[base + q0 : base + q1, q_lanes]
                do_all = dout[base + q0 : base + q1, q_lanes]
                prob = jnp.exp2(nt(kh, q_all) * LOG2E - lse[line : line + 1, q0:q1])
                if q0 == k0:
                    prob = jnp.where(seen, prob, 0.0)
                low = (prob * (nt(vh, do_all) - delta[line : line + 1, q0:q1])).astype(BF)
                more_v, more_k = nn(prob.astype(BF), do_all), nn(low, q_all)
                dv = more_v if dv is None else dv + more_v
                dk = more_k if dk is None else dk + more_k
                dq_acc[gi * span + h * HD : gi * span + (h + 1) * HD, q0:q1] += nn(kt, low)
            parts.append((dk, dv))
        for h in range(0, plan.heads, 2):
            lanes = (h // 2) * LANES
            for j in range(2):
                value = head_lanes(parts[h][j], False)
                if h + 1 < plan.heads:
                    value = value + head_lanes(parts[h + 1][j], True)
                start = (1 + j) * pad + lanes
                dqkv[k_rows, start : start + LANES] = value.astype(BF)

    def qkv_weight_grad(gi):
        def turn_dq(i, carry):
            here = rows_at(i * TILE, TILE, TILE)
            there = rows_at(gi * seq + i * TILE, TILE, TILE)
            turned = jnp.concatenate(
                [dq_acc[gi * span : (gi + 1) * span, here], jnp.zeros((pad - span, TILE), F32)], axis=0
            )
            dqkv[there, 0:pad] = (turned.T * HD**-0.5).astype(BF)
            return carry

        lax.fori_loop(0, seq // TILE, turn_dq, 0)
        return lambda: weigh(gi)

    def weigh(gi):
        for j in range(3):
            row0 = gi * width + j * span
            grads2[row0 : row0 + span, :] = tn(
                dqkv[gi * seq : (gi + 1) * seq, j * pad : j * pad + span], n1[...]
            ).astype(BF)

    for i in range(blocks):
        go()
        attend_back(1, i)
    go()
    qkv_weight_grad(1)()
    for entry in TOTALS:
        if entry[1] == "A" and entry[5]:
            pieces[entry[0]].step()
    for i in range(blocks):
        go()
        attend_back(0, i)
    go()
    weigh_mine = qkv_weight_grad(0)
    for c in range(HALVES):

        def back_project(i, carry, c=c):
            here = rows_at(c * plan.half + i * TILE, TILE, TILE)
            total = None
            for gi in range(2):
                there = rows_at(gi * seq + c * plan.half + i * TILE, TILE, TILE)
                add_line((G_QKVB, G_QKVB2)[gi], dqkv[there, :].astype(F32))
                for j in range(3):
                    more = nn(dqkv[there, j * pad : j * pad + span], weight(gi, 0, j * span, (j + 1) * span))
                    total = more if total is None else total + more
            term[here, :] = total.astype(BF)
            return carry

        lax.fori_loop(0, plan.half // TILE, back_project, 0)
        norm_sum.start(c)
    go()
    for c in range(HALVES):
        mine = slice(c * part_rows, (c + 1) * part_rows)
        grad1 = norm_sum.finish(c)
        normal, inv = normal_rows(own_x[mine, :].astype(F32))
        dx = mid[mine, :] + norm_back(grad1, normal, inv, row(V_LN1G))
        if c == 0:
            res_mate.drain()
        res[rows_at(at.mine(c), part_rows), :] = dx.astype(BF)
        dx_mate.start(c)
        add_line(G_LN1G, grad1 * normal)
        add_line(G_LN1B, grad1)
    bias_copy.wait_send()
    pieces["v"].step()
    go()
    for c in range(HALVES):
        dx_mate.finish(c)
    for c in range(CHUNKS):
        unpack(c, going.at[1])
        pieces["rstu"[c]].step()
    go()
    weigh_mine()
    for entry in TOTALS:
        if entry[1] == "A" and not entry[5]:
            pieces[entry[0]].step()
    for _ in range(TAIL):
        go()
    need(pieces)
    out_way.drain()
    grad_way.drain()

    def told_all(j, carry):
        k = lax.rem(at.d + j, n)
        left(tab_out.at[rows_at(k * 8, 8, 8)], (tab_s, tab_r), j, {"dp": k})
        return carry

    lax.fori_loop(1, n, told_all, 0)
    tab_copy.wait_send()
    landed(tab.at[1 - at.side], (tab_s, tab_r), n, {"mp": at.across})
    for each in (n1_mate, cot_mate, n2_mate, dattn_mate, dx_mate, norm_sum):
        each.drain()


def finish_kernel(rows_a, rows_b, tab, proj, fc, qkv, out, out_a, out_b, proj_f, fc_f, qkv_f, out_f):
    proj_f[...] = proj[...].astype(F32)
    fc_f[...] = fc[...].astype(F32)
    qkv_f[...] = qkv[...].astype(F32)
    out_f[...] = out[...].astype(F32)
    n = tab.shape[1] // 8
    slots = rows_a.shape[0] // n

    def one(k, carry):
        here = rows_at(k * slots, slots)
        lines = [tab[side, rows_at(k * 8, 8, 8), :][0:1, 0 : slots // 2] for side in range(2)]
        slot = jnp.concatenate(lines, axis=1).astype(jnp.int32) - 1
        place = lax.broadcasted_iota(jnp.int32, (slots, slots), 0)
        hot = jnp.where(place == slot, 1.0, 0.0).astype(BF)
        out_a[here, :] = nn(hot, rows_a[here, :]).astype(BF)
        out_b[here, :] = nn(hot, rows_b[here, :]).astype(BF)
        return carry

    lax.fori_loop(0, n, one, 0)


def body(
    tokens,
    cotangent,
    seq_lengths,
    source_slot,
    ln1_gain,
    ln1_bias,
    qkv_weight,
    qv_bias,
    output_projection_weight,
    out_bias,
    ln2_gain,
    ln2_bias,
    fc_weight,
    fc_bias,
    proj_weight,
    proj_bias,
):
    rows, width = tokens.shape
    span = qkv_weight.shape[2]
    n, members = lax.axis_size("dp"), lax.axis_size("mp")
    plan = Plan(n, members, rows, width, span // HD)
    pad, seq = plan.pad, plan.seq

    vectors = (ln1_gain, ln1_bias, out_bias, ln2_gain, ln2_bias, proj_bias, fc_bias)
    line = jnp.arange(8, dtype=jnp.int32)[:, None]
    vec = jnp.zeros((8, width), BF)
    for i, v in enumerate(vectors):
        vec = jnp.where(line == i, v[None, :], vec)
    vm = pl.BlockSpec(memory_space=pltpu.VMEM)
    hbm = pl.BlockSpec(memory_space=pl.ANY)
    shape = jax.ShapeDtypeStruct
    quarter = rows // members
    dma = pltpu.SemaphoreType.DMA
    rooms = [total_room(entry[3] - entry[2], n, entry[5]) for entry in TOTALS]
    landing, sems = (sum(room[i] for room in rooms) for i in range(2))
    hops = 2 + (n - 1).bit_length()

    def vmem(*dims, dtype=BF):
        return pltpu.VMEM(dims, dtype)

    block_rows, grad_rows, proj_total, fc_total, attn_total, vec_total, tab = pl.pallas_call(
        functools.partial(block_kernel, plan),
        out_shape=(
            shape((rows, width), BF),
            shape((rows, width), BF),
            shape((width, width), BF),
            shape((width, width), BF),
            shape((width, width), BF),
            shape((8, width), F32),
            shape((2, 8 * n, LANES), F32),
        ),
        in_specs=[hbm, hbm, vm, pl.BlockSpec(memory_space=pltpu.SMEM), vm, vm, hbm, hbm, vm, vm],
        out_specs=(hbm,) * 5 + (vm, vm),
        scratch_shapes=[
            vmem(8, width, dtype=F32),
            vmem(8 * n, LANES, dtype=F32),
            vmem(8, seq, dtype=jnp.int32),
            vmem(width, width),
            vmem(8, width, dtype=F32),
            vmem(3 * width, width),
            vmem(rows, width),
            vmem(rows, width),
            vmem(quarter, width),
            vmem(seq, width),
            vmem(seq, width),
            vmem(seq, width),
            vmem(seq, width),
            vmem(2 * seq, 3 * pad),
            vmem(2 * span, seq),
            vmem(2 * span, seq),
            vmem(8, seq, dtype=F32),
            vmem(8, seq, dtype=F32),
            vmem(seq, width),
            vmem(seq // 2, width),
            vmem(seq // 2, width),
            vmem(seq // 2, width),
            vmem(seq // 2, width, dtype=F32),
            vmem(2 * seq, pad),
            vmem(2 * span, seq, dtype=F32),
            vmem(4 * width, width),
            vmem(landing, width),
            vmem(seq, width),
            vmem(2, quarter, width),
            vmem(hops, GLINES, width, dtype=F32),
            vmem(hops, GLINES, width, dtype=F32),
            dma((plan.split, n)),
            dma((CHUNKS, plan.in_chunk)),
            dma((plan.split, n)),
            dma((CHUNKS, plan.in_chunk)),
            dma((2, CHUNKS)),
            dma((2, CHUNKS)),
            dma((6, HALVES)),
            dma((6, HALVES)),
            dma((4, HALVES)),
            dma((4, HALVES)),
            dma((len(MOVES), 4)),
            dma((len(MOVES), 4)),
            dma((n + 1,)),
            dma((n + 1,)),
            dma((2, CHUNKS, plan.in_chunk)),
            dma((2, plan.split, n)),
            dma((2, plan.split)),
            dma((2, 3, plan.split, n)),
            dma((2, 3, plan.split, n)),
            dma((sems,)),
            dma((sems,)),
            dma((hops + 1,)),
            dma((hops + 1,)),
            dma((4,)),
        ],
        compiler_params=pltpu.CompilerParams(
            collective_id=0, has_side_effects=True, vmem_limit_bytes=VMEM_LIMIT
        ),
        name="block",
    )(
        tokens,
        cotangent,
        source_slot.reshape(1, rows),
        seq_lengths,
        vec,
        qv_bias,
        qkv_weight.transpose(1, 2, 0).reshape(3 * span, width),
        output_projection_weight,
        fc_weight,
        proj_weight,
    )
    def tall(count):
        return pl.BlockSpec((count // STEPS, width), lambda i: (i, 0))

    block_out, input_grad, proj_grad, fc_grad, qkv_grad, out_grad = pl.pallas_call(
        finish_kernel,
        out_shape=(
            shape((rows, width), BF),
            shape((rows, width), BF),
            shape((width, width), F32),
            shape((width, width), F32),
            shape((3 * span, width), F32),
            shape((span, width), F32),
        ),
        grid=(STEPS,),
        in_specs=[
            tall(rows),
            tall(rows),
            pl.BlockSpec((2, 8 * n // STEPS, LANES), lambda i: (0, i, 0)),
            tall(width),
            tall(width),
            tall(3 * span),
            pl.BlockSpec((span // STEPS, width), lambda i: (3 * STEPS + i, 0)),
        ],
        out_specs=(tall(rows), tall(rows), tall(width), tall(width), tall(3 * span), tall(span)),
        compiler_params=pltpu.CompilerParams(vmem_limit_bytes=VMEM_LIMIT),
        name="finish",
    )(block_rows, grad_rows, tab, proj_total, fc_total, attn_total, attn_total)
    qkv_sums = vec_total[G_QKVB].reshape(3, pad)[:, :span]
    return (
        block_out,
        input_grad,
        vec_total[G_LN1G],
        vec_total[G_LN1B],
        qkv_grad.reshape(3, span, width).transpose(2, 0, 1),
        jnp.stack([qkv_sums[0], qkv_sums[2]]),
        out_grad,
        vec_total[G_OUTB],
        vec_total[G_LN2G],
        vec_total[G_LN2B],
        fc_grad,
        vec_total[G_FCB],
        proj_grad,
        vec_total[G_PROJB],
    )


def solution(mesh):
    return jax.shard_map(
        body,
        mesh=mesh,
        in_specs=(
            P("dp", None),
            P("dp", None),
            P("dp", None),
            P("dp"),
            P(),
            P(),
            P(None, None, "mp"),
            P(None, "mp"),
            P("mp", None),
            P(),
            P(),
            P(),
            P(None, "mp"),
            P("mp"),
            P("mp", None),
            P(),
        ),
        out_specs=(
            P("dp", None),
            P("dp", None),
            P(),
            P(),
            P(None, None, "mp"),
            P(None, "mp"),
            P("mp", None),
            P(),
            P(),
            P(),
            P(None, "mp"),
            P("mp"),
            P("mp", None),
            P(),
        ),
        check_vma=False,
    )
```

```python
import functools

import jax
import jax.numpy as jnp
from jax import lax
from jax.experimental import pallas as pl
from jax.experimental.pallas import tpu as pltpu
from jax.sharding import PartitionSpec as P

MESH = pl.DeviceIdType.MESH
BF = jnp.bfloat16
F32 = jnp.float32
HD = 64
EPSILON = 1e-05
NEG = -1e30
LOG2E = 1.4426950408889634
TILE = 256
HALVES = 2
STEPS = 8
CHUNKS = 4
LANES = 128
VMEM_LIMIT = 60 * 2**20


class Plan:
    def __init__(self, n, members, rows, width, heads):
        self.n, self.members, self.rows, self.width, self.heads = n, members, rows, width, heads
        self.slots = rows // n
        self.seq = rows // 2
        self.per = self.seq // n
        self.group = max(1, 32 // self.per)
        self.share = self.group * self.per // 2
        self.groups = n // self.group
        self.own = self.seq // (2 * CHUNKS)
        self.take = max(16, self.share // CHUNKS)
        self.split = self.share // self.take
        self.in_chunk = self.own // self.take
        self.half = self.seq // HALVES
        self.part = self.half // 2
        self.pad = -(-heads * HD // LANES) * LANES

    def come_index(self, source, turn):
        grp = over(source, self.group)
        inside = under(source, self.group) * self.per + turn
        core, row = over(inside, self.share), under(inside, self.share)
        chunk = over(grp, self.in_chunk) * self.split + over(row, self.take)
        return (
            (2 * chunk + core) * self.own
            + under(grp, self.in_chunk) * self.take
            + under(row, self.take)
        )

    def source_of(self, core):
        return (core * self.share) // self.per, lax.rem(core * self.share, self.per)


def over(x, size):
    return lax.shift_right_logical(x, jnp.full_like(x, size.bit_length() - 1))


def under(x, size):
    return x & (size - 1)


def nn(a, b):
    return lax.dot_general(a, b, (((1,), (0,)), ((), ())), preferred_element_type=F32)


def nt(a, b):
    return lax.dot_general(a, b, (((1,), (1,)), ((), ())), preferred_element_type=F32)


def tn(a, b):
    return lax.dot_general(a, b, (((0,), (0,)), ((), ())), preferred_element_type=F32)


def rows_at(start, count, step=16):
    if not isinstance(start, int):
        start = pl.multiple_of(start, step)
    return pl.ds(start, count)


class Place:
    def __init__(self, plan):
        self.plan = plan
        self.d = lax.axis_index("dp")
        self.m = lax.axis_index("mp")
        self.core = lax.rem(self.m, 2)
        self.side = self.m // 2
        self.mate = self.m + 1 - 2 * self.core
        self.across = lax.rem(self.m + 2, plan.members)
        self.source, self.offset = plan.source_of(self.core)

    def mine(self, c, flip=False):
        core = 1 - self.core if flip else self.core
        return (2 * c + core) * self.plan.part


def send(src, dst, sems, index, device):
    copy = pltpu.make_async_remote_copy(
        src_ref=src,
        dst_ref=dst,
        send_sem=sems[0].at[index],
        recv_sem=sems[1].at[index],
        device_id=device,
        device_id_type=MESH,
    )
    copy.start()
    return copy


def landed(dst, sems, index, device):
    pltpu.make_async_remote_copy(
        src_ref=dst,
        dst_ref=dst,
        send_sem=sems[0].at[index],
        recv_sem=sems[1].at[index],
        device_id=device,
        device_id_type=MESH,
    ).wait_recv()


def left(src, sems, index, device):
    pltpu.make_async_remote_copy(
        src_ref=src,
        dst_ref=src,
        send_sem=sems[0].at[index],
        recv_sem=sems[1].at[index],
        device_id=device,
        device_id_type=MESH,
    ).wait_send()


def greet(plan, at):
    barrier = pltpu.get_barrier_semaphore()

    def signal(j, carry):
        pl.semaphore_signal(
            barrier, inc=1, device_id={"dp": lax.rem(at.d + j, plan.n)}, device_id_type=MESH
        )
        return carry

    lax.fori_loop(1, plan.n, signal, 0)
    pl.semaphore_signal(barrier, inc=1, device_id={"mp": at.mate}, device_id_type=MESH)
    pl.semaphore_signal(barrier, inc=1, device_id={"mp": at.across}, device_id_type=MESH)


def all_here(plan):
    pl.semaphore_wait(pltpu.get_barrier_semaphore(), plan.n + 1)


class MateGather:
    def __init__(self, at, buf, sems, count):
        self.at, self.buf, self.sems, self.count, self.copies = at, buf, sems, count, []

    def rows(self, c, core):
        return self.buf.at[rows_at((2 * c + core) * self.count, self.count)]

    def start(self, c):
        here = self.rows(c, self.at.core)
        self.copies.append(send(here, here, self.sems, c, {"mp": self.at.mate}))

    def finish(self, c):
        landed(self.rows(c, 1 - self.at.core), self.sems, c, {"mp": self.at.mate})

    def drain(self):
        for copy in self.copies:
            copy.wait_send()
        self.copies = []


class MateSum:
    def __init__(self, at, term, land, sems):
        self.at, self.term, self.land, self.sems, self.copies = at, term, land, sems, []

    def start(self, c):
        plan, at = self.at.plan, self.at
        src = self.term.at[rows_at(at.mine(c, True), plan.part)]
        dst = self.land.at[rows_at(c * plan.part, plan.part)]
        self.copies.append(send(src, dst, self.sems, c, {"mp": at.mate}))

    def finish(self, c):
        plan, at = self.at.plan, self.at
        where = rows_at(c * plan.part, plan.part)
        landed(self.land.at[where], self.sems, c, {"mp": at.mate})
        mine = self.term[rows_at(at.mine(c), plan.part), :]
        return mine.astype(F32) + self.land[where, :].astype(F32)

    def drain(self):
        for copy in self.copies:
            copy.wait_send()
        self.copies = []


class Incoming:
    def __init__(self, at, source, sems, landing):
        plan = at.plan
        self.at, self.source, self.sems, self.landing = at, source, sems, landing
        self.sends = None
        if plan.group > 1:
            self.sends = lax.rem(at.d, plan.group) == at.source

    def guarded(self, run):
        if self.sends is None:
            run()
        else:
            pl.when(self.sends)(run)

    def mine(self, part):
        plan, at = self.at.plan, self.at
        grp = at.d // plan.group
        return (grp // plan.in_chunk) * plan.split + part, lax.rem(grp, plan.in_chunk)

    def piece(self, k, part):
        plan = self.at.plan
        start = k * plan.per + self.at.offset + part * plan.take
        return self.source.at[rows_at(start, plan.take)]

    def start(self, part):
        plan, at = self.at.plan, self.at
        c, gi = self.mine(part)

        def one(j, carry):
            k = lax.rem(at.d + j, plan.n)
            pltpu.make_async_remote_copy(
                src_ref=self.piece(k, part),
                dst_ref=self.landing(c, gi),
                send_sem=self.sems[0].at[part, j],
                recv_sem=self.sems[1].at[c, gi],
                device_id={"dp": k},
                device_id_type=MESH,
            ).start()
            return carry

        def run():
            lax.fori_loop(1, plan.n, one, 0)
            pltpu.make_async_copy(
                self.piece(at.d, part), self.landing(c, gi), self.sems[1].at[c, gi]
            ).start()

        self.guarded(run)

    def wait(self, c):
        plan, at = self.at.plan, self.at

        def one(gi, carry):
            landed(self.landing(c, gi), (self.sems[1], self.sems[1]), (c, gi), {"dp": at.d})
            return carry

        lax.fori_loop(0, plan.in_chunk, one, 0)

    def drain(self):
        plan, at = self.at.plan, self.at

        def run():
            for part in range(plan.split):

                def one(j, carry, part=part):
                    k = lax.rem(at.d + j, plan.n)
                    left(self.piece(k, part), (self.sems[0], self.sems[0]), (part, j), {"dp": k})
                    return carry

                lax.fori_loop(1, plan.n, one, 0)

        self.guarded(run)


class Outgoing:
    def __init__(self, at, rows_ref, out, sems, local_sem, share_sems):
        plan = at.plan
        self.at, self.rows_ref, self.out = at, rows_ref, out
        self.sems, self.local_sem, self.share_sems = sems, local_sem, share_sems

    def holds(self, member):
        plan = self.at.plan
        if plan.group == 1:
            return None
        return lax.rem(self.at.d, plan.group) == plan.source_of(lax.rem(member, 2))[0]

    def guarded(self, member, run):
        if self.at.plan.group == 1:
            run()
        else:
            pl.when(self.holds(member))(run)

    def place(self, k, part, member):
        plan = self.at.plan
        first = (member // 2) * plan.per + plan.source_of(lax.rem(member, 2))[1]
        start = k * plan.slots + first + part * plan.take
        return self.out.at[rows_at(start, plan.take)]

    def each(self, c, remote, local):
        plan, at = self.at.plan, self.at
        part = c % plan.split

        def one(gi, carry):
            grp = (c // plan.split) * plan.in_chunk + gi
            dest = grp * plan.group + at.source
            src = self.rows_ref.at[rows_at(c * plan.own + gi * plan.take, plan.take)]
            dst = self.place(at.d, part, at.m)
            pl.when(dest != at.d)(lambda: remote(gi, part, src, dst, dest))
            pl.when(dest == at.d)(lambda: local(gi, part, src, dst))
            return carry

        lax.fori_loop(0, plan.in_chunk, one, 0)

    def copy(self, c, gi, part, src, dst, dest):
        return pltpu.make_async_remote_copy(
            src_ref=src,
            dst_ref=dst,
            send_sem=self.sems[0].at[c, gi],
            recv_sem=self.sems[1].at[part, self.at.d],
            device_id={"dp": dest},
            device_id_type=MESH,
        )

    def start(self, c):
        def local(gi, part, src, dst):
            pltpu.make_async_copy(src, dst, self.local_sem.at[part]).start()

        self.each(c, lambda gi, part, src, dst, dest: self.copy(c, gi, part, src, dst, dest).start(), local)

    def drain(self):
        for c in range(CHUNKS):
            self.each(
                c,
                lambda gi, part, src, dst, dest: self.copy(c, gi, part, src, dst, dest).wait_send(),
                lambda gi, part, src, dst: None,
            )

    def loop(self, part, run):
        lax.fori_loop(0, self.at.plan.n, lambda k, carry: (run(k), carry)[1], 0)

    def share(self, part):
        at = self.at

        def run():
            def one(k):
                here = self.place(k, part, at.m)

                def remote():
                    landed(here, (self.sems[1], self.sems[1]), (part, k), {"dp": at.d})

                def local():
                    pltpu.make_async_copy(here, here, self.local_sem.at[part]).wait()

                pl.when(k != at.d)(remote)
                pl.when(k == at.d)(local)
                send(here, here, self.share_sems, (1, part, k), {"mp": at.across})
                send(here, here, self.share_sems, (0, part, k), {"mp": at.mate})

            self.loop(part, one)

        self.guarded(at.m, run)

    def forward(self, part):
        at = self.at

        def run():
            def one(k):
                there = self.place(k, part, at.across)
                landed(there, self.share_sems, (1, part, k), {"mp": at.across})
                send(there, there, self.share_sems, (2, part, k), {"mp": at.mate})

            self.loop(part, one)

        self.guarded(at.across, run)

    def finish(self, part):
        at = self.at
        corner = (1 - at.side) * 2 + 1 - at.core

        def near():
            self.loop(
                part,
                lambda k: landed(
                    self.place(k, part, at.mate), self.share_sems, (0, part, k), {"mp": at.mate}
                ),
            )

        def far():
            self.loop(
                part,
                lambda k: landed(
                    self.place(k, part, corner), self.share_sems, (2, part, k), {"mp": at.mate}
                ),
            )

        def sent():
            def one(k):
                here = self.place(k, part, at.m)
                left(here, self.share_sems, (1, part, k), {"mp": at.across})
                left(here, self.share_sems, (0, part, k), {"mp": at.mate})

            self.loop(part, one)

        def passed():
            self.loop(
                part,
                lambda k: left(
                    self.place(k, part, at.across), self.share_sems, (2, part, k), {"mp": at.mate}
                ),
            )

        self.guarded(at.mate, near)
        self.guarded(corner, far)
        self.guarded(at.m, sent)
        self.guarded(at.across, passed)


def halvings(rows, n, order):
    steps, size = [], rows
    bits = [1 << i for i in range((n - 1).bit_length())]
    for i in order:
        bits.insert(0, bits.pop(i))
    for bit in bits:
        if size % 32 == 0:
            size //= 2
            steps.append((bit, True, size))
        else:
            steps.append((bit, False, size))
    return steps


def trail_of(at, rows, order):
    offset, trail, size = 0, [], rows
    for bit, halve, size in halvings(rows, at.plan.n, order):
        if halve:
            high = lax.rem(at.d // bit, 2)
            partner = {"dp": at.d + (1 - 2 * high) * bit}
            trail.append((offset, offset + high * size, size, partner))
            offset = offset + high * size
    return offset, size, trail


class Steps:
    def __init__(self, *runs):
        self.runs, self.next = list(runs), 0

    def step(self):
        if self.next < len(self.runs):
            self.next += 1
            self.runs[self.next - 1]()

    def finish(self):
        while self.next < len(self.runs):
            self.step()


class Stepped:
    def __init__(self):
        self.jobs, self.next, self.pending = [], 0, None

    def step(self):
        if self.pending is not None:
            self.pending[0](self.pending[1])
            self.pending = None
        if self.next < len(self.jobs):
            start, end = self.jobs[self.next]
            self.next += 1
            self.pending = (end, start())

    def finish(self):
        while self.pending is not None or self.next < len(self.jobs):
            self.step()

    def spread(self, buf, keep, other, size, sems, index, partner, source=None, before_end=None):
        def start():
            here = buf.at[rows_at(keep, size)]
            return send(here if source is None else source, here, sems, index, partner)

        def end(copy):
            copy.wait_send()
            landed(buf.at[rows_at(other, size)], sems, index, partner)
            if before_end is not None:
                before_end()

        self.jobs.append((start, end))


class Weights(Stepped):
    def __init__(self, at, source, dst, sems, index, bits):
        super().__init__()
        offset, trail, size = 0, [], source.shape[0]
        for bit in bits:
            if bit < at.plan.n:
                size //= 2
                high = lax.rem(at.d // bit, 2)
                partner = {"dp": at.d + (1 - 2 * high) * bit}
                trail.append((offset, offset + high * size, size, partner))
                offset = offset + high * size
        slice_rows = rows_at(offset, size)
        across = {"mp": at.across}

        def start():
            return send(source.at[slice_rows], dst.at[slice_rows], sems, index, across)

        def end(copy):
            copy.wait_send()
            landed(dst.at[slice_rows], sems, index, across)

        self.jobs.append((start, end))
        for i, (before, keep, length, partner) in enumerate(reversed(trail)):
            self.spread(dst, keep, 2 * before + length - keep, length, sems, index + 1 + i, partner)


class Total(Stepped):
    def __init__(self, at, first, origins, out, landing, base, sems, index, order, early):
        super().__init__()
        self.at, self.landing = at, landing
        rows, n = out.shape[0], at.plan.n
        steps = halvings(rows, n, order)
        room = sum(size for _, _, size in steps)
        sources = [(first, origin) for origin in origins]
        if early:
            self.cross(sources, base, rows, (sems, index))
            sources, index, base = [(landing, base)], index + 1, base + rows
        lands = [base + i * room for i in range(len(sources))]
        for bit, halve, size in steps:
            high = lax.rem(at.d // bit, 2)
            partner = {"dp": at.d + (1 - 2 * high) * bit}
            keep = high * size if halve else 0
            give = (1 - high) * size if halve else 0
            self.exchange(sources, give, keep, size, list(lands), (sems, index), partner)
            index += len(sources)
            sources = [(landing, land) for land in lands]
            lands = [land + size for land in lands]
        offset, size, trail = trail_of(at, rows, order)
        if not early:
            self.cross(sources, base + 2 * room, size, (sems, index))
            sources, index = [(landing, base + 2 * room)], index + 1
        done = landing.at[rows_at(sources[0][1], size)]
        local = pltpu.make_async_copy(done, out.at[rows_at(offset, size)], sems[0].at[index])
        self.jobs[-1] = (self.jobs[-1][0], self.then(self.jobs[-1][1], local.start))
        index += 1
        for i, (before, keep, length, partner) in enumerate(reversed(trail)):
            source, settle = (done, local.wait) if i == 0 else (None, None)
            self.spread(
                out, keep, 2 * before + length - keep, length, sems, index + i, partner, source, settle
            )

    def then(self, end, more):
        def both(copy):
            end(copy)
            more()

        return both

    def add(self, first, origin, land, size):
        step = 96 if size % 96 == 0 else (32 if size % 32 == 0 else 16)

        def one(i, carry):
            here = rows_at(origin + i * step, step)
            there = rows_at(land + i * step, step)
            value = first[here, :].astype(F32) + self.landing[there, :].astype(F32)
            self.landing[there, :] = value.astype(BF)
            return carry

        lax.fori_loop(0, size // step, one, 0)

    def exchange(self, sources, give, keep, size, lands, sems, partner):
        sems, index = sems

        def start():
            return [
                send(
                    ref.at[rows_at(origin + give, size)],
                    self.landing.at[rows_at(land, size)],
                    sems,
                    index + i,
                    partner,
                )
                for i, ((ref, origin), land) in enumerate(zip(sources, lands))
            ]

        def end(copies):
            for copy, (ref, origin), land in zip(copies, sources, lands):
                copy.wait()
                self.add(ref, origin + keep, land, size)

        self.jobs.append((start, end))

    def cross(self, sources, land, size, sems):
        sems, index = sems
        (mine, mine_at), (theirs, theirs_at) = sources

        def start():
            return send(
                theirs.at[rows_at(theirs_at, size)],
                self.landing.at[rows_at(land, size)],
                sems,
                index,
                {"mp": self.at.across},
            )

        def end(copy):
            copy.wait()
            self.add(mine, mine_at, land, size)

        self.jobs.append((start, end))


def total_room(rows, n, early):
    steps = halvings(rows, n, ())
    size, spreads = steps[-1][2], sum(1 for _, halve, _ in steps if halve)
    room, groups = sum(step[2] for step in steps), 1 if early else 2
    return groups * room + (rows if early else size), groups * len(steps) + 2 + spreads


def normal_rows(x):
    centered = x - jnp.mean(x, axis=-1, keepdims=True)
    inv = lax.rsqrt(jnp.mean(centered * centered, axis=-1, keepdims=True) + EPSILON)
    return centered * inv, inv


def norm_back(grad, normal, inv, gain):
    scaled = grad * gain
    return inv * (
        scaled
        - jnp.mean(scaled, axis=-1, keepdims=True)
        - normal * jnp.mean(scaled * normal, axis=-1, keepdims=True)
    )


def pick(index_col, count):
    lanes = lax.broadcasted_iota(jnp.int32, (index_col.shape[0], count), 1)
    return jnp.where(lanes == index_col, 1.0, 0.0).astype(BF)


def pick_rows(index_row, first, count):
    lines = lax.broadcasted_iota(jnp.int32, (count, index_row.shape[1]), 0) + first
    return jnp.where(lines == index_row, 1.0, 0.0).astype(BF)


def head_lanes(x, odd):
    lane = lax.broadcasted_iota(jnp.int32, x.shape, 1)
    return jnp.where((lane >= HD) == odd, x, jnp.zeros_like(x))


V_LN1G, V_LN1B, V_OUTB, V_LN2G, V_LN2B, V_PROJB, V_FCB, V_QKVB = range(8)
G_LN1G, G_LN1B, G_LN2G, G_LN2B, G_OUTB, G_PROJB, G_FCB, G_QKVB, G_FCB2, G_QKVB2 = range(10)
SHARED = 6
MOVES = (
    ("a", 0, 0, 256, (2,)),
    ("b", 0, 256, 512, (1,)),
    ("c", 0, 512, 768, (1,)),
    ("f", 1, 0, 384, (2, 1)),
    ("g", 1, 384, 768, (1,)),
    ("p", 2, 0, 768, ()),
)
TOTALS = (
    ("F", "F", 0, 256, (), True),
    ("G", "F", 256, 512, (), True),
    ("H", "F", 512, 768, (), True),
    ("A", "A", 0, 256, (1,), True),
    ("B", "A", 256, 512, (), True),
    ("C", "A", 512, 768, (), True),
    ("P", "P", 0, 256, (), False),
    ("Q", "P", 256, 512, (), True),
    ("X", "P", 512, 768, (1,), False),
)
SCHEDULE = (
    "",
    "fgpa",
    "b045670c1f12b23ag3",
    "4c",
    "",
    "54",
    "",
    "f",
    "65",
    "",
    "6",
    "7",
    "",
    "7g",
    "",
    "pf",
    "",
    "",
    "",
    "",
    "",
    "",
    "",
    "",
    "QPX",
    "",
    "",
    "F",
    "",
    "Q",
    "",
    "G",
    "PX",
    "jkil",
    "FQ",
    "HP",
    "G",
    "FXQHAGrsBHtuCBFQjACGjAHBkFkQiCiGlvQFAPXlHBGFrCrH",
    "AsGPsXtHBPtCAuvBXvuCvPvABXC",
)
TAIL = 2
GLINES = 16
GELU = 0.7978845608028654
CUBE = 0.044715


class VecTotal(Stepped):
    def __init__(self, hops, given, taken, out, sems):
        super().__init__()
        line = lax.broadcasted_iota(jnp.int32, (8, out.shape[1]), 0)
        for i, device in enumerate(hops):

            def start(i=i, device=device):
                return send(given.at[i], taken.at[i], sems, i + 1, device)

            def end(copy, i=i):
                copy.wait()
                low, high = taken[i, 0:8, :], taken[i, 8:16, :]
                if i == 0:
                    low, high = jnp.where(line < SHARED, low, 0.0), jnp.zeros_like(high)
                elif i == 1:
                    low = jnp.concatenate([low[0:SHARED, :], high[0:2, :]], axis=0)
                    high = jnp.zeros_like(high)
                if i + 1 < len(hops):
                    given[i + 1, 0:8, :] = given[i, 0:8, :] + low
                    given[i + 1, 8:16, :] = given[i, 8:16, :] + high
                else:
                    out[...] = given[i, 0:8, :] + low

            self.jobs.append((start, end))


def list_slots(plan, at, slot_row, lengths, wrow, tab_out):
    n, rows, seq, slots = plan.n, plan.rows, plan.seq, plan.slots
    line = jnp.broadcast_to(slot_row[...], (8, rows))
    begins = jnp.where(at.side == 0, 0, lengths[0, 0])
    count = jnp.where(at.side == 0, lengths[0, 0], lengths[0, 1])
    back = rows - begins
    bit = 1
    while bit < rows:
        turn_it = jnp.broadcast_to(back & bit, line.shape) != 0
        line = jnp.where(turn_it, pltpu.roll(line, bit, 1), line)
        bit *= 2
    slot = line[0:1, 0:seq]
    token = lax.broadcasted_iota(jnp.int32, (1, seq), 1)
    named = (token < count) & (slot < rows)
    slot = jnp.where(named, slot, 0)
    source = jnp.where(named, over(slot, slots), -1)
    wrow[0:1, :] = jnp.where(named, plan.come_index(over(slot, slots), over(token, n)), -1)
    lines = over(lax.broadcasted_iota(jnp.int32, (8 * n, seq), 0), 8)
    told = jnp.where(lines == source, (under(slot, slots) + 1).astype(F32), 0.0).astype(BF)
    turn = over(lax.broadcasted_iota(jnp.int32, (seq, LANES), 0), n)
    turns = jnp.where(turn == lax.broadcasted_iota(jnp.int32, (seq, LANES), 1), 1.0, 0.0).astype(BF)
    tab_out[...] = nn(told, turns)


def block_kernel(
    plan,
    tokens,
    cotangent,
    slot_row,
    lengths,
    vec_in,
    qv_in,
    wqkv_in,
    wo_in,
    wfc,
    wproj,
    block_out,
    input_grad,
    proj_total,
    fc_total,
    attn_total,
    vec_total,
    tab,
    vec,
    tab_out,
    wrow,
    wattn,
    vec2,
    weights2,
    act,
    dhid,
    own_x,
    n1,
    cot_p,
    n2,
    dattn,
    qkv,
    v_t,
    att_t,
    lse,
    delta,
    term,
    land_a,
    land_b,
    land_c,
    mid,
    dout,
    dq_acc,
    grads,
    landing,
    res,
    going,
    vec_s,
    vec_r,
    tok_s,
    tok_r,
    cot_s,
    cot_r,
    ag_s,
    ag_r,
    mate_s,
    mate_r,
    sum_s,
    sum_r,
    weight_s,
    weight_r,
    tab_s,
    tab_r,
    back_s,
    back_r,
    back_l,
    share_s,
    share_r,
    total_s,
    total_r,
    vec_ss,
    vec_sr,
    local,
):
    at = Place(plan)
    rows, width, pad, seq = plan.rows, plan.width, plan.pad, plan.seq
    own, part_rows, per, slots = plan.own, plan.part, plan.per, plan.slots
    n = plan.n
    span = plan.heads * HD
    fetch = [
        pltpu.make_async_copy(wqkv_in, wattn.at[0 : 3 * span], local.at[0]),
        pltpu.make_async_copy(wo_in, wattn.at[3 * span : 4 * span], local.at[1]),
        pltpu.make_async_copy(tokens, act, local.at[2]),
        pltpu.make_async_copy(cotangent, dhid, local.at[3]),
    ]
    for copy in fetch:
        copy.start()
    vec[...] = vec_in[...].astype(F32)
    vec[V_QKVB : V_QKVB + 1, 0:span] = qv_in[0:1, :].astype(F32)
    vec[V_QKVB : V_QKVB + 1, 2 * pad : 2 * pad + span] = qv_in[1:2, :].astype(F32)
    greet(plan, at)
    list_slots(plan, at, slot_row, lengths, wrow, tab_out)
    all_here(plan)
    dqkv, grads2 = act, dhid
    mlp_term = grads.at[2 * width : 2 * width + seq]
    tok_come, cot_come = grads.at[0:seq], grads.at[seq : 2 * seq]
    tok_stage, cot_stage = term, grads.at[2 * seq : 3 * seq]

    def come(buf):
        return lambda c, gi: buf.at[rows_at((2 * c + at.core) * own + gi * plan.take, plan.take)]

    tok = Incoming(at, tok_stage, (tok_s, tok_r), come(tok_come))
    cot = Incoming(at, cot_stage, (cot_s, cot_r), come(cot_come))
    tok_all = MateGather(at, tok_come, (ag_s.at[0], ag_r.at[0]), own)
    cot_all = MateGather(at, cot_come, (ag_s.at[1], ag_r.at[1]), own)
    n1_mate, cot_mate, n2_mate, dattn_mate, res_mate, dx_mate = (
        MateGather(at, buf, (mate_s.at[i], mate_r.at[i]), part_rows)
        for i, buf in enumerate((n1, cot_p, n2, dattn, res, res))
    )
    attn_sum, back_sum, mlp_sum, norm_sum = (
        MateSum(at, ref, land, (sum_s.at[i], sum_r.at[i]))
        for i, (ref, land) in enumerate(
            ((term, land_a), (term, land_b), (mlp_term, land_c), (term, land_a))
        )
    )
    weights = (wattn, wfc, wproj)
    pieces = {}
    for i, (name, which, start, stop, bits) in enumerate(MOVES):
        pieces[name] = Weights(
            at,
            weights[which].at[start:stop],
            weights2.at[which * width + start : which * width + stop],
            (weight_s.at[i], weight_r.at[i]),
            0,
            bits,
        )

    def weight(gi, i, start=0, stop=width):
        if gi:
            return weights2[i * width + start : i * width + stop, :]
        return weights[i][start:stop, :]

    vec_g = (vec, vec2)
    out_way, grad_way = (
        Outgoing(
            at,
            going.at[i],
            out,
            (back_s.at[i], back_r.at[i]),
            back_l.at[i],
            (share_s.at[i], share_r.at[i]),
        )
        for i, out in enumerate((block_out, input_grad))
    )
    outs = {"P": proj_total, "F": fc_total, "A": attn_total}
    room, index = 0, 0
    for name, kind, start, stop, order, early in TOTALS:
        first, at_row = {"P": (grads, 0), "F": (grads, 2 * width), "A": (grads2, 0)}[kind]
        pieces[name] = Total(
            at,
            first,
            [at_row + gi * width + start for gi in range(2)],
            outs[kind].at[start:stop],
            landing,
            room,
            (total_s, total_r),
            index,
            order,
            early,
        )
        more, sems = total_room(stop - start, n, early)
        room, index = room + more, index + sems

    def incoming(way, every, c):
        def first():
            if c < plan.split:
                way.start(c)

        def second():
            way.wait(c)
            every.start(c)

        return Steps(first, second, lambda: every.finish(c))

    def outgoing(way, c):
        part_of = c - (CHUNKS - plan.split)

        def when_part(run):
            return lambda: run(part_of) if part_of >= 0 else None

        return Steps(
            lambda: way.start(c),
            when_part(way.share),
            when_part(way.forward),
            when_part(way.finish),
        )

    for c in range(CHUNKS):
        pieces["0123"[c]] = incoming(tok, tok_all, c)
        pieces["4567"[c]] = incoming(cot, cot_all, c)
        pieces["ijkl"[c]] = outgoing(out_way, c)
        pieces["rstu"[c]] = outgoing(grad_way, c)

    hops = [{"mp": at.mate}, {"mp": at.across}]
    bit = 1
    while bit < n:
        high = lax.rem(at.d // bit, 2)
        hops.append({"dp": at.d + (1 - 2 * high) * bit})
        bit *= 2
    vec_total_sum = VecTotal(hops, vec_s, vec_r, vec_total, (vec_ss, vec_sr))
    pieces["v"] = vec_total_sum
    schedule = iter(SCHEDULE)

    def go():
        for name in next(schedule, ""):
            pieces[name].step()

    def need(names):
        for name in names:
            pieces[name].finish()

    def begin(table, kind, early=None):
        for entry in table:
            if entry[1] == kind and early in (None, entry[-1]):
                pieces[entry[0]].step()

    def names_of(table, *kinds):
        return [entry[0] for entry in table if entry[1] in kinds]

    def row(i):
        return vec[i : i + 1, :]

    def add_line(line, value):
        vec_s[0, line : line + 1, :] += jnp.sum(value, axis=0, keepdims=True)

    def pack(c, buf):
        line = wrow[0:1, rows_at(at.mine(c), part_rows, LANES)].astype(F32)
        col = jnp.broadcast_to(line, (8, part_rows)).T[:, 0:1].astype(jnp.int32)
        return nn(pick(col, seq), buf[...])

    fetch[0].wait()
    fetch[1].wait()
    begin(MOVES, 0)
    bias_copy = send(vec, vec2, (vec_ss, vec_sr), 0, {"mp": at.across})
    go()
    def tell(j, carry):
        k = lax.rem(at.d + j, n)
        pltpu.make_async_remote_copy(
            src_ref=tab_out.at[rows_at(k * 8, 8, 8)],
            dst_ref=tab.at[at.side, rows_at(at.d * 8, 8, 8)],
            send_sem=tab_s.at[j],
            recv_sem=tab_r.at[at.d],
            device_id={"dp": k},
            device_id_type=MESH,
        ).start()
        return carry

    lax.fori_loop(1, n, tell, 0)
    tab[at.side, rows_at(at.d * 8, 8, 8), :] = tab_out[rows_at(at.d * 8, 8, 8), :]
    vec_s[0, :, :] = jnp.zeros((GLINES, width), F32)
    dq_acc[...] = jnp.zeros_like(dq_acc)
    qkv[...] = jnp.zeros_like(qkv)
    dout[...] = jnp.zeros_like(dout)

    def hear(j, carry):
        k = lax.rem(at.d + j, n)
        landed(tab.at[at.side, rows_at(k * 8, 8, 8)], (tab_s, tab_r), k, {"dp": k})
        return carry

    lax.fori_loop(1, n, hear, 0)

    def choose(buf, stage):
        def one(k, carry):
            col = tab[at.side, rows_at(k * 8, 8, 8), :].T[0:per, 0:1].astype(jnp.int32) - 1
            rows_of = nn(pick(col, slots), buf[rows_at(k * slots, slots), :])
            stage[rows_at(k * per, per), :] = rows_of.astype(BF)
            return carry

        lax.fori_loop(0, n, one, 0)

    fetch[2].wait()
    choose(act, tok_stage)
    for c in range(CHUNKS):
        pieces["0123"[c]].step()
    go()
    tab_copy = send(tab.at[at.side], tab.at[at.side], (tab_s, tab_r), n, {"mp": at.across})
    fetch[3].wait()
    choose(dhid, cot_stage)
    go()
    need("0123")
    for c in range(HALVES):
        packed = pack(c, tok_come)
        own_x[c * part_rows : (c + 1) * part_rows, :] = packed.astype(BF)
        normal, _ = normal_rows(packed)
        n1[rows_at(at.mine(c), part_rows), :] = (normal * row(V_LN1G) + row(V_LN1B)).astype(BF)
        n1_mate.start(c)
    go()
    for c in range(HALVES):
        n1_mate.finish(c)

    def project(gi):
        def one(i, carry):
            here = rows_at(i * TILE, TILE, TILE)
            there = rows_at(gi * seq + i * TILE, TILE, TILE)
            for j in range(3):
                made = nt(n1[here, :], weight(gi, 0, j * span, (j + 1) * span))
                made = made + vec_g[gi][V_QKVB : V_QKVB + 1, j * pad : j * pad + span]
                if j == 0:
                    made = made * HD**-0.5
                qkv[there, j * pad : j * pad + span] = made.astype(BF)
            turned = qkv[there, 2 * pad :].astype(F32).T.astype(BF)
            v_t[gi * span : (gi + 1) * span, here] = turned[0:span, :]
            return carry

        lax.fori_loop(0, seq // TILE, one, 0)

    key_line = lax.broadcasted_iota(jnp.int32, (TILE, TILE), 0)
    query_line = lax.broadcasted_iota(jnp.int32, (TILE, TILE), 1)
    seen = key_line <= query_line

    def attend(gi, i):
        q0, base = i * TILE, gi * seq
        cols = slice(q0, q0 + TILE)
        for h in range(plan.heads):
            lanes = (h // 2) * LANES
            q_lanes = slice(lanes, lanes + LANES)
            k_lanes = slice(pad + lanes, pad + lanes + LANES)
            vh = v_t.at[gi * span + h * HD : gi * span + (h + 1) * HD]
            qh = head_lanes(qkv[base + q0 : base + q0 + TILE, q_lanes], h % 2 == 1)
            near = jnp.where(seen, nt(qkv[base + q0 : base + q0 + TILE, k_lanes], qh), NEG)
            top = jnp.max(near, axis=0, keepdims=True)
            if i:
                old = nt(qkv[base : base + q0, k_lanes], qh)
                top = jnp.maximum(top, jnp.max(old, axis=0, keepdims=True))
            expo = jnp.exp2((near - top) * LOG2E)
            total = jnp.sum(expo, axis=0, keepdims=True)
            out = nn(vh[:, cols], expo.astype(BF))
            if i:
                expo = jnp.exp2((old - top) * LOG2E)
                total = total + jnp.sum(expo, axis=0, keepdims=True)
                out = out + nn(vh[:, 0:q0], expo.astype(BF))
            line = gi * 4 + h
            att_t[gi * span + h * HD : gi * span + (h + 1) * HD, cols] = (out * (1.0 / total)).astype(BF)
            lse[line : line + 1, cols] = top * LOG2E + jnp.log2(total)

    blocks = seq // TILE

    def merge(c):
        def one(i, carry):
            here = rows_at(c * plan.half + i * TILE, TILE, TILE)
            total = None
            for gi in range(2):
                att = att_t[gi * span : (gi + 1) * span, here].astype(F32).T.astype(BF)
                value = nn(att, weight(gi, 0, 3 * span, 4 * span))
                total = value if total is None else total + value
            term[here, :] = total.astype(BF)
            return carry

        lax.fori_loop(0, plan.half // TILE, one, 0)

    project(0)
    for i in range(blocks):
        go()
        attend(0, i)
    go()
    need(names_of(MOVES, 0))
    landed(vec2, (vec_ss, vec_sr), 0, {"mp": at.across})
    project(1)
    for i in range(blocks):
        go()
        attend(1, i)
    go()
    tok.drain()
    for c in range(HALVES):
        merge(c)
        attn_sum.start(c)
    go()
    need("4567")
    for c in range(HALVES):
        packed = pack(c, cot_come)
        cot_p[rows_at(at.mine(c), part_rows), :] = packed.astype(BF)
        add_line(G_PROJB, packed)
        cot_mate.start(c)
        middle = own_x[c * part_rows : (c + 1) * part_rows, :].astype(F32) + (
            attn_sum.finish(c) + row(V_OUTB)
        )
        mid[c * part_rows : (c + 1) * part_rows, :] = middle
        normal, _ = normal_rows(middle)
        n2[rows_at(at.mine(c), part_rows), :] = (normal * row(V_LN2G) + row(V_LN2B)).astype(BF)
        n2_mate.start(c)
    attn_sum.drain()
    go()
    need(names_of(MOVES, 1, 2))
    tok_all.drain()
    cot_all.drain()
    cot.drain()
    for c in range(HALVES):
        n2_mate.finish(c)
        cot_mate.finish(c)

        def feed(i, carry, c=c):
            here = rows_at(c * plan.half + i * TILE, TILE, TILE)
            up, down = None, None
            for gi in range(2):
                there = rows_at(gi * seq + c * plan.half + i * TILE, TILE, TILE)
                v = nn(n2[here, :], weight(gi, 1)) + vec_g[gi][V_FCB : V_FCB + 1, :]
                square = v * v
                t = jnp.tanh(GELU * v * (1.0 + CUBE * square))
                halved = 0.5 * (1.0 + t)
                active = (v * halved).astype(BF)
                slope = halved + 0.5 * v * (1.0 - t * t) * (GELU * (1.0 + 3.0 * CUBE * square))
                act[there, :] = active
                more = nn(active, weight(gi, 2))
                up = more if up is None else up + more
                low = (nt(cot_p[here, :], weight(gi, 2)) * slope).astype(BF)
                dhid[there, :] = low
                add_line((G_FCB, G_FCB2)[gi], low.astype(F32))
                more = nt(low, weight(gi, 1))
                down = more if down is None else down + more
            mlp_term[here, :] = up.astype(BF)
            term[here, :] = down.astype(BF)
            return carry

        lax.fori_loop(0, plan.half // TILE, feed, 0)
        back_sum.start(c)
        mlp_sum.start(c)
        go()

    def weight_grad(left_ref, left_row, right_ref, right_row, dst, place):
        def one(i, carry):
            cols = rows_at(i * TILE, TILE, TILE)
            value = tn(left_ref[left_row : left_row + seq, cols], right_ref[right_row : right_row + seq, :])
            dst[rows_at(place + i * TILE, TILE, TILE), :] = value.astype(BF)
            return carry

        lax.fori_loop(0, width // TILE, one, 0)

    for gi in (1, 0):
        weight_grad(act, gi * seq, cot_p, 0, grads, gi * width)
        if gi:
            begin(TOTALS, "P", True)
            go()
    begin(TOTALS, "P", False)
    go()
    for c in range(HALVES):
        mine = slice(c * part_rows, (c + 1) * part_rows)
        where = rows_at(at.mine(c), part_rows)
        grad2 = back_sum.finish(c)
        middle = mid[mine, :]
        res[where, :] = (middle + (mlp_sum.finish(c) + row(V_PROJB))).astype(BF)
        res_mate.start(c)
        normal, inv = normal_rows(middle)
        grad_mid = cot_p[where, :].astype(F32) + norm_back(grad2, normal, inv, row(V_LN2G))
        low = grad_mid.astype(BF)
        mid[mine, :] = grad_mid
        dattn[where, :] = low
        dattn_mate.start(c)
        add_line(G_LN2G, grad2 * normal)
        add_line(G_LN2B, grad2)
        add_line(G_OUTB, low.astype(F32))
    mlp_sum.drain()
    go()
    for gi in (1, 0):
        weight_grad(n2, 0, dhid, gi * seq, grads, (2 + gi) * width)
        if gi:
            begin(TOTALS, "F", True)
            go()
    begin(TOTALS, "F", False)
    back_sum.drain()
    go()

    def unpack(c, out):
        start = (2 * c + at.core) * own
        out[c * own : (c + 1) * own, :] = nn(pick_rows(wrow[0:1, :], start, own), res[...]).astype(BF)

    for c in range(HALVES):
        res_mate.finish(c)
    for c in range(CHUNKS):
        unpack(c, going.at[0])
        pieces["ijkl"[c]].step()
    go()
    for c in range(HALVES):
        dattn_mate.finish(c)
    for gi in range(2):

        def back_out(i, carry, gi=gi):
            here = rows_at(i * TILE, TILE, TILE)
            there = rows_at(gi * seq + i * TILE, TILE, TILE)
            low = nt(dattn[here, :], weight(gi, 0, 3 * span, 4 * span)).astype(BF)
            dout[there, 0:span] = low
            turned = dout[there, :].astype(F32).T
            both = turned[0:span, :] * att_t[gi * span : (gi + 1) * span, here].astype(F32)
            for h in range(plan.heads):
                line = gi * 4 + h
                delta[line : line + 1, here] = jnp.sum(both[h * HD : (h + 1) * HD, :], axis=0, keepdims=True)
            return carry

        lax.fori_loop(0, seq // TILE, back_out, 0)
        grads2[gi * width + 3 * span : gi * width + 4 * span, :] = nn(
            att_t[gi * span : (gi + 1) * span, :], dattn[...]
        ).astype(BF)

    def attend_back(gi, i):
        k0, base = i * TILE, gi * seq
        k_rows = slice(base + k0, base + k0 + TILE)
        parts = []
        for h in range(plan.heads):
            lanes = (h // 2) * LANES
            q_lanes = slice(lanes, lanes + LANES)
            kh = head_lanes(qkv[k_rows, pad + lanes : pad + lanes + LANES], h % 2 == 1)
            vh = head_lanes(qkv[k_rows, 2 * pad + lanes : 2 * pad + lanes + LANES], h % 2 == 1)
            if h % 2 == 0:
                turned = qkv[k_rows, pad + lanes : pad + lanes + LANES].astype(F32).T.astype(BF)
            kt = turned[(h % 2) * HD : (h % 2 + 1) * HD, :]
            line = gi * 4 + h
            dk = dv = None
            for q0, q1 in ((k0, k0 + TILE), (k0 + TILE, seq)):
                if q0 == q1:
                    continue
                q_all = qkv[base + q0 : base + q1, q_lanes]
                do_all = dout[base + q0 : base + q1, q_lanes]
                prob = jnp.exp2(nt(kh, q_all) * LOG2E - lse[line : line + 1, q0:q1])
                if q0 == k0:
                    prob = jnp.where(seen, prob, 0.0)
                low = (prob * (nt(vh, do_all) - delta[line : line + 1, q0:q1])).astype(BF)
                more_v, more_k = nn(prob.astype(BF), do_all), nn(low, q_all)
                dv = more_v if dv is None else dv + more_v
                dk = more_k if dk is None else dk + more_k
                dq_acc[gi * span + h * HD : gi * span + (h + 1) * HD, q0:q1] += nn(kt, low)
            parts.append((dk, dv))
        for h in range(0, plan.heads, 2):
            lanes = (h // 2) * LANES
            for j in range(2):
                value = head_lanes(parts[h][j], False)
                if h + 1 < plan.heads:
                    value = value + head_lanes(parts[h + 1][j], True)
                start = (1 + j) * pad + lanes
                dqkv[k_rows, start : start + LANES] = value.astype(BF)

    def qkv_weight_grad(gi):
        def turn_dq(i, carry):
            here = rows_at(i * TILE, TILE, TILE)
            there = rows_at(gi * seq + i * TILE, TILE, TILE)
            turned = jnp.concatenate(
                [dq_acc[gi * span : (gi + 1) * span, here], jnp.zeros((pad - span, TILE), F32)], axis=0
            )
            dqkv[there, 0:pad] = (turned.T * HD**-0.5).astype(BF)
            return carry

        lax.fori_loop(0, seq // TILE, turn_dq, 0)
        return lambda: weigh(gi)

    def weigh(gi):
        for j in range(3):
            row0 = gi * width + j * span
            grads2[row0 : row0 + span, :] = tn(
                dqkv[gi * seq : (gi + 1) * seq, j * pad : j * pad + span], n1[...]
            ).astype(BF)

    for i in range(blocks):
        go()
        attend_back(1, i)
    go()
    qkv_weight_grad(1)()
    begin(TOTALS, "A", True)
    for i in range(blocks):
        go()
        attend_back(0, i)
    go()
    weigh_mine = qkv_weight_grad(0)
    for c in range(HALVES):

        def back_project(i, carry, c=c):
            here = rows_at(c * plan.half + i * TILE, TILE, TILE)
            total = None
            for gi in range(2):
                there = rows_at(gi * seq + c * plan.half + i * TILE, TILE, TILE)
                add_line((G_QKVB, G_QKVB2)[gi], dqkv[there, :].astype(F32))
                for j in range(3):
                    more = nn(dqkv[there, j * pad : j * pad + span], weight(gi, 0, j * span, (j + 1) * span))
                    total = more if total is None else total + more
            term[here, :] = total.astype(BF)
            return carry

        lax.fori_loop(0, plan.half // TILE, back_project, 0)
        norm_sum.start(c)
    go()
    for c in range(HALVES):
        mine = slice(c * part_rows, (c + 1) * part_rows)
        grad1 = norm_sum.finish(c)
        normal, inv = normal_rows(own_x[mine, :].astype(F32))
        dx = mid[mine, :] + norm_back(grad1, normal, inv, row(V_LN1G))
        if c == 0:
            res_mate.drain()
        res[rows_at(at.mine(c), part_rows), :] = dx.astype(BF)
        dx_mate.start(c)
        add_line(G_LN1G, grad1 * normal)
        add_line(G_LN1B, grad1)
    bias_copy.wait_send()
    pieces["v"].step()
    go()
    for c in range(HALVES):
        dx_mate.finish(c)
    for c in range(CHUNKS):
        unpack(c, going.at[1])
        pieces["rstu"[c]].step()
    go()
    weigh_mine()
    begin(TOTALS, "A", False)
    for _ in range(TAIL):
        go()
    need(pieces)
    out_way.drain()
    grad_way.drain()

    def told_all(j, carry):
        k = lax.rem(at.d + j, n)
        left(tab_out.at[rows_at(k * 8, 8, 8)], (tab_s, tab_r), j, {"dp": k})
        return carry

    lax.fori_loop(1, n, told_all, 0)
    tab_copy.wait_send()
    landed(tab.at[1 - at.side], (tab_s, tab_r), n, {"mp": at.across})
    for each in (n1_mate, cot_mate, n2_mate, dattn_mate, dx_mate, norm_sum):
        each.drain()


def finish_kernel(rows_a, rows_b, tab, proj, fc, attn, out_a, out_b, proj_f, fc_f, qkv_f, out_f):
    proj_f[...] = proj[...].astype(F32)
    fc_f[...] = fc[...].astype(F32)
    step = pl.program_id(0)
    turned = 3 * STEPS // 4

    @pl.when(step < turned)
    def _():
        qkv_f[...] = attn[...].astype(F32)

    @pl.when(step >= turned)
    def _():
        out_f[...] = attn[...].astype(F32)

    n = tab.shape[1] // 8
    slots = rows_a.shape[0] // n

    def one(k, carry):
        here = rows_at(k * slots, slots)
        lines = [tab[side, rows_at(k * 8, 8, 8), :][0:1, 0 : slots // 2] for side in range(2)]
        slot = jnp.concatenate(lines, axis=1).astype(jnp.int32) - 1
        place = lax.broadcasted_iota(jnp.int32, (slots, slots), 0)
        hot = jnp.where(place == slot, 1.0, 0.0).astype(BF)
        out_a[here, :] = nn(hot, rows_a[here, :]).astype(BF)
        out_b[here, :] = nn(hot, rows_b[here, :]).astype(BF)
        return carry

    lax.fori_loop(0, n, one, 0)


def body(
    tokens,
    cotangent,
    seq_lengths,
    source_slot,
    ln1_gain,
    ln1_bias,
    qkv_weight,
    qv_bias,
    output_projection_weight,
    out_bias,
    ln2_gain,
    ln2_bias,
    fc_weight,
    fc_bias,
    proj_weight,
    proj_bias,
):
    rows, width = tokens.shape
    span = qkv_weight.shape[2]
    n, members = lax.axis_size("dp"), lax.axis_size("mp")
    plan = Plan(n, members, rows, width, span // HD)
    pad, seq = plan.pad, plan.seq

    vectors = (ln1_gain, ln1_bias, out_bias, ln2_gain, ln2_bias, proj_bias, fc_bias)
    line = jnp.arange(8, dtype=jnp.int32)[:, None]
    vec = jnp.zeros((8, width), BF)
    for i, v in enumerate(vectors):
        vec = jnp.where(line == i, v[None, :], vec)
    vm = pl.BlockSpec(memory_space=pltpu.VMEM)
    hbm = pl.BlockSpec(memory_space=pl.ANY)
    shape = jax.ShapeDtypeStruct
    quarter = rows // members
    dma = pltpu.SemaphoreType.DMA
    rooms = [total_room(entry[3] - entry[2], n, entry[5]) for entry in TOTALS]
    landing, sems = (sum(room[i] for room in rooms) for i in range(2))
    hops = 2 + (n - 1).bit_length()

    def vmem(*dims, dtype=BF):
        return pltpu.VMEM(dims, dtype)

    block_rows, grad_rows, proj_total, fc_total, attn_total, vec_total, tab = pl.pallas_call(
        functools.partial(block_kernel, plan),
        out_shape=(
            shape((rows, width), BF),
            shape((rows, width), BF),
            shape((width, width), BF),
            shape((width, width), BF),
            shape((width, width), BF),
            shape((8, width), F32),
            shape((2, 8 * n, LANES), F32),
        ),
        in_specs=[hbm, hbm, vm, pl.BlockSpec(memory_space=pltpu.SMEM), vm, vm, hbm, hbm, vm, vm],
        out_specs=(hbm,) * 5 + (vm, vm),
        scratch_shapes=[
            vmem(8, width, dtype=F32),
            vmem(8 * n, LANES, dtype=F32),
            vmem(8, seq, dtype=jnp.int32),
            vmem(width, width),
            vmem(8, width, dtype=F32),
            vmem(3 * width, width),
            vmem(rows, width),
            vmem(rows, width),
            vmem(quarter, width),
            vmem(seq, width),
            vmem(seq, width),
            vmem(seq, width),
            vmem(seq, width),
            vmem(2 * seq, 3 * pad),
            vmem(2 * span, seq),
            vmem(2 * span, seq),
            vmem(8, seq, dtype=F32),
            vmem(8, seq, dtype=F32),
            vmem(seq, width),
            vmem(seq // 2, width),
            vmem(seq // 2, width),
            vmem(seq // 2, width),
            vmem(seq // 2, width, dtype=F32),
            vmem(2 * seq, pad),
            vmem(2 * span, seq, dtype=F32),
            vmem(4 * width, width),
            vmem(landing, width),
            vmem(seq, width),
            vmem(2, quarter, width),
            vmem(hops, GLINES, width, dtype=F32),
            vmem(hops, GLINES, width, dtype=F32),
            dma((plan.split, n)),
            dma((CHUNKS, plan.in_chunk)),
            dma((plan.split, n)),
            dma((CHUNKS, plan.in_chunk)),
            dma((2, CHUNKS)),
            dma((2, CHUNKS)),
            dma((6, HALVES)),
            dma((6, HALVES)),
            dma((4, HALVES)),
            dma((4, HALVES)),
            dma((len(MOVES), 4)),
            dma((len(MOVES), 4)),
            dma((n + 1,)),
            dma((n + 1,)),
            dma((2, CHUNKS, plan.in_chunk)),
            dma((2, plan.split, n)),
            dma((2, plan.split)),
            dma((2, 3, plan.split, n)),
            dma((2, 3, plan.split, n)),
            dma((sems,)),
            dma((sems,)),
            dma((hops + 1,)),
            dma((hops + 1,)),
            dma((4,)),
        ],
        compiler_params=pltpu.CompilerParams(
            collective_id=0, has_side_effects=True, vmem_limit_bytes=VMEM_LIMIT
        ),
        name="block",
    )(
        tokens,
        cotangent,
        source_slot.reshape(1, rows),
        seq_lengths,
        vec,
        qv_bias,
        qkv_weight.transpose(1, 2, 0).reshape(3 * span, width),
        output_projection_weight,
        fc_weight,
        proj_weight,
    )
    def tall(count):
        return pl.BlockSpec((count // STEPS, width), lambda i: (i, 0))

    block_out, input_grad, proj_grad, fc_grad, qkv_grad, out_grad = pl.pallas_call(
        finish_kernel,
        out_shape=(
            shape((rows, width), BF),
            shape((rows, width), BF),
            shape((width, width), F32),
            shape((width, width), F32),
            shape((3 * span, width), F32),
            shape((span, width), F32),
        ),
        grid=(STEPS,),
        in_specs=[
            tall(rows),
            tall(rows),
            pl.BlockSpec((2, 8 * n // STEPS, LANES), lambda i: (0, i, 0)),
            tall(width),
            tall(width),
            tall(width),
        ],
        out_specs=(
            tall(rows),
            tall(rows),
            tall(width),
            tall(width),
            pl.BlockSpec((width // STEPS, width), lambda i: (jnp.minimum(i, 3 * STEPS // 4 - 1), 0)),
            pl.BlockSpec((width // STEPS, width), lambda i: (jnp.maximum(i - 3 * STEPS // 4, 0), 0)),
        ),
        compiler_params=pltpu.CompilerParams(vmem_limit_bytes=VMEM_LIMIT),
        name="finish",
    )(block_rows, grad_rows, tab, proj_total, fc_total, attn_total)
    qkv_sums = vec_total[G_QKVB].reshape(3, pad)[:, :span]
    return (
        block_out,
        input_grad,
        vec_total[G_LN1G],
        vec_total[G_LN1B],
        qkv_grad.reshape(3, span, width).transpose(2, 0, 1),
        jnp.stack([qkv_sums[0], qkv_sums[2]]),
        out_grad,
        vec_total[G_OUTB],
        vec_total[G_LN2G],
        vec_total[G_LN2B],
        fc_grad,
        vec_total[G_FCB],
        proj_grad,
        vec_total[G_PROJB],
    )


def solution(mesh):
    return jax.shard_map(
        body,
        mesh=mesh,
        in_specs=(
            P("dp", None),
            P("dp", None),
            P("dp", None),
            P("dp"),
            P(),
            P(),
            P(None, None, "mp"),
            P(None, "mp"),
            P("mp", None),
            P(),
            P(),
            P(),
            P(None, "mp"),
            P("mp"),
            P("mp", None),
            P(),
        ),
        out_specs=(
            P("dp", None),
            P("dp", None),
            P(),
            P(),
            P(None, None, "mp"),
            P(None, "mp"),
            P("mp", None),
            P(),
            P(),
            P(),
            P(None, "mp"),
            P("mp"),
            P("mp", None),
            P(),
        ),
        check_vma=False,
    )
```

```python
import functools

import jax
import jax.numpy as jnp
from jax import lax
from jax.experimental import pallas as pl
from jax.experimental.pallas import tpu as pltpu
from jax.sharding import PartitionSpec as P

MESH = pl.DeviceIdType.MESH
BF = jnp.bfloat16
F32 = jnp.float32
HD = 64
EPSILON = 1e-05
NEG = -1e30
LOG2E = 1.4426950408889634
TILE = 256
HALVES = 2
STEPS = 2
CHUNKS = 4
LANES = 128
VMEM_LIMIT = 60 * 2**20


class Plan:
    def __init__(self, n, members, rows, width, heads):
        self.n, self.members, self.rows, self.width, self.heads = n, members, rows, width, heads
        self.slots = rows // n
        self.seq = rows // 2
        self.per = self.seq // n
        self.group = max(1, 32 // self.per)
        self.share = self.group * self.per // 2
        self.groups = n // self.group
        self.own = self.seq // (2 * CHUNKS)
        self.take = max(16, self.share // CHUNKS)
        self.split = self.share // self.take
        self.in_chunk = self.own // self.take
        self.half = self.seq // HALVES
        self.part = self.half // 2
        self.pad = -(-heads * HD // LANES) * LANES

    def come_index(self, source, turn):
        grp = over(source, self.group)
        inside = under(source, self.group) * self.per + turn
        core, row = over(inside, self.share), under(inside, self.share)
        chunk = over(grp, self.in_chunk) * self.split + over(row, self.take)
        return (
            (2 * chunk + core) * self.own
            + under(grp, self.in_chunk) * self.take
            + under(row, self.take)
        )

    def source_of(self, core):
        return (core * self.share) // self.per, lax.rem(core * self.share, self.per)


def over(x, size):
    return lax.shift_right_logical(x, jnp.full_like(x, size.bit_length() - 1))


def under(x, size):
    return x & (size - 1)


def nn(a, b):
    return lax.dot_general(a, b, (((1,), (0,)), ((), ())), preferred_element_type=F32)


def nt(a, b):
    return lax.dot_general(a, b, (((1,), (1,)), ((), ())), preferred_element_type=F32)


def tn(a, b):
    return lax.dot_general(a, b, (((0,), (0,)), ((), ())), preferred_element_type=F32)


def rows_at(start, count, step=16):
    if not isinstance(start, int):
        start = pl.multiple_of(start, step)
    return pl.ds(start, count)


class Place:
    def __init__(self, plan):
        self.plan = plan
        self.d = lax.axis_index("dp")
        self.m = lax.axis_index("mp")
        self.core = lax.rem(self.m, 2)
        self.side = self.m // 2
        self.mate = self.m + 1 - 2 * self.core
        self.across = lax.rem(self.m + 2, plan.members)
        self.source, self.offset = plan.source_of(self.core)

    def mine(self, c, flip=False):
        core = 1 - self.core if flip else self.core
        return (2 * c + core) * self.plan.part


def send(src, dst, sems, index, device):
    copy = pltpu.make_async_remote_copy(
        src_ref=src,
        dst_ref=dst,
        send_sem=sems[0].at[index],
        recv_sem=sems[1].at[index],
        device_id=device,
        device_id_type=MESH,
    )
    copy.start()
    return copy


def landed(dst, sems, index, device):
    pltpu.make_async_remote_copy(
        src_ref=dst,
        dst_ref=dst,
        send_sem=sems[0].at[index],
        recv_sem=sems[1].at[index],
        device_id=device,
        device_id_type=MESH,
    ).wait_recv()


def left(src, sems, index, device):
    pltpu.make_async_remote_copy(
        src_ref=src,
        dst_ref=src,
        send_sem=sems[0].at[index],
        recv_sem=sems[1].at[index],
        device_id=device,
        device_id_type=MESH,
    ).wait_send()


def greet(plan, at):
    barrier = pltpu.get_barrier_semaphore()

    def signal(j, carry):
        pl.semaphore_signal(
            barrier, inc=1, device_id={"dp": lax.rem(at.d + j, plan.n)}, device_id_type=MESH
        )
        return carry

    lax.fori_loop(1, plan.n, signal, 0)
    pl.semaphore_signal(barrier, inc=1, device_id={"mp": at.mate}, device_id_type=MESH)
    pl.semaphore_signal(barrier, inc=1, device_id={"mp": at.across}, device_id_type=MESH)


def all_here(plan):
    pl.semaphore_wait(pltpu.get_barrier_semaphore(), plan.n + 1)


class MateGather:
    def __init__(self, at, buf, sems, count):
        self.at, self.buf, self.sems, self.count, self.copies = at, buf, sems, count, []

    def rows(self, c, core):
        return self.buf.at[rows_at((2 * c + core) * self.count, self.count)]

    def start(self, c):
        here = self.rows(c, self.at.core)
        self.copies.append(send(here, here, self.sems, c, {"mp": self.at.mate}))

    def finish(self, c):
        landed(self.rows(c, 1 - self.at.core), self.sems, c, {"mp": self.at.mate})

    def drain(self):
        for copy in self.copies:
            copy.wait_send()
        self.copies = []


class MateSum:
    def __init__(self, at, term, land, sems):
        self.at, self.term, self.land, self.sems, self.copies = at, term, land, sems, []

    def start(self, c):
        plan, at = self.at.plan, self.at
        src = self.term.at[rows_at(at.mine(c, True), plan.part)]
        dst = self.land.at[rows_at(c * plan.part, plan.part)]
        self.copies.append(send(src, dst, self.sems, c, {"mp": at.mate}))

    def finish(self, c):
        plan, at = self.at.plan, self.at
        where = rows_at(c * plan.part, plan.part)
        landed(self.land.at[where], self.sems, c, {"mp": at.mate})
        mine = self.term[rows_at(at.mine(c), plan.part), :]
        return mine.astype(F32) + self.land[where, :].astype(F32)

    def drain(self):
        for copy in self.copies:
            copy.wait_send()
        self.copies = []


class Incoming:
    def __init__(self, at, source, sems, landing):
        plan = at.plan
        self.at, self.source, self.sems, self.landing = at, source, sems, landing
        self.sends = None
        if plan.group > 1:
            self.sends = lax.rem(at.d, plan.group) == at.source

    def guarded(self, run):
        if self.sends is None:
            run()
        else:
            pl.when(self.sends)(run)

    def mine(self, part):
        plan, at = self.at.plan, self.at
        grp = at.d // plan.group
        return (grp // plan.in_chunk) * plan.split + part, lax.rem(grp, plan.in_chunk)

    def piece(self, k, part):
        plan = self.at.plan
        start = k * plan.per + self.at.offset + part * plan.take
        return self.source.at[rows_at(start, plan.take)]

    def start(self, part):
        plan, at = self.at.plan, self.at
        c, gi = self.mine(part)

        def one(j, carry):
            k = lax.rem(at.d + j, plan.n)
            pltpu.make_async_remote_copy(
                src_ref=self.piece(k, part),
                dst_ref=self.landing(c, gi),
                send_sem=self.sems[0].at[part, j],
                recv_sem=self.sems[1].at[c, gi],
                device_id={"dp": k},
                device_id_type=MESH,
            ).start()
            return carry

        def run():
            lax.fori_loop(1, plan.n, one, 0)
            pltpu.make_async_copy(
                self.piece(at.d, part), self.landing(c, gi), self.sems[1].at[c, gi]
            ).start()

        self.guarded(run)

    def wait(self, c):
        plan, at = self.at.plan, self.at

        def one(gi, carry):
            landed(self.landing(c, gi), (self.sems[1], self.sems[1]), (c, gi), {"dp": at.d})
            return carry

        lax.fori_loop(0, plan.in_chunk, one, 0)

    def drain(self):
        plan, at = self.at.plan, self.at

        def run():
            for part in range(plan.split):

                def one(j, carry, part=part):
                    k = lax.rem(at.d + j, plan.n)
                    left(self.piece(k, part), (self.sems[0], self.sems[0]), (part, j), {"dp": k})
                    return carry

                lax.fori_loop(1, plan.n, one, 0)

        self.guarded(run)


class Outgoing:
    def __init__(self, at, rows_ref, out, sems, local_sem, share_sems):
        plan = at.plan
        self.at, self.rows_ref, self.out = at, rows_ref, out
        self.sems, self.local_sem, self.share_sems = sems, local_sem, share_sems

    def holds(self, member):
        plan = self.at.plan
        if plan.group == 1:
            return None
        return lax.rem(self.at.d, plan.group) == plan.source_of(lax.rem(member, 2))[0]

    def guarded(self, member, run):
        if self.at.plan.group == 1:
            run()
        else:
            pl.when(self.holds(member))(run)

    def place(self, k, part, member):
        plan = self.at.plan
        first = (member // 2) * plan.per + plan.source_of(lax.rem(member, 2))[1]
        start = k * plan.slots + first + part * plan.take
        return self.out.at[rows_at(start, plan.take)]

    def each(self, c, remote, local):
        plan, at = self.at.plan, self.at
        part = c % plan.split

        def one(gi, carry):
            grp = (c // plan.split) * plan.in_chunk + gi
            dest = grp * plan.group + at.source
            src = self.rows_ref.at[rows_at(c * plan.own + gi * plan.take, plan.take)]
            dst = self.place(at.d, part, at.m)
            pl.when(dest != at.d)(lambda: remote(gi, part, src, dst, dest))
            pl.when(dest == at.d)(lambda: local(gi, part, src, dst))
            return carry

        lax.fori_loop(0, plan.in_chunk, one, 0)

    def copy(self, c, gi, part, src, dst, dest):
        return pltpu.make_async_remote_copy(
            src_ref=src,
            dst_ref=dst,
            send_sem=self.sems[0].at[c, gi],
            recv_sem=self.sems[1].at[part, self.at.d],
            device_id={"dp": dest},
            device_id_type=MESH,
        )

    def start(self, c):
        def local(gi, part, src, dst):
            pltpu.make_async_copy(src, dst, self.local_sem.at[part]).start()

        self.each(c, lambda gi, part, src, dst, dest: self.copy(c, gi, part, src, dst, dest).start(), local)

    def drain(self):
        for c in range(CHUNKS):
            self.each(
                c,
                lambda gi, part, src, dst, dest: self.copy(c, gi, part, src, dst, dest).wait_send(),
                lambda gi, part, src, dst: None,
            )

    def loop(self, part, run):
        lax.fori_loop(0, self.at.plan.n, lambda k, carry: (run(k), carry)[1], 0)

    def share(self, part):
        at = self.at

        def run():
            def one(k):
                here = self.place(k, part, at.m)

                def remote():
                    landed(here, (self.sems[1], self.sems[1]), (part, k), {"dp": at.d})

                def local():
                    pltpu.make_async_copy(here, here, self.local_sem.at[part]).wait()

                pl.when(k != at.d)(remote)
                pl.when(k == at.d)(local)
                send(here, here, self.share_sems, (1, part, k), {"mp": at.across})
                send(here, here, self.share_sems, (0, part, k), {"mp": at.mate})

            self.loop(part, one)

        self.guarded(at.m, run)

    def forward(self, part):
        at = self.at

        def run():
            def one(k):
                there = self.place(k, part, at.across)
                landed(there, self.share_sems, (1, part, k), {"mp": at.across})
                send(there, there, self.share_sems, (2, part, k), {"mp": at.mate})

            self.loop(part, one)

        self.guarded(at.across, run)

    def finish(self, part):
        at = self.at
        corner = (1 - at.side) * 2 + 1 - at.core

        def near():
            self.loop(
                part,
                lambda k: landed(
                    self.place(k, part, at.mate), self.share_sems, (0, part, k), {"mp": at.mate}
                ),
            )

        def far():
            self.loop(
                part,
                lambda k: landed(
                    self.place(k, part, corner), self.share_sems, (2, part, k), {"mp": at.mate}
                ),
            )

        def sent():
            def one(k):
                here = self.place(k, part, at.m)
                left(here, self.share_sems, (1, part, k), {"mp": at.across})
                left(here, self.share_sems, (0, part, k), {"mp": at.mate})

            self.loop(part, one)

        def passed():
            self.loop(
                part,
                lambda k: left(
                    self.place(k, part, at.across), self.share_sems, (2, part, k), {"mp": at.mate}
                ),
            )

        self.guarded(at.mate, near)
        self.guarded(corner, far)
        self.guarded(at.m, sent)
        self.guarded(at.across, passed)


def halvings(rows, n, order):
    steps, size = [], rows
    bits = [1 << i for i in range((n - 1).bit_length())]
    for i in order:
        bits.insert(0, bits.pop(i))
    for bit in bits:
        if size % 32 == 0:
            size //= 2
            steps.append((bit, True, size))
        else:
            steps.append((bit, False, size))
    return steps


def trail_of(at, rows, order):
    offset, trail, size = 0, [], rows
    for bit, halve, size in halvings(rows, at.plan.n, order):
        if halve:
            high = lax.rem(at.d // bit, 2)
            partner = {"dp": at.d + (1 - 2 * high) * bit}
            trail.append((offset, offset + high * size, size, partner))
            offset = offset + high * size
    return offset, size, trail


class Steps:
    def __init__(self, *runs):
        self.runs, self.next = list(runs), 0

    def step(self):
        if self.next < len(self.runs):
            self.next += 1
            self.runs[self.next - 1]()

    def finish(self):
        while self.next < len(self.runs):
            self.step()


class Stepped:
    def __init__(self):
        self.jobs, self.next, self.pending = [], 0, None

    def step(self):
        if self.pending is not None:
            self.pending[0](self.pending[1])
            self.pending = None
        if self.next < len(self.jobs):
            start, end = self.jobs[self.next]
            self.next += 1
            self.pending = (end, start())

    def finish(self):
        while self.pending is not None or self.next < len(self.jobs):
            self.step()

    def spread(self, buf, keep, other, size, sems, index, partner, source=None, before_end=None):
        def start():
            here = buf.at[rows_at(keep, size)]
            return send(here if source is None else source, here, sems, index, partner)

        def end(copy):
            copy.wait_send()
            landed(buf.at[rows_at(other, size)], sems, index, partner)
            if before_end is not None:
                before_end()

        self.jobs.append((start, end))


class Weights(Stepped):
    def __init__(self, at, source, dst, sems, index, bits):
        super().__init__()
        offset, trail, size = 0, [], source.shape[0]
        for bit in bits:
            if bit < at.plan.n:
                size //= 2
                high = lax.rem(at.d // bit, 2)
                partner = {"dp": at.d + (1 - 2 * high) * bit}
                trail.append((offset, offset + high * size, size, partner))
                offset = offset + high * size
        slice_rows = rows_at(offset, size)
        across = {"mp": at.across}

        def start():
            return send(source.at[slice_rows], dst.at[slice_rows], sems, index, across)

        def end(copy):
            copy.wait_send()
            landed(dst.at[slice_rows], sems, index, across)

        self.jobs.append((start, end))
        for i, (before, keep, length, partner) in enumerate(reversed(trail)):
            self.spread(dst, keep, 2 * before + length - keep, length, sems, index + 1 + i, partner)


class Total(Stepped):
    def __init__(self, at, first, origins, out, landing, base, sems, index, order, early):
        super().__init__()
        self.at, self.landing = at, landing
        rows, n = out.shape[0], at.plan.n
        steps = halvings(rows, n, order)
        room = sum(size for _, _, size in steps)
        sources = [(first, origin) for origin in origins]
        if early:
            self.cross(sources, base, rows, (sems, index))
            sources, index, base = [(landing, base)], index + 1, base + rows
        lands = [base + i * room for i in range(len(sources))]
        for bit, halve, size in steps:
            high = lax.rem(at.d // bit, 2)
            partner = {"dp": at.d + (1 - 2 * high) * bit}
            keep = high * size if halve else 0
            give = (1 - high) * size if halve else 0
            self.exchange(sources, give, keep, size, list(lands), (sems, index), partner)
            index += len(sources)
            sources = [(landing, land) for land in lands]
            lands = [land + size for land in lands]
        offset, size, trail = trail_of(at, rows, order)
        if not early:
            self.cross(sources, base + 2 * room, size, (sems, index))
            sources, index = [(landing, base + 2 * room)], index + 1
        done = landing.at[rows_at(sources[0][1], size)]
        local = pltpu.make_async_copy(done, out.at[rows_at(offset, size)], sems[0].at[index])
        self.jobs[-1] = (self.jobs[-1][0], self.then(self.jobs[-1][1], local.start))
        index += 1
        for i, (before, keep, length, partner) in enumerate(reversed(trail)):
            source, settle = (done, local.wait) if i == 0 else (None, None)
            self.spread(
                out, keep, 2 * before + length - keep, length, sems, index + i, partner, source, settle
            )

    def then(self, end, more):
        def both(copy):
            end(copy)
            more()

        return both

    def add(self, first, origin, land, size):
        step = 96 if size % 96 == 0 else (32 if size % 32 == 0 else 16)

        def one(i, carry):
            here = rows_at(origin + i * step, step)
            there = rows_at(land + i * step, step)
            value = first[here, :].astype(F32) + self.landing[there, :].astype(F32)
            self.landing[there, :] = value.astype(BF)
            return carry

        lax.fori_loop(0, size // step, one, 0)

    def exchange(self, sources, give, keep, size, lands, sems, partner):
        sems, index = sems

        def start():
            return [
                send(
                    ref.at[rows_at(origin + give, size)],
                    self.landing.at[rows_at(land, size)],
                    sems,
                    index + i,
                    partner,
                )
                for i, ((ref, origin), land) in enumerate(zip(sources, lands))
            ]

        def end(copies):
            for copy, (ref, origin), land in zip(copies, sources, lands):
                copy.wait()
                self.add(ref, origin + keep, land, size)

        self.jobs.append((start, end))

    def cross(self, sources, land, size, sems):
        sems, index = sems
        (mine, mine_at), (theirs, theirs_at) = sources

        def start():
            return send(
                theirs.at[rows_at(theirs_at, size)],
                self.landing.at[rows_at(land, size)],
                sems,
                index,
                {"mp": self.at.across},
            )

        def end(copy):
            copy.wait()
            self.add(mine, mine_at, land, size)

        self.jobs.append((start, end))


def total_room(rows, n, early):
    steps = halvings(rows, n, ())
    size, spreads = steps[-1][2], sum(1 for _, halve, _ in steps if halve)
    room, groups = sum(step[2] for step in steps), 1 if early else 2
    return groups * room + (rows if early else size), groups * len(steps) + 2 + spreads


def normal_rows(x):
    centered = x - jnp.mean(x, axis=-1, keepdims=True)
    inv = lax.rsqrt(jnp.mean(centered * centered, axis=-1, keepdims=True) + EPSILON)
    return centered * inv, inv


def norm_back(grad, normal, inv, gain):
    scaled = grad * gain
    return inv * (
        scaled
        - jnp.mean(scaled, axis=-1, keepdims=True)
        - normal * jnp.mean(scaled * normal, axis=-1, keepdims=True)
    )


def pick(index_col, count):
    lanes = lax.broadcasted_iota(jnp.int32, (index_col.shape[0], count), 1)
    return jnp.where(lanes == index_col, 1.0, 0.0).astype(BF)


def pick_rows(index_row, first, count):
    lines = lax.broadcasted_iota(jnp.int32, (count, index_row.shape[1]), 0) + first
    return jnp.where(lines == index_row, 1.0, 0.0).astype(BF)


def head_lanes(x, odd):
    lane = lax.broadcasted_iota(jnp.int32, x.shape, 1)
    return jnp.where((lane >= HD) == odd, x, jnp.zeros_like(x))


V_LN1G, V_LN1B, V_OUTB, V_LN2G, V_LN2B, V_PROJB, V_FCB, V_QKVB = range(8)
G_LN1G, G_LN1B, G_LN2G, G_LN2B, G_OUTB, G_PROJB, G_FCB, G_QKVB, G_FCB2, G_QKVB2 = range(10)
SHARED = 6
MOVES = (
    ("a", 0, 0, 256, (2,)),
    ("b", 0, 256, 512, (1,)),
    ("c", 0, 512, 768, (1,)),
    ("f", 1, 0, 384, (2, 1)),
    ("g", 1, 384, 768, (1,)),
    ("p", 2, 0, 768, ()),
)
TOTALS = (
    ("F", "F", 0, 256, (), True),
    ("G", "F", 256, 512, (), True),
    ("H", "F", 512, 768, (), True),
    ("A", "A", 0, 256, (1,), True),
    ("B", "A", 256, 512, (), True),
    ("C", "A", 512, 768, (), True),
    ("P", "P", 0, 256, (), False),
    ("Q", "P", 256, 512, (), True),
    ("X", "P", 512, 768, (1,), False),
)
SCHEDULE = (
    "",
    "fgpa",
    "b045670c1f12b23ag3",
    "4c",
    "",
    "54",
    "",
    "f",
    "65",
    "",
    "6",
    "7",
    "",
    "7g",
    "",
    "pf",
    "",
    "",
    "",
    "",
    "",
    "",
    "",
    "",
    "QPX",
    "",
    "",
    "F",
    "",
    "Q",
    "",
    "G",
    "PX",
    "jkil",
    "FQ",
    "HP",
    "G",
    "FXQHAGrsBHtuCBFQjACGjAHBkFkQiCiGlvQFAPXlHBGFrCrH",
    "AsGPsXtHBPtCAuvBXvuCvPvABXC",
)
TAIL = 2
GLINES = 16
GELU = 0.7978845608028654
CUBE = 0.044715


class VecTotal(Stepped):
    def __init__(self, hops, given, taken, out, sems):
        super().__init__()
        line = lax.broadcasted_iota(jnp.int32, (8, out.shape[1]), 0)
        for i, device in enumerate(hops):

            def start(i=i, device=device):
                return send(given.at[i], taken.at[i], sems, i + 1, device)

            def end(copy, i=i):
                copy.wait()
                low, high = taken[i, 0:8, :], taken[i, 8:16, :]
                if i == 0:
                    low, high = jnp.where(line < SHARED, low, 0.0), jnp.zeros_like(high)
                elif i == 1:
                    low = jnp.concatenate([low[0:SHARED, :], high[0:2, :]], axis=0)
                    high = jnp.zeros_like(high)
                if i + 1 < len(hops):
                    given[i + 1, 0:8, :] = given[i, 0:8, :] + low
                    given[i + 1, 8:16, :] = given[i, 8:16, :] + high
                else:
                    out[...] = given[i, 0:8, :] + low

            self.jobs.append((start, end))


def list_slots(plan, at, slot_row, lengths, wrow, tab_out):
    n, rows, seq, slots = plan.n, plan.rows, plan.seq, plan.slots
    line = jnp.broadcast_to(slot_row[...], (8, rows))
    begins = jnp.where(at.side == 0, 0, lengths[0, 0])
    count = jnp.where(at.side == 0, lengths[0, 0], lengths[0, 1])
    back = rows - begins
    bit = 1
    while bit < rows:
        turn_it = jnp.broadcast_to(back & bit, line.shape) != 0
        line = jnp.where(turn_it, pltpu.roll(line, bit, 1), line)
        bit *= 2
    slot = line[0:1, 0:seq]
    token = lax.broadcasted_iota(jnp.int32, (1, seq), 1)
    named = (token < count) & (slot < rows)
    slot = jnp.where(named, slot, 0)
    source = jnp.where(named, over(slot, slots), -1)
    wrow[0:1, :] = jnp.where(named, plan.come_index(over(slot, slots), over(token, n)), -1)
    lines = over(lax.broadcasted_iota(jnp.int32, (8 * n, seq), 0), 8)
    told = jnp.where(lines == source, (under(slot, slots) + 1).astype(F32), 0.0).astype(BF)
    turn = over(lax.broadcasted_iota(jnp.int32, (seq, LANES), 0), n)
    turns = jnp.where(turn == lax.broadcasted_iota(jnp.int32, (seq, LANES), 1), 1.0, 0.0).astype(BF)
    tab_out[...] = nn(told, turns)


def block_kernel(
    plan,
    tokens,
    cotangent,
    slot_row,
    lengths,
    vec_in,
    qv_in,
    wqkv_in,
    wo_in,
    wfc,
    wproj,
    block_out,
    input_grad,
    proj_total,
    fc_total,
    attn_total,
    vec_total,
    tab,
    vec,
    tab_out,
    wrow,
    wattn,
    vec2,
    weights2,
    act,
    dhid,
    own_x,
    n1,
    cot_p,
    n2,
    dattn,
    qkv,
    v_t,
    att_t,
    lse,
    delta,
    term,
    land_a,
    land_b,
    land_c,
    mid,
    dout,
    dq_acc,
    grads,
    landing,
    res,
    going,
    vec_s,
    vec_r,
    tok_s,
    tok_r,
    cot_s,
    cot_r,
    ag_s,
    ag_r,
    mate_s,
    mate_r,
    sum_s,
    sum_r,
    weight_s,
    weight_r,
    tab_s,
    tab_r,
    back_s,
    back_r,
    back_l,
    share_s,
    share_r,
    total_s,
    total_r,
    vec_ss,
    vec_sr,
    local,
):
    at = Place(plan)
    rows, width, pad, seq = plan.rows, plan.width, plan.pad, plan.seq
    own, part_rows, per, slots = plan.own, plan.part, plan.per, plan.slots
    n = plan.n
    span = plan.heads * HD
    fetch = [
        pltpu.make_async_copy(wqkv_in, wattn.at[0 : 3 * span], local.at[0]),
        pltpu.make_async_copy(wo_in, wattn.at[3 * span : 4 * span], local.at[1]),
        pltpu.make_async_copy(tokens, act, local.at[2]),
        pltpu.make_async_copy(cotangent, dhid, local.at[3]),
    ]
    for copy in fetch:
        copy.start()
    vec[...] = vec_in[...].astype(F32)
    vec[V_QKVB : V_QKVB + 1, 0:span] = qv_in[0:1, :].astype(F32)
    vec[V_QKVB : V_QKVB + 1, 2 * pad : 2 * pad + span] = qv_in[1:2, :].astype(F32)
    greet(plan, at)
    list_slots(plan, at, slot_row, lengths, wrow, tab_out)
    all_here(plan)
    dqkv, grads2 = act, dhid
    mlp_term = grads.at[2 * width : 2 * width + seq]
    tok_come, cot_come = grads.at[0:seq], grads.at[seq : 2 * seq]
    tok_stage, cot_stage = term, grads.at[2 * seq : 3 * seq]

    def come(buf):
        return lambda c, gi: buf.at[rows_at((2 * c + at.core) * own + gi * plan.take, plan.take)]

    tok = Incoming(at, tok_stage, (tok_s, tok_r), come(tok_come))
    cot = Incoming(at, cot_stage, (cot_s, cot_r), come(cot_come))
    tok_all = MateGather(at, tok_come, (ag_s.at[0], ag_r.at[0]), own)
    cot_all = MateGather(at, cot_come, (ag_s.at[1], ag_r.at[1]), own)
    n1_mate, cot_mate, n2_mate, dattn_mate, res_mate, dx_mate = (
        MateGather(at, buf, (mate_s.at[i], mate_r.at[i]), part_rows)
        for i, buf in enumerate((n1, cot_p, n2, dattn, res, res))
    )
    attn_sum, back_sum, mlp_sum, norm_sum = (
        MateSum(at, ref, land, (sum_s.at[i], sum_r.at[i]))
        for i, (ref, land) in enumerate(
            ((term, land_a), (term, land_b), (mlp_term, land_c), (term, land_a))
        )
    )
    weights = (wattn, wfc, wproj)
    pieces = {}
    for i, (name, which, start, stop, bits) in enumerate(MOVES):
        pieces[name] = Weights(
            at,
            weights[which].at[start:stop],
            weights2.at[which * width + start : which * width + stop],
            (weight_s.at[i], weight_r.at[i]),
            0,
            bits,
        )

    def weight(gi, i, start=0, stop=width):
        if gi:
            return weights2[i * width + start : i * width + stop, :]
        return weights[i][start:stop, :]

    vec_g = (vec, vec2)
    out_way, grad_way = (
        Outgoing(
            at,
            going.at[i],
            out,
            (back_s.at[i], back_r.at[i]),
            back_l.at[i],
            (share_s.at[i], share_r.at[i]),
        )
        for i, out in enumerate((block_out, input_grad))
    )
    outs = {"P": proj_total, "F": fc_total, "A": attn_total}
    room, index = 0, 0
    for name, kind, start, stop, order, early in TOTALS:
        first, at_row = {"P": (grads, 0), "F": (grads, 2 * width), "A": (grads2, 0)}[kind]
        pieces[name] = Total(
            at,
            first,
            [at_row + gi * width + start for gi in range(2)],
            outs[kind].at[start:stop],
            landing,
            room,
            (total_s, total_r),
            index,
            order,
            early,
        )
        more, sems = total_room(stop - start, n, early)
        room, index = room + more, index + sems

    def incoming(way, every, c):
        def first():
            if c < plan.split:
                way.start(c)

        def second():
            way.wait(c)
            every.start(c)

        return Steps(first, second, lambda: every.finish(c))

    def outgoing(way, c):
        part_of = c - (CHUNKS - plan.split)

        def when_part(run):
            return lambda: run(part_of) if part_of >= 0 else None

        return Steps(
            lambda: way.start(c),
            when_part(way.share),
            when_part(way.forward),
            when_part(way.finish),
        )

    for c in range(CHUNKS):
        pieces["0123"[c]] = incoming(tok, tok_all, c)
        pieces["4567"[c]] = incoming(cot, cot_all, c)
        pieces["ijkl"[c]] = outgoing(out_way, c)
        pieces["rstu"[c]] = outgoing(grad_way, c)

    hops = [{"mp": at.mate}, {"mp": at.across}]
    bit = 1
    while bit < n:
        high = lax.rem(at.d // bit, 2)
        hops.append({"dp": at.d + (1 - 2 * high) * bit})
        bit *= 2
    vec_total_sum = VecTotal(hops, vec_s, vec_r, vec_total, (vec_ss, vec_sr))
    pieces["v"] = vec_total_sum
    schedule = iter(SCHEDULE)

    def go():
        for name in next(schedule, ""):
            pieces[name].step()

    def need(names):
        for name in names:
            pieces[name].finish()

    def begin(table, kind, early=None):
        for entry in table:
            if entry[1] == kind and early in (None, entry[-1]):
                pieces[entry[0]].step()

    def names_of(table, *kinds):
        return [entry[0] for entry in table if entry[1] in kinds]

    def row(i):
        return vec[i : i + 1, :]

    def add_line(line, value):
        vec_s[0, line : line + 1, :] += jnp.sum(value, axis=0, keepdims=True)

    def pack(c, buf):
        line = wrow[0:1, rows_at(at.mine(c), part_rows, LANES)].astype(F32)
        col = jnp.broadcast_to(line, (8, part_rows)).T[:, 0:1].astype(jnp.int32)
        return nn(pick(col, seq), buf[...])

    fetch[0].wait()
    fetch[1].wait()
    begin(MOVES, 0)
    bias_copy = send(vec, vec2, (vec_ss, vec_sr), 0, {"mp": at.across})
    go()
    def tell(j, carry):
        k = lax.rem(at.d + j, n)
        pltpu.make_async_remote_copy(
            src_ref=tab_out.at[rows_at(k * 8, 8, 8)],
            dst_ref=tab.at[at.side, rows_at(at.d * 8, 8, 8)],
            send_sem=tab_s.at[j],
            recv_sem=tab_r.at[at.d],
            device_id={"dp": k},
            device_id_type=MESH,
        ).start()
        return carry

    lax.fori_loop(1, n, tell, 0)
    tab[at.side, rows_at(at.d * 8, 8, 8), :] = tab_out[rows_at(at.d * 8, 8, 8), :]
    vec_s[0, :, :] = jnp.zeros((GLINES, width), F32)
    dq_acc[...] = jnp.zeros_like(dq_acc)
    qkv[...] = jnp.zeros_like(qkv)
    dout[...] = jnp.zeros_like(dout)

    def hear(j, carry):
        k = lax.rem(at.d + j, n)
        landed(tab.at[at.side, rows_at(k * 8, 8, 8)], (tab_s, tab_r), k, {"dp": k})
        return carry

    lax.fori_loop(1, n, hear, 0)

    def choose(buf, stage):
        def one(k, carry):
            col = tab[at.side, rows_at(k * 8, 8, 8), :].T[0:per, 0:1].astype(jnp.int32) - 1
            rows_of = nn(pick(col, slots), buf[rows_at(k * slots, slots), :])
            stage[rows_at(k * per, per), :] = rows_of.astype(BF)
            return carry

        lax.fori_loop(0, n, one, 0)

    fetch[2].wait()
    choose(act, tok_stage)
    for c in range(CHUNKS):
        pieces["0123"[c]].step()
    go()
    tab_copy = send(tab.at[at.side], tab.at[at.side], (tab_s, tab_r), n, {"mp": at.across})
    fetch[3].wait()
    choose(dhid, cot_stage)
    go()
    need("0123")
    for c in range(HALVES):
        packed = pack(c, tok_come)
        own_x[c * part_rows : (c + 1) * part_rows, :] = packed.astype(BF)
        normal, _ = normal_rows(packed)
        n1[rows_at(at.mine(c), part_rows), :] = (normal * row(V_LN1G) + row(V_LN1B)).astype(BF)
        n1_mate.start(c)
    go()
    for c in range(HALVES):
        n1_mate.finish(c)

    def project(gi):
        def one(i, carry):
            here = rows_at(i * TILE, TILE, TILE)
            there = rows_at(gi * seq + i * TILE, TILE, TILE)
            for j in range(3):
                made = nt(n1[here, :], weight(gi, 0, j * span, (j + 1) * span))
                made = made + vec_g[gi][V_QKVB : V_QKVB + 1, j * pad : j * pad + span]
                if j == 0:
                    made = made * HD**-0.5
                qkv[there, j * pad : j * pad + span] = made.astype(BF)
            turned = qkv[there, 2 * pad :].astype(F32).T.astype(BF)
            v_t[gi * span : (gi + 1) * span, here] = turned[0:span, :]
            return carry

        lax.fori_loop(0, seq // TILE, one, 0)

    key_line = lax.broadcasted_iota(jnp.int32, (TILE, TILE), 0)
    query_line = lax.broadcasted_iota(jnp.int32, (TILE, TILE), 1)
    seen = key_line <= query_line

    def attend(gi, i):
        q0, base = i * TILE, gi * seq
        cols = slice(q0, q0 + TILE)
        for h in range(plan.heads):
            lanes = (h // 2) * LANES
            q_lanes = slice(lanes, lanes + LANES)
            k_lanes = slice(pad + lanes, pad + lanes + LANES)
            vh = v_t.at[gi * span + h * HD : gi * span + (h + 1) * HD]
            qh = head_lanes(qkv[base + q0 : base + q0 + TILE, q_lanes], h % 2 == 1)
            near = jnp.where(seen, nt(qkv[base + q0 : base + q0 + TILE, k_lanes], qh), NEG)
            top = jnp.max(near, axis=0, keepdims=True)
            if i:
                old = nt(qkv[base : base + q0, k_lanes], qh)
                top = jnp.maximum(top, jnp.max(old, axis=0, keepdims=True))
            expo = jnp.exp2((near - top) * LOG2E)
            total = jnp.sum(expo, axis=0, keepdims=True)
            out = nn(vh[:, cols], expo.astype(BF))
            if i:
                expo = jnp.exp2((old - top) * LOG2E)
                total = total + jnp.sum(expo, axis=0, keepdims=True)
                out = out + nn(vh[:, 0:q0], expo.astype(BF))
            line = gi * 4 + h
            att_t[gi * span + h * HD : gi * span + (h + 1) * HD, cols] = (out * (1.0 / total)).astype(BF)
            lse[line : line + 1, cols] = top * LOG2E + jnp.log2(total)

    blocks = seq // TILE

    def merge(c):
        def one(i, carry):
            here = rows_at(c * plan.half + i * TILE, TILE, TILE)
            total = None
            for gi in range(2):
                att = att_t[gi * span : (gi + 1) * span, here].astype(F32).T.astype(BF)
                value = nn(att, weight(gi, 0, 3 * span, 4 * span))
                total = value if total is None else total + value
            term[here, :] = total.astype(BF)
            return carry

        lax.fori_loop(0, plan.half // TILE, one, 0)

    project(0)
    for i in range(blocks):
        go()
        attend(0, i)
    go()
    need(names_of(MOVES, 0))
    landed(vec2, (vec_ss, vec_sr), 0, {"mp": at.across})
    project(1)
    for i in range(blocks):
        go()
        attend(1, i)
    go()
    tok.drain()
    for c in range(HALVES):
        merge(c)
        attn_sum.start(c)
    go()
    need("4567")
    for c in range(HALVES):
        packed = pack(c, cot_come)
        cot_p[rows_at(at.mine(c), part_rows), :] = packed.astype(BF)
        add_line(G_PROJB, packed)
        cot_mate.start(c)
        middle = own_x[c * part_rows : (c + 1) * part_rows, :].astype(F32) + (
            attn_sum.finish(c) + row(V_OUTB)
        )
        mid[c * part_rows : (c + 1) * part_rows, :] = middle
        normal, _ = normal_rows(middle)
        n2[rows_at(at.mine(c), part_rows), :] = (normal * row(V_LN2G) + row(V_LN2B)).astype(BF)
        n2_mate.start(c)
    attn_sum.drain()
    go()
    need(names_of(MOVES, 1, 2))
    tok_all.drain()
    cot_all.drain()
    cot.drain()
    for c in range(HALVES):
        n2_mate.finish(c)
        cot_mate.finish(c)

        def feed(i, carry, c=c):
            here = rows_at(c * plan.half + i * TILE, TILE, TILE)
            up, down = None, None
            for gi in range(2):
                there = rows_at(gi * seq + c * plan.half + i * TILE, TILE, TILE)
                v = nn(n2[here, :], weight(gi, 1)) + vec_g[gi][V_FCB : V_FCB + 1, :]
                square = v * v
                t = jnp.tanh(GELU * v * (1.0 + CUBE * square))
                halved = 0.5 * (1.0 + t)
                active = (v * halved).astype(BF)
                slope = halved + 0.5 * v * (1.0 - t * t) * (GELU * (1.0 + 3.0 * CUBE * square))
                act[there, :] = active
                more = nn(active, weight(gi, 2))
                up = more if up is None else up + more
                low = (nt(cot_p[here, :], weight(gi, 2)) * slope).astype(BF)
                dhid[there, :] = low
                add_line((G_FCB, G_FCB2)[gi], low.astype(F32))
                more = nt(low, weight(gi, 1))
                down = more if down is None else down + more
            mlp_term[here, :] = up.astype(BF)
            term[here, :] = down.astype(BF)
            return carry

        lax.fori_loop(0, plan.half // TILE, feed, 0)
        back_sum.start(c)
        mlp_sum.start(c)
        go()

    def weight_grad(left_ref, left_row, right_ref, right_row, dst, place):
        def one(i, carry):
            cols = rows_at(i * TILE, TILE, TILE)
            value = tn(left_ref[left_row : left_row + seq, cols], right_ref[right_row : right_row + seq, :])
            dst[rows_at(place + i * TILE, TILE, TILE), :] = value.astype(BF)
            return carry

        lax.fori_loop(0, width // TILE, one, 0)

    for gi in (1, 0):
        weight_grad(act, gi * seq, cot_p, 0, grads, gi * width)
        if gi:
            begin(TOTALS, "P", True)
            go()
    begin(TOTALS, "P", False)
    go()
    for c in range(HALVES):
        mine = slice(c * part_rows, (c + 1) * part_rows)
        where = rows_at(at.mine(c), part_rows)
        grad2 = back_sum.finish(c)
        middle = mid[mine, :]
        res[where, :] = (middle + (mlp_sum.finish(c) + row(V_PROJB))).astype(BF)
        res_mate.start(c)
        normal, inv = normal_rows(middle)
        grad_mid = cot_p[where, :].astype(F32) + norm_back(grad2, normal, inv, row(V_LN2G))
        low = grad_mid.astype(BF)
        mid[mine, :] = grad_mid
        dattn[where, :] = low
        dattn_mate.start(c)
        add_line(G_LN2G, grad2 * normal)
        add_line(G_LN2B, grad2)
        add_line(G_OUTB, low.astype(F32))
    mlp_sum.drain()
    go()
    for gi in (1, 0):
        weight_grad(n2, 0, dhid, gi * seq, grads, (2 + gi) * width)
        if gi:
            begin(TOTALS, "F", True)
            go()
    begin(TOTALS, "F", False)
    back_sum.drain()
    go()

    def unpack(c, out):
        start = (2 * c + at.core) * own
        out[c * own : (c + 1) * own, :] = nn(pick_rows(wrow[0:1, :], start, own), res[...]).astype(BF)

    for c in range(HALVES):
        res_mate.finish(c)
    for c in range(CHUNKS):
        unpack(c, going.at[0])
        pieces["ijkl"[c]].step()
    go()
    for c in range(HALVES):
        dattn_mate.finish(c)
    for gi in range(2):

        def back_out(i, carry, gi=gi):
            here = rows_at(i * TILE, TILE, TILE)
            there = rows_at(gi * seq + i * TILE, TILE, TILE)
            low = nt(dattn[here, :], weight(gi, 0, 3 * span, 4 * span)).astype(BF)
            dout[there, 0:span] = low
            turned = dout[there, :].astype(F32).T
            both = turned[0:span, :] * att_t[gi * span : (gi + 1) * span, here].astype(F32)
            for h in range(plan.heads):
                line = gi * 4 + h
                delta[line : line + 1, here] = jnp.sum(both[h * HD : (h + 1) * HD, :], axis=0, keepdims=True)
            return carry

        lax.fori_loop(0, seq // TILE, back_out, 0)
        grads2[gi * width + 3 * span : gi * width + 4 * span, :] = nn(
            att_t[gi * span : (gi + 1) * span, :], dattn[...]
        ).astype(BF)

    def attend_back(gi, i):
        k0, base = i * TILE, gi * seq
        k_rows = slice(base + k0, base + k0 + TILE)
        parts = []
        for h in range(plan.heads):
            lanes = (h // 2) * LANES
            q_lanes = slice(lanes, lanes + LANES)
            kh = head_lanes(qkv[k_rows, pad + lanes : pad + lanes + LANES], h % 2 == 1)
            vh = head_lanes(qkv[k_rows, 2 * pad + lanes : 2 * pad + lanes + LANES], h % 2 == 1)
            if h % 2 == 0:
                turned = qkv[k_rows, pad + lanes : pad + lanes + LANES].astype(F32).T.astype(BF)
            kt = turned[(h % 2) * HD : (h % 2 + 1) * HD, :]
            line = gi * 4 + h
            dk = dv = None
            for q0, q1 in ((k0, k0 + TILE), (k0 + TILE, seq)):
                if q0 == q1:
                    continue
                q_all = qkv[base + q0 : base + q1, q_lanes]
                do_all = dout[base + q0 : base + q1, q_lanes]
                prob = jnp.exp2(nt(kh, q_all) * LOG2E - lse[line : line + 1, q0:q1])
                if q0 == k0:
                    prob = jnp.where(seen, prob, 0.0)
                low = (prob * (nt(vh, do_all) - delta[line : line + 1, q0:q1])).astype(BF)
                more_v, more_k = nn(prob.astype(BF), do_all), nn(low, q_all)
                dv = more_v if dv is None else dv + more_v
                dk = more_k if dk is None else dk + more_k
                dq_acc[gi * span + h * HD : gi * span + (h + 1) * HD, q0:q1] += nn(kt, low)
            parts.append((dk, dv))
        for h in range(0, plan.heads, 2):
            lanes = (h // 2) * LANES
            for j in range(2):
                value = head_lanes(parts[h][j], False)
                if h + 1 < plan.heads:
                    value = value + head_lanes(parts[h + 1][j], True)
                start = (1 + j) * pad + lanes
                dqkv[k_rows, start : start + LANES] = value.astype(BF)

    def qkv_weight_grad(gi):
        def turn_dq(i, carry):
            here = rows_at(i * TILE, TILE, TILE)
            there = rows_at(gi * seq + i * TILE, TILE, TILE)
            turned = jnp.concatenate(
                [dq_acc[gi * span : (gi + 1) * span, here], jnp.zeros((pad - span, TILE), F32)], axis=0
            )
            dqkv[there, 0:pad] = (turned.T * HD**-0.5).astype(BF)
            return carry

        lax.fori_loop(0, seq // TILE, turn_dq, 0)
        return lambda: weigh(gi)

    def weigh(gi):
        for j in range(3):
            row0 = gi * width + j * span
            grads2[row0 : row0 + span, :] = tn(
                dqkv[gi * seq : (gi + 1) * seq, j * pad : j * pad + span], n1[...]
            ).astype(BF)

    for i in range(blocks):
        go()
        attend_back(1, i)
    go()
    qkv_weight_grad(1)()
    begin(TOTALS, "A", True)
    for i in range(blocks):
        go()
        attend_back(0, i)
    go()
    weigh_mine = qkv_weight_grad(0)
    for c in range(HALVES):

        def back_project(i, carry, c=c):
            here = rows_at(c * plan.half + i * TILE, TILE, TILE)
            total = None
            for gi in range(2):
                there = rows_at(gi * seq + c * plan.half + i * TILE, TILE, TILE)
                add_line((G_QKVB, G_QKVB2)[gi], dqkv[there, :].astype(F32))
                for j in range(3):
                    more = nn(dqkv[there, j * pad : j * pad + span], weight(gi, 0, j * span, (j + 1) * span))
                    total = more if total is None else total + more
            term[here, :] = total.astype(BF)
            return carry

        lax.fori_loop(0, plan.half // TILE, back_project, 0)
        norm_sum.start(c)
    go()
    for c in range(HALVES):
        mine = slice(c * part_rows, (c + 1) * part_rows)
        grad1 = norm_sum.finish(c)
        normal, inv = normal_rows(own_x[mine, :].astype(F32))
        dx = mid[mine, :] + norm_back(grad1, normal, inv, row(V_LN1G))
        if c == 0:
            res_mate.drain()
        res[rows_at(at.mine(c), part_rows), :] = dx.astype(BF)
        dx_mate.start(c)
        add_line(G_LN1G, grad1 * normal)
        add_line(G_LN1B, grad1)
    bias_copy.wait_send()
    pieces["v"].step()
    go()
    for c in range(HALVES):
        dx_mate.finish(c)
    for c in range(CHUNKS):
        unpack(c, going.at[1])
        pieces["rstu"[c]].step()
    go()
    weigh_mine()
    begin(TOTALS, "A", False)
    for _ in range(TAIL):
        go()
    need(pieces)
    out_way.drain()
    grad_way.drain()

    def told_all(j, carry):
        k = lax.rem(at.d + j, n)
        left(tab_out.at[rows_at(k * 8, 8, 8)], (tab_s, tab_r), j, {"dp": k})
        return carry

    lax.fori_loop(1, n, told_all, 0)
    tab_copy.wait_send()
    landed(tab.at[1 - at.side], (tab_s, tab_r), n, {"mp": at.across})
    for each in (n1_mate, cot_mate, n2_mate, dattn_mate, dx_mate, norm_sum):
        each.drain()


def finish_kernel(rows_a, rows_b, tab, proj, fc, qkv, out, out_a, out_b, proj_f, fc_f, qkv_f, out_f):
    proj_f[...] = proj[...].astype(F32)
    fc_f[...] = fc[...].astype(F32)
    qkv_f[...] = qkv[...].astype(F32)
    out_f[...] = out[...].astype(F32)
    n = tab.shape[1] // 8
    slots = rows_a.shape[0] // n

    def one(k, carry):
        here = rows_at(k * slots, slots)
        lines = [tab[side, rows_at(k * 8, 8, 8), :][0:1, 0 : slots // 2] for side in range(2)]
        slot = jnp.concatenate(lines, axis=1).astype(jnp.int32) - 1
        place = lax.broadcasted_iota(jnp.int32, (slots, slots), 0)
        hot = jnp.where(place == slot, 1.0, 0.0).astype(BF)
        out_a[here, :] = nn(hot, rows_a[here, :]).astype(BF)
        out_b[here, :] = nn(hot, rows_b[here, :]).astype(BF)
        return carry

    lax.fori_loop(0, n, one, 0)


def body(
    tokens,
    cotangent,
    seq_lengths,
    source_slot,
    ln1_gain,
    ln1_bias,
    qkv_weight,
    qv_bias,
    output_projection_weight,
    out_bias,
    ln2_gain,
    ln2_bias,
    fc_weight,
    fc_bias,
    proj_weight,
    proj_bias,
):
    rows, width = tokens.shape
    span = qkv_weight.shape[2]
    n, members = lax.axis_size("dp"), lax.axis_size("mp")
    plan = Plan(n, members, rows, width, span // HD)
    pad, seq = plan.pad, plan.seq

    vectors = (ln1_gain, ln1_bias, out_bias, ln2_gain, ln2_bias, proj_bias, fc_bias)
    line = jnp.arange(8, dtype=jnp.int32)[:, None]
    vec = jnp.zeros((8, width), BF)
    for i, v in enumerate(vectors):
        vec = jnp.where(line == i, v[None, :], vec)
    vm = pl.BlockSpec(memory_space=pltpu.VMEM)
    hbm = pl.BlockSpec(memory_space=pl.ANY)
    shape = jax.ShapeDtypeStruct
    quarter = rows // members
    dma = pltpu.SemaphoreType.DMA
    rooms = [total_room(entry[3] - entry[2], n, entry[5]) for entry in TOTALS]
    landing, sems = (sum(room[i] for room in rooms) for i in range(2))
    hops = 2 + (n - 1).bit_length()

    def vmem(*dims, dtype=BF):
        return pltpu.VMEM(dims, dtype)

    block_rows, grad_rows, proj_total, fc_total, attn_total, vec_total, tab = pl.pallas_call(
        functools.partial(block_kernel, plan),
        out_shape=(
            shape((rows, width), BF),
            shape((rows, width), BF),
            shape((width, width), BF),
            shape((width, width), BF),
            shape((width, width), BF),
            shape((8, width), F32),
            shape((2, 8 * n, LANES), F32),
        ),
        in_specs=[hbm, hbm, vm, pl.BlockSpec(memory_space=pltpu.SMEM), vm, vm, hbm, hbm, vm, vm],
        out_specs=(hbm,) * 5 + (vm, vm),
        scratch_shapes=[
            vmem(8, width, dtype=F32),
            vmem(8 * n, LANES, dtype=F32),
            vmem(8, seq, dtype=jnp.int32),
            vmem(width, width),
            vmem(8, width, dtype=F32),
            vmem(3 * width, width),
            vmem(rows, width),
            vmem(rows, width),
            vmem(quarter, width),
            vmem(seq, width),
            vmem(seq, width),
            vmem(seq, width),
            vmem(seq, width),
            vmem(2 * seq, 3 * pad),
            vmem(2 * span, seq),
            vmem(2 * span, seq),
            vmem(8, seq, dtype=F32),
            vmem(8, seq, dtype=F32),
            vmem(seq, width),
            vmem(seq // 2, width),
            vmem(seq // 2, width),
            vmem(seq // 2, width),
            vmem(seq // 2, width, dtype=F32),
            vmem(2 * seq, pad),
            vmem(2 * span, seq, dtype=F32),
            vmem(4 * width, width),
            vmem(landing, width),
            vmem(seq, width),
            vmem(2, quarter, width),
            vmem(hops, GLINES, width, dtype=F32),
            vmem(hops, GLINES, width, dtype=F32),
            dma((plan.split, n)),
            dma((CHUNKS, plan.in_chunk)),
            dma((plan.split, n)),
            dma((CHUNKS, plan.in_chunk)),
            dma((2, CHUNKS)),
            dma((2, CHUNKS)),
            dma((6, HALVES)),
            dma((6, HALVES)),
            dma((4, HALVES)),
            dma((4, HALVES)),
            dma((len(MOVES), 4)),
            dma((len(MOVES), 4)),
            dma((n + 1,)),
            dma((n + 1,)),
            dma((2, CHUNKS, plan.in_chunk)),
            dma((2, plan.split, n)),
            dma((2, plan.split)),
            dma((2, 3, plan.split, n)),
            dma((2, 3, plan.split, n)),
            dma((sems,)),
            dma((sems,)),
            dma((hops + 1,)),
            dma((hops + 1,)),
            dma((4,)),
        ],
        compiler_params=pltpu.CompilerParams(
            collective_id=0, has_side_effects=True, vmem_limit_bytes=VMEM_LIMIT
        ),
        name="block",
    )(
        tokens,
        cotangent,
        source_slot.reshape(1, rows),
        seq_lengths,
        vec,
        qv_bias,
        qkv_weight.transpose(1, 2, 0).reshape(3 * span, width),
        output_projection_weight,
        fc_weight,
        proj_weight,
    )
    def tall(count):
        return pl.BlockSpec((count // STEPS, width), lambda i: (i, 0))

    block_out, input_grad, proj_grad, fc_grad, qkv_grad, out_grad = pl.pallas_call(
        finish_kernel,
        out_shape=(
            shape((rows, width), BF),
            shape((rows, width), BF),
            shape((width, width), F32),
            shape((width, width), F32),
            shape((3 * span, width), F32),
            shape((span, width), F32),
        ),
        grid=(STEPS,),
        in_specs=[
            tall(rows),
            tall(rows),
            pl.BlockSpec((2, 8 * n // STEPS, LANES), lambda i: (0, i, 0)),
            tall(width),
            tall(width),
            tall(3 * span),
            pl.BlockSpec((span // STEPS, width), lambda i: (3 * STEPS + i, 0)),
        ],
        out_specs=(tall(rows), tall(rows), tall(width), tall(width), tall(3 * span), tall(span)),
        compiler_params=pltpu.CompilerParams(vmem_limit_bytes=VMEM_LIMIT),
        name="finish",
    )(block_rows, grad_rows, tab, proj_total, fc_total, attn_total, attn_total)
    qkv_sums = vec_total[G_QKVB].reshape(3, pad)[:, :span]
    return (
        block_out,
        input_grad,
        vec_total[G_LN1G],
        vec_total[G_LN1B],
        qkv_grad.reshape(3, span, width).transpose(2, 0, 1),
        jnp.stack([qkv_sums[0], qkv_sums[2]]),
        out_grad,
        vec_total[G_OUTB],
        vec_total[G_LN2G],
        vec_total[G_LN2B],
        fc_grad,
        vec_total[G_FCB],
        proj_grad,
        vec_total[G_PROJB],
    )


def solution(mesh):
    return jax.shard_map(
        body,
        mesh=mesh,
        in_specs=(
            P("dp", None),
            P("dp", None),
            P("dp", None),
            P("dp"),
            P(),
            P(),
            P(None, None, "mp"),
            P(None, "mp"),
            P("mp", None),
            P(),
            P(),
            P(),
            P(None, "mp"),
            P("mp"),
            P("mp", None),
            P(),
        ),
        out_specs=(
            P("dp", None),
            P("dp", None),
            P(),
            P(),
            P(None, None, "mp"),
            P(None, "mp"),
            P("mp", None),
            P(),
            P(),
            P(),
            P(None, "mp"),
            P("mp"),
            P("mp", None),
            P(),
        ),
        check_vma=False,
    )
```

```python
import functools

import jax
import jax.numpy as jnp
from jax import lax
from jax.experimental import pallas as pl
from jax.experimental.pallas import tpu as pltpu
from jax.sharding import PartitionSpec as P

MESH = pl.DeviceIdType.MESH
BF = jnp.bfloat16
F32 = jnp.float32
HD = 64
EPSILON = 1e-05
NEG = -1e30
LOG2E = 1.4426950408889634
TILE = 256
HALVES = 2
STEPS = 2
CHUNKS = 4
LANES = 128
VMEM_LIMIT = 60 * 2**20


class Plan:
    def __init__(self, n, members, rows, width, heads):
        self.n, self.members, self.rows, self.width, self.heads = n, members, rows, width, heads
        self.slots = rows // n
        self.seq = rows // 2
        self.per = self.seq // n
        self.group = max(1, 32 // self.per)
        self.share = self.group * self.per // 2
        self.groups = n // self.group
        self.own = self.seq // (2 * CHUNKS)
        self.take = max(16, self.share // CHUNKS)
        self.split = self.share // self.take
        self.in_chunk = self.own // self.take
        self.half = self.seq // HALVES
        self.part = self.half // 2
        self.pad = -(-heads * HD // LANES) * LANES

    def come_index(self, source, turn):
        grp = over(source, self.group)
        inside = under(source, self.group) * self.per + turn
        core, row = over(inside, self.share), under(inside, self.share)
        chunk = over(grp, self.in_chunk) * self.split + over(row, self.take)
        return (
            (2 * chunk + core) * self.own
            + under(grp, self.in_chunk) * self.take
            + under(row, self.take)
        )

    def source_of(self, core):
        return (core * self.share) // self.per, lax.rem(core * self.share, self.per)


def over(x, size):
    return lax.shift_right_logical(x, jnp.full_like(x, size.bit_length() - 1))


def under(x, size):
    return x & (size - 1)


def nn(a, b):
    return lax.dot_general(a, b, (((1,), (0,)), ((), ())), preferred_element_type=F32)


def nt(a, b):
    return lax.dot_general(a, b, (((1,), (1,)), ((), ())), preferred_element_type=F32)


def tn(a, b):
    return lax.dot_general(a, b, (((0,), (0,)), ((), ())), preferred_element_type=F32)


def rows_at(start, count, step=16):
    if not isinstance(start, int):
        start = pl.multiple_of(start, step)
    return pl.ds(start, count)


class Place:
    def __init__(self, plan):
        self.plan = plan
        self.d = lax.axis_index("dp")
        self.m = lax.axis_index("mp")
        self.core = lax.rem(self.m, 2)
        self.side = self.m // 2
        self.mate = self.m + 1 - 2 * self.core
        self.across = lax.rem(self.m + 2, plan.members)
        self.source, self.offset = plan.source_of(self.core)

    def mine(self, c, flip=False):
        core = 1 - self.core if flip else self.core
        return (2 * c + core) * self.plan.part


def send(src, dst, sems, index, device):
    copy = pltpu.make_async_remote_copy(
        src_ref=src,
        dst_ref=dst,
        send_sem=sems[0].at[index],
        recv_sem=sems[1].at[index],
        device_id=device,
        device_id_type=MESH,
    )
    copy.start()
    return copy


def landed(dst, sems, index, device):
    pltpu.make_async_remote_copy(
        src_ref=dst,
        dst_ref=dst,
        send_sem=sems[0].at[index],
        recv_sem=sems[1].at[index],
        device_id=device,
        device_id_type=MESH,
    ).wait_recv()


def left(src, sems, index, device):
    pltpu.make_async_remote_copy(
        src_ref=src,
        dst_ref=src,
        send_sem=sems[0].at[index],
        recv_sem=sems[1].at[index],
        device_id=device,
        device_id_type=MESH,
    ).wait_send()


def greet(plan, at):
    barrier = pltpu.get_barrier_semaphore()

    def signal(j, carry):
        pl.semaphore_signal(
            barrier, inc=1, device_id={"dp": lax.rem(at.d + j, plan.n)}, device_id_type=MESH
        )
        return carry

    lax.fori_loop(1, plan.n, signal, 0)
    pl.semaphore_signal(barrier, inc=1, device_id={"mp": at.mate}, device_id_type=MESH)
    pl.semaphore_signal(barrier, inc=1, device_id={"mp": at.across}, device_id_type=MESH)


def all_here(plan):
    pl.semaphore_wait(pltpu.get_barrier_semaphore(), plan.n + 1)


class MateGather:
    def __init__(self, at, buf, sems, count):
        self.at, self.buf, self.sems, self.count, self.copies = at, buf, sems, count, []

    def rows(self, c, core):
        return self.buf.at[rows_at((2 * c + core) * self.count, self.count)]

    def start(self, c):
        here = self.rows(c, self.at.core)
        self.copies.append(send(here, here, self.sems, c, {"mp": self.at.mate}))

    def finish(self, c):
        landed(self.rows(c, 1 - self.at.core), self.sems, c, {"mp": self.at.mate})

    def drain(self):
        for copy in self.copies:
            copy.wait_send()
        self.copies = []


class MateSum:
    def __init__(self, at, term, land, sems):
        self.at, self.term, self.land, self.sems, self.copies = at, term, land, sems, []

    def start(self, c):
        plan, at = self.at.plan, self.at
        src = self.term.at[rows_at(at.mine(c, True), plan.part)]
        dst = self.land.at[rows_at(c * plan.part, plan.part)]
        self.copies.append(send(src, dst, self.sems, c, {"mp": at.mate}))

    def finish(self, c):
        plan, at = self.at.plan, self.at
        where = rows_at(c * plan.part, plan.part)
        landed(self.land.at[where], self.sems, c, {"mp": at.mate})
        mine = self.term[rows_at(at.mine(c), plan.part), :]
        return mine.astype(F32) + self.land[where, :].astype(F32)

    def drain(self):
        for copy in self.copies:
            copy.wait_send()
        self.copies = []


class Incoming:
    def __init__(self, at, source, sems, landing):
        plan = at.plan
        self.at, self.source, self.sems, self.landing = at, source, sems, landing
        self.sends = None
        if plan.group > 1:
            self.sends = lax.rem(at.d, plan.group) == at.source

    def guarded(self, run):
        if self.sends is None:
            run()
        else:
            pl.when(self.sends)(run)

    def mine(self, part):
        plan, at = self.at.plan, self.at
        grp = at.d // plan.group
        return (grp // plan.in_chunk) * plan.split + part, lax.rem(grp, plan.in_chunk)

    def piece(self, k, part):
        plan = self.at.plan
        start = k * plan.per + self.at.offset + part * plan.take
        return self.source.at[rows_at(start, plan.take)]

    def start(self, part):
        plan, at = self.at.plan, self.at
        c, gi = self.mine(part)

        def one(j, carry):
            k = lax.rem(at.d + j, plan.n)
            pltpu.make_async_remote_copy(
                src_ref=self.piece(k, part),
                dst_ref=self.landing(c, gi),
                send_sem=self.sems[0].at[part, j],
                recv_sem=self.sems[1].at[c, gi],
                device_id={"dp": k},
                device_id_type=MESH,
            ).start()
            return carry

        def run():
            lax.fori_loop(1, plan.n, one, 0)
            pltpu.make_async_copy(
                self.piece(at.d, part), self.landing(c, gi), self.sems[1].at[c, gi]
            ).start()

        self.guarded(run)

    def wait(self, c):
        plan, at = self.at.plan, self.at

        def one(gi, carry):
            landed(self.landing(c, gi), (self.sems[1], self.sems[1]), (c, gi), {"dp": at.d})
            return carry

        lax.fori_loop(0, plan.in_chunk, one, 0)

    def drain(self):
        plan, at = self.at.plan, self.at

        def run():
            for part in range(plan.split):

                def one(j, carry, part=part):
                    k = lax.rem(at.d + j, plan.n)
                    left(self.piece(k, part), (self.sems[0], self.sems[0]), (part, j), {"dp": k})
                    return carry

                lax.fori_loop(1, plan.n, one, 0)

        self.guarded(run)


class Outgoing:
    def __init__(self, at, rows_ref, out, sems, local_sem, share_sems):
        plan = at.plan
        self.at, self.rows_ref, self.out = at, rows_ref, out
        self.sems, self.local_sem, self.share_sems = sems, local_sem, share_sems

    def holds(self, member):
        plan = self.at.plan
        if plan.group == 1:
            return None
        return lax.rem(self.at.d, plan.group) == plan.source_of(lax.rem(member, 2))[0]

    def guarded(self, member, run):
        if self.at.plan.group == 1:
            run()
        else:
            pl.when(self.holds(member))(run)

    def place(self, k, part, member):
        plan = self.at.plan
        first = (member // 2) * plan.per + plan.source_of(lax.rem(member, 2))[1]
        start = k * plan.slots + first + part * plan.take
        return self.out.at[rows_at(start, plan.take)]

    def each(self, c, remote, local):
        plan, at = self.at.plan, self.at
        part = c % plan.split

        def one(gi, carry):
            grp = (c // plan.split) * plan.in_chunk + gi
            dest = grp * plan.group + at.source
            src = self.rows_ref.at[rows_at(c * plan.own + gi * plan.take, plan.take)]
            dst = self.place(at.d, part, at.m)
            pl.when(dest != at.d)(lambda: remote(gi, part, src, dst, dest))
            pl.when(dest == at.d)(lambda: local(gi, part, src, dst))
            return carry

        lax.fori_loop(0, plan.in_chunk, one, 0)

    def copy(self, c, gi, part, src, dst, dest):
        return pltpu.make_async_remote_copy(
            src_ref=src,
            dst_ref=dst,
            send_sem=self.sems[0].at[c, gi],
            recv_sem=self.sems[1].at[part, self.at.d],
            device_id={"dp": dest},
            device_id_type=MESH,
        )

    def start(self, c):
        def local(gi, part, src, dst):
            pltpu.make_async_copy(src, dst, self.local_sem.at[part]).start()

        self.each(c, lambda gi, part, src, dst, dest: self.copy(c, gi, part, src, dst, dest).start(), local)

    def drain(self):
        for c in range(CHUNKS):
            self.each(
                c,
                lambda gi, part, src, dst, dest: self.copy(c, gi, part, src, dst, dest).wait_send(),
                lambda gi, part, src, dst: None,
            )

    def loop(self, part, run):
        lax.fori_loop(0, self.at.plan.n, lambda k, carry: (run(k), carry)[1], 0)

    def share(self, part):
        at = self.at

        def run():
            def one(k):
                here = self.place(k, part, at.m)

                def remote():
                    landed(here, (self.sems[1], self.sems[1]), (part, k), {"dp": at.d})

                def local():
                    pltpu.make_async_copy(here, here, self.local_sem.at[part]).wait()

                pl.when(k != at.d)(remote)
                pl.when(k == at.d)(local)
                send(here, here, self.share_sems, (1, part, k), {"mp": at.across})
                send(here, here, self.share_sems, (0, part, k), {"mp": at.mate})

            self.loop(part, one)

        self.guarded(at.m, run)

    def forward(self, part):
        at = self.at

        def run():
            def one(k):
                there = self.place(k, part, at.across)
                landed(there, self.share_sems, (1, part, k), {"mp": at.across})
                send(there, there, self.share_sems, (2, part, k), {"mp": at.mate})

            self.loop(part, one)

        self.guarded(at.across, run)

    def finish(self, part):
        at = self.at
        corner = (1 - at.side) * 2 + 1 - at.core

        def near():
            self.loop(
                part,
                lambda k: landed(
                    self.place(k, part, at.mate), self.share_sems, (0, part, k), {"mp": at.mate}
                ),
            )

        def far():
            self.loop(
                part,
                lambda k: landed(
                    self.place(k, part, corner), self.share_sems, (2, part, k), {"mp": at.mate}
                ),
            )

        def sent():
            def one(k):
                here = self.place(k, part, at.m)
                left(here, self.share_sems, (1, part, k), {"mp": at.across})
                left(here, self.share_sems, (0, part, k), {"mp": at.mate})

            self.loop(part, one)

        def passed():
            self.loop(
                part,
                lambda k: left(
                    self.place(k, part, at.across), self.share_sems, (2, part, k), {"mp": at.mate}
                ),
            )

        self.guarded(at.mate, near)
        self.guarded(corner, far)
        self.guarded(at.m, sent)
        self.guarded(at.across, passed)


def halvings(rows, n, order):
    steps, size = [], rows
    bits = [1 << i for i in range((n - 1).bit_length())]
    for i in order:
        bits.insert(0, bits.pop(i))
    for bit in bits:
        if size % 32 == 0:
            size //= 2
            steps.append((bit, True, size))
        else:
            steps.append((bit, False, size))
    return steps


def trail_of(at, rows, order):
    offset, trail, size = 0, [], rows
    for bit, halve, size in halvings(rows, at.plan.n, order):
        if halve:
            high = lax.rem(at.d // bit, 2)
            partner = {"dp": at.d + (1 - 2 * high) * bit}
            trail.append((offset, offset + high * size, size, partner))
            offset = offset + high * size
    return offset, size, trail


class Steps:
    def __init__(self, *runs):
        self.runs, self.next = list(runs), 0

    def step(self):
        if self.next < len(self.runs):
            self.next += 1
            self.runs[self.next - 1]()

    def finish(self):
        while self.next < len(self.runs):
            self.step()


class Stepped:
    def __init__(self):
        self.jobs, self.next, self.pending = [], 0, None

    def step(self):
        if self.pending is not None:
            self.pending[0](self.pending[1])
            self.pending = None
        if self.next < len(self.jobs):
            start, end = self.jobs[self.next]
            self.next += 1
            self.pending = (end, start())

    def finish(self):
        while self.pending is not None or self.next < len(self.jobs):
            self.step()

    def spread(self, buf, keep, other, size, sems, index, partner, source=None, before_end=None):
        def start():
            here = buf.at[rows_at(keep, size)]
            return send(here if source is None else source, here, sems, index, partner)

        def end(copy):
            copy.wait_send()
            landed(buf.at[rows_at(other, size)], sems, index, partner)
            if before_end is not None:
                before_end()

        self.jobs.append((start, end))


class Weights(Stepped):
    def __init__(self, at, source, dst, sems, index, bits):
        super().__init__()
        offset, trail, size = 0, [], source.shape[0]
        for bit in bits:
            if bit < at.plan.n:
                size //= 2
                high = lax.rem(at.d // bit, 2)
                partner = {"dp": at.d + (1 - 2 * high) * bit}
                trail.append((offset, offset + high * size, size, partner))
                offset = offset + high * size
        slice_rows = rows_at(offset, size)
        across = {"mp": at.across}

        def start():
            return send(source.at[slice_rows], dst.at[slice_rows], sems, index, across)

        def end(copy):
            copy.wait_send()
            landed(dst.at[slice_rows], sems, index, across)

        self.jobs.append((start, end))
        for i, (before, keep, length, partner) in enumerate(reversed(trail)):
            self.spread(dst, keep, 2 * before + length - keep, length, sems, index + 1 + i, partner)


class Total(Stepped):
    def __init__(self, at, first, origins, out, landing, base, sems, index, order, early):
        super().__init__()
        self.at, self.landing = at, landing
        rows, n = out.shape[0], at.plan.n
        steps = halvings(rows, n, order)
        room = sum(size for _, _, size in steps)
        sources = [(first, origin) for origin in origins]
        if early:
            self.cross(sources, base, rows, (sems, index))
            sources, index, base = [(landing, base)], index + 1, base + rows
        lands = [base + i * room for i in range(len(sources))]
        for bit, halve, size in steps:
            high = lax.rem(at.d // bit, 2)
            partner = {"dp": at.d + (1 - 2 * high) * bit}
            keep = high * size if halve else 0
            give = (1 - high) * size if halve else 0
            self.exchange(sources, give, keep, size, list(lands), (sems, index), partner)
            index += len(sources)
            sources = [(landing, land) for land in lands]
            lands = [land + size for land in lands]
        offset, size, trail = trail_of(at, rows, order)
        if not early:
            self.cross(sources, base + 2 * room, size, (sems, index))
            sources, index = [(landing, base + 2 * room)], index + 1
        done = landing.at[rows_at(sources[0][1], size)]
        local = pltpu.make_async_copy(done, out.at[rows_at(offset, size)], sems[0].at[index])
        self.jobs[-1] = (self.jobs[-1][0], self.then(self.jobs[-1][1], local.start))
        index += 1
        for i, (before, keep, length, partner) in enumerate(reversed(trail)):
            source, settle = (done, local.wait) if i == 0 else (None, None)
            self.spread(
                out, keep, 2 * before + length - keep, length, sems, index + i, partner, source, settle
            )

    def then(self, end, more):
        def both(copy):
            end(copy)
            more()

        return both

    def add(self, first, origin, land, size):
        step = 96 if size % 96 == 0 else (32 if size % 32 == 0 else 16)

        def one(i, carry):
            here = rows_at(origin + i * step, step)
            there = rows_at(land + i * step, step)
            value = first[here, :].astype(F32) + self.landing[there, :].astype(F32)
            self.landing[there, :] = value.astype(BF)
            return carry

        lax.fori_loop(0, size // step, one, 0)

    def exchange(self, sources, give, keep, size, lands, sems, partner):
        sems, index = sems

        def start():
            return [
                send(
                    ref.at[rows_at(origin + give, size)],
                    self.landing.at[rows_at(land, size)],
                    sems,
                    index + i,
                    partner,
                )
                for i, ((ref, origin), land) in enumerate(zip(sources, lands))
            ]

        def end(copies):
            for copy, (ref, origin), land in zip(copies, sources, lands):
                copy.wait()
                self.add(ref, origin + keep, land, size)

        self.jobs.append((start, end))

    def cross(self, sources, land, size, sems):
        sems, index = sems
        (mine, mine_at), (theirs, theirs_at) = sources

        def start():
            return send(
                theirs.at[rows_at(theirs_at, size)],
                self.landing.at[rows_at(land, size)],
                sems,
                index,
                {"mp": self.at.across},
            )

        def end(copy):
            copy.wait()
            self.add(mine, mine_at, land, size)

        self.jobs.append((start, end))


def total_room(rows, n, early):
    steps = halvings(rows, n, ())
    size, spreads = steps[-1][2], sum(1 for _, halve, _ in steps if halve)
    room, groups = sum(step[2] for step in steps), 1 if early else 2
    return groups * room + (rows if early else size), groups * len(steps) + 2 + spreads


def normal_rows(x):
    centered = x - jnp.mean(x, axis=-1, keepdims=True)
    inv = lax.rsqrt(jnp.mean(centered * centered, axis=-1, keepdims=True) + EPSILON)
    return centered * inv, inv


def norm_back(grad, normal, inv, gain):
    scaled = grad * gain
    return inv * (
        scaled
        - jnp.mean(scaled, axis=-1, keepdims=True)
        - normal * jnp.mean(scaled * normal, axis=-1, keepdims=True)
    )


def pick(index_col, count):
    lanes = lax.broadcasted_iota(jnp.int32, (index_col.shape[0], count), 1)
    return jnp.where(lanes == index_col, 1.0, 0.0).astype(BF)


def pick_rows(index_row, first, count):
    lines = lax.broadcasted_iota(jnp.int32, (count, index_row.shape[1]), 0) + first
    return jnp.where(lines == index_row, 1.0, 0.0).astype(BF)


def head_lanes(x, odd):
    lane = lax.broadcasted_iota(jnp.int32, x.shape, 1)
    return jnp.where((lane >= HD) == odd, x, jnp.zeros_like(x))


V_LN1G, V_LN1B, V_OUTB, V_LN2G, V_LN2B, V_PROJB, V_FCB, V_QKVB = range(8)
G_LN1G, G_LN1B, G_LN2G, G_LN2B, G_OUTB, G_PROJB, G_FCB, G_QKVB, G_FCB2, G_QKVB2 = range(10)
SHARED = 6
MOVES = (
    ("a", 0, 0, 256, (2,)),
    ("b", 0, 256, 512, (1,)),
    ("c", 0, 512, 768, (1,)),
    ("f", 1, 0, 384, (2, 1)),
    ("g", 1, 384, 768, (1,)),
    ("p", 2, 0, 768, ()),
)
TOTALS = (
    ("F", "F", 0, 256, (), True),
    ("G", "F", 256, 512, (), True),
    ("H", "F", 512, 768, (), True),
    ("A", "A", 0, 256, (1,), True),
    ("B", "A", 256, 512, (), True),
    ("C", "A", 512, 768, (), True),
    ("P", "P", 0, 256, (), False),
    ("Q", "P", 256, 512, (), True),
    ("X", "P", 512, 768, (1,), False),
)
SCHEDULE = (
    "",
    "fgpa",
    "b045670c1f12b23ag3",
    "4c",
    "",
    "54",
    "",
    "f",
    "65",
    "",
    "6",
    "7",
    "",
    "7g",
    "",
    "pf",
    "",
    "",
    "",
    "",
    "",
    "",
    "",
    "",
    "QPX",
    "",
    "",
    "F",
    "",
    "Q",
    "",
    "G",
    "PX",
    "jkil",
    "FQ",
    "HP",
    "G",
    "FXQHAGrsBHtuCBFQjACGjAHBkFkQiCiGlvQFAPXlHBGFrCrH",
    "AsGPsXtHBPtCAuvBXvuCvPvABXC",
)
TAIL = 2
GLINES = 16
GELU = 0.7978845608028654
CUBE = 0.044715


class VecTotal(Stepped):
    def __init__(self, hops, given, taken, out, sems):
        super().__init__()
        line = lax.broadcasted_iota(jnp.int32, (8, out.shape[1]), 0)
        for i, device in enumerate(hops):

            def start(i=i, device=device):
                return send(given.at[i], taken.at[i], sems, i + 1, device)

            def end(copy, i=i):
                copy.wait()
                low, high = taken[i, 0:8, :], taken[i, 8:16, :]
                if i == 0:
                    low, high = jnp.where(line < SHARED, low, 0.0), jnp.zeros_like(high)
                elif i == 1:
                    low = jnp.concatenate([low[0:SHARED, :], high[0:2, :]], axis=0)
                    high = jnp.zeros_like(high)
                if i + 1 < len(hops):
                    given[i + 1, 0:8, :] = given[i, 0:8, :] + low
                    given[i + 1, 8:16, :] = given[i, 8:16, :] + high
                else:
                    out[...] = given[i, 0:8, :] + low

            self.jobs.append((start, end))


def list_slots(plan, at, slot_row, lengths, wrow, tab_out):
    n, rows, seq, slots = plan.n, plan.rows, plan.seq, plan.slots
    line = jnp.broadcast_to(slot_row[...], (8, rows))
    begins = jnp.where(at.side == 0, 0, lengths[0, 0])
    count = jnp.where(at.side == 0, lengths[0, 0], lengths[0, 1])
    back = rows - begins
    bit = 1
    while bit < rows:
        turn_it = jnp.broadcast_to(back & bit, line.shape) != 0
        line = jnp.where(turn_it, pltpu.roll(line, bit, 1), line)
        bit *= 2
    slot = line[0:1, 0:seq]
    token = lax.broadcasted_iota(jnp.int32, (1, seq), 1)
    named = (token < count) & (slot < rows)
    slot = jnp.where(named, slot, 0)
    source = jnp.where(named, over(slot, slots), -1)
    wrow[0:1, :] = jnp.where(named, plan.come_index(over(slot, slots), over(token, n)), -1)
    lines = over(lax.broadcasted_iota(jnp.int32, (8 * n, seq), 0), 8)
    told = jnp.where(lines == source, (under(slot, slots) + 1).astype(F32), 0.0).astype(BF)
    turn = over(lax.broadcasted_iota(jnp.int32, (seq, LANES), 0), n)
    turns = jnp.where(turn == lax.broadcasted_iota(jnp.int32, (seq, LANES), 1), 1.0, 0.0).astype(BF)
    tab_out[...] = nn(told, turns)


def block_kernel(
    plan,
    tokens,
    cotangent,
    slot_row,
    lengths,
    vec_in,
    qv_in,
    wqkv_in,
    wo_in,
    wfc,
    wproj,
    block_out,
    input_grad,
    proj_total,
    fc_total,
    attn_total,
    vec_total,
    tab,
    vec,
    tab_out,
    wrow,
    wattn,
    vec2,
    weights2,
    act,
    dhid,
    own_x,
    n1,
    cot_p,
    n2,
    dattn,
    qkv,
    v_t,
    att_t,
    lse,
    delta,
    term,
    land_a,
    land_b,
    land_c,
    mid,
    dout,
    dq_acc,
    grads,
    landing,
    res,
    going,
    vec_s,
    vec_r,
    tok_s,
    tok_r,
    cot_s,
    cot_r,
    ag_s,
    ag_r,
    mate_s,
    mate_r,
    sum_s,
    sum_r,
    weight_s,
    weight_r,
    tab_s,
    tab_r,
    back_s,
    back_r,
    back_l,
    share_s,
    share_r,
    total_s,
    total_r,
    vec_ss,
    vec_sr,
    local,
):
    at = Place(plan)
    rows, width, pad, seq = plan.rows, plan.width, plan.pad, plan.seq
    own, part_rows, per, slots = plan.own, plan.part, plan.per, plan.slots
    n = plan.n
    span = plan.heads * HD
    fetch = [
        pltpu.make_async_copy(wqkv_in, wattn.at[0 : 3 * span], local.at[0]),
        pltpu.make_async_copy(wo_in, wattn.at[3 * span : 4 * span], local.at[1]),
        pltpu.make_async_copy(tokens, act, local.at[2]),
        pltpu.make_async_copy(cotangent, dhid, local.at[3]),
    ]
    for copy in fetch:
        copy.start()
    vec[...] = vec_in[...].astype(F32)
    vec[V_QKVB : V_QKVB + 1, 0:span] = qv_in[0:1, :].astype(F32)
    vec[V_QKVB : V_QKVB + 1, 2 * pad : 2 * pad + span] = qv_in[1:2, :].astype(F32)
    greet(plan, at)
    list_slots(plan, at, slot_row, lengths, wrow, tab_out)
    all_here(plan)
    dqkv, grads2 = act, dhid
    mlp_term = grads.at[2 * width : 2 * width + seq]
    tok_come, cot_come = grads.at[0:seq], grads.at[seq : 2 * seq]
    tok_stage, cot_stage = term, grads.at[2 * seq : 3 * seq]

    def come(buf):
        return lambda c, gi: buf.at[rows_at((2 * c + at.core) * own + gi * plan.take, plan.take)]

    tok = Incoming(at, tok_stage, (tok_s, tok_r), come(tok_come))
    cot = Incoming(at, cot_stage, (cot_s, cot_r), come(cot_come))
    tok_all = MateGather(at, tok_come, (ag_s.at[0], ag_r.at[0]), own)
    cot_all = MateGather(at, cot_come, (ag_s.at[1], ag_r.at[1]), own)
    n1_mate, cot_mate, n2_mate, dattn_mate, res_mate, dx_mate = (
        MateGather(at, buf, (mate_s.at[i], mate_r.at[i]), part_rows)
        for i, buf in enumerate((n1, cot_p, n2, dattn, res, res))
    )
    attn_sum, back_sum, mlp_sum, norm_sum = (
        MateSum(at, ref, land, (sum_s.at[i], sum_r.at[i]))
        for i, (ref, land) in enumerate(
            ((term, land_a), (term, land_b), (mlp_term, land_c), (term, land_a))
        )
    )
    weights = (wattn, wfc, wproj)
    pieces = {}
    for i, (name, which, start, stop, bits) in enumerate(MOVES):
        pieces[name] = Weights(
            at,
            weights[which].at[start:stop],
            weights2.at[which * width + start : which * width + stop],
            (weight_s.at[i], weight_r.at[i]),
            0,
            bits,
        )

    def weight(gi, i, start=0, stop=width):
        if gi:
            return weights2[i * width + start : i * width + stop, :]
        return weights[i][start:stop, :]

    vec_g = (vec, vec2)
    out_way, grad_way = (
        Outgoing(
            at,
            going.at[i],
            out,
            (back_s.at[i], back_r.at[i]),
            back_l.at[i],
            (share_s.at[i], share_r.at[i]),
        )
        for i, out in enumerate((block_out, input_grad))
    )
    outs = {"P": proj_total, "F": fc_total, "A": attn_total}
    room, index = 0, 0
    for name, kind, start, stop, order, early in TOTALS:
        first, at_row = {"P": (grads, 0), "F": (grads, 2 * width), "A": (grads2, 0)}[kind]
        pieces[name] = Total(
            at,
            first,
            [at_row + gi * width + start for gi in range(2)],
            outs[kind].at[start:stop],
            landing,
            room,
            (total_s, total_r),
            index,
            order,
            early,
        )
        more, sems = total_room(stop - start, n, early)
        room, index = room + more, index + sems

    def incoming(way, every, c):
        def first():
            if c < plan.split:
                way.start(c)

        def second():
            way.wait(c)
            every.start(c)

        return Steps(first, second, lambda: every.finish(c))

    def outgoing(way, c):
        part_of = c - (CHUNKS - plan.split)

        def when_part(run):
            return lambda: run(part_of) if part_of >= 0 else None

        return Steps(
            lambda: way.start(c),
            when_part(way.share),
            when_part(way.forward),
            when_part(way.finish),
        )

    for c in range(CHUNKS):
        pieces["0123"[c]] = incoming(tok, tok_all, c)
        pieces["4567"[c]] = incoming(cot, cot_all, c)
        pieces["ijkl"[c]] = outgoing(out_way, c)
        pieces["rstu"[c]] = outgoing(grad_way, c)

    hops = [{"mp": at.mate}, {"mp": at.across}]
    bit = 1
    while bit < n:
        high = lax.rem(at.d // bit, 2)
        hops.append({"dp": at.d + (1 - 2 * high) * bit})
        bit *= 2
    vec_total_sum = VecTotal(hops, vec_s, vec_r, vec_total, (vec_ss, vec_sr))
    pieces["v"] = vec_total_sum
    schedule = iter(SCHEDULE)

    def go():
        for name in next(schedule, ""):
            pieces[name].step()

    def need(names):
        for name in names:
            pieces[name].finish()

    def begin(table, kind, early=None):
        for entry in table:
            if entry[1] == kind and early in (None, entry[-1]):
                pieces[entry[0]].step()

    def names_of(table, *kinds):
        return [entry[0] for entry in table if entry[1] in kinds]

    def row(i):
        return vec[i : i + 1, :]

    def add_line(line, value):
        vec_s[0, line : line + 1, :] += jnp.sum(value, axis=0, keepdims=True)

    def pack(c, buf):
        line = wrow[0:1, rows_at(at.mine(c), part_rows, LANES)].astype(F32)
        col = jnp.broadcast_to(line, (8, part_rows)).T[:, 0:1].astype(jnp.int32)
        return nn(pick(col, seq), buf[...])

    fetch[0].wait()
    fetch[1].wait()
    begin(MOVES, 0)
    bias_copy = send(vec, vec2, (vec_ss, vec_sr), 0, {"mp": at.across})
    go()
    def tell(j, carry):
        k = lax.rem(at.d + j, n)
        pltpu.make_async_remote_copy(
            src_ref=tab_out.at[rows_at(k * 8, 8, 8)],
            dst_ref=tab.at[at.side, rows_at(at.d * 8, 8, 8)],
            send_sem=tab_s.at[j],
            recv_sem=tab_r.at[at.d],
            device_id={"dp": k},
            device_id_type=MESH,
        ).start()
        return carry

    lax.fori_loop(1, n, tell, 0)
    tab[at.side, rows_at(at.d * 8, 8, 8), :] = tab_out[rows_at(at.d * 8, 8, 8), :]
    vec_s[0, :, :] = jnp.zeros((GLINES, width), F32)
    dq_acc[...] = jnp.zeros_like(dq_acc)
    qkv[...] = jnp.zeros_like(qkv)
    dout[...] = jnp.zeros_like(dout)

    def hear(j, carry):
        k = lax.rem(at.d + j, n)
        landed(tab.at[at.side, rows_at(k * 8, 8, 8)], (tab_s, tab_r), k, {"dp": k})
        return carry

    lax.fori_loop(1, n, hear, 0)

    def choose(buf, stage):
        def one(k, carry):
            col = tab[at.side, rows_at(k * 8, 8, 8), :].T[0:per, 0:1].astype(jnp.int32) - 1
            rows_of = nn(pick(col, slots), buf[rows_at(k * slots, slots), :])
            stage[rows_at(k * per, per), :] = rows_of.astype(BF)
            return carry

        lax.fori_loop(0, n, one, 0)

    fetch[2].wait()
    choose(act, tok_stage)
    for c in range(CHUNKS):
        pieces["0123"[c]].step()
    go()
    tab_copy = send(tab.at[at.side], tab.at[at.side], (tab_s, tab_r), n, {"mp": at.across})
    fetch[3].wait()
    choose(dhid, cot_stage)
    go()
    need("0123")
    for c in range(HALVES):
        packed = pack(c, tok_come)
        own_x[c * part_rows : (c + 1) * part_rows, :] = packed.astype(BF)
        normal, _ = normal_rows(packed)
        n1[rows_at(at.mine(c), part_rows), :] = (normal * row(V_LN1G) + row(V_LN1B)).astype(BF)
        n1_mate.start(c)
    go()
    for c in range(HALVES):
        n1_mate.finish(c)

    def project(gi):
        def one(i, carry):
            here = rows_at(i * TILE, TILE, TILE)
            there = rows_at(gi * seq + i * TILE, TILE, TILE)
            for j in range(3):
                made = nt(n1[here, :], weight(gi, 0, j * span, (j + 1) * span))
                made = made + vec_g[gi][V_QKVB : V_QKVB + 1, j * pad : j * pad + span]
                if j == 0:
                    made = made * HD**-0.5
                qkv[there, j * pad : j * pad + span] = made.astype(BF)
            turned = qkv[there, 2 * pad :].astype(F32).T.astype(BF)
            v_t[gi * span : (gi + 1) * span, here] = turned[0:span, :]
            return carry

        lax.fori_loop(0, seq // TILE, one, 0)

    key_line = lax.broadcasted_iota(jnp.int32, (TILE, TILE), 0)
    query_line = lax.broadcasted_iota(jnp.int32, (TILE, TILE), 1)
    seen = key_line <= query_line

    def attend(gi, i):
        q0, base = i * TILE, gi * seq
        cols = slice(q0, q0 + TILE)
        for h in range(plan.heads):
            lanes = (h // 2) * LANES
            q_lanes = slice(lanes, lanes + LANES)
            k_lanes = slice(pad + lanes, pad + lanes + LANES)
            vh = v_t.at[gi * span + h * HD : gi * span + (h + 1) * HD]
            qh = head_lanes(qkv[base + q0 : base + q0 + TILE, q_lanes], h % 2 == 1)
            near = jnp.where(seen, nt(qkv[base + q0 : base + q0 + TILE, k_lanes], qh), NEG)
            top = jnp.max(near, axis=0, keepdims=True)
            if i:
                old = nt(qkv[base : base + q0, k_lanes], qh)
                top = jnp.maximum(top, jnp.max(old, axis=0, keepdims=True))
            expo = jnp.exp2((near - top) * LOG2E)
            total = jnp.sum(expo, axis=0, keepdims=True)
            out = nn(vh[:, cols], expo.astype(BF))
            if i:
                expo = jnp.exp2((old - top) * LOG2E)
                total = total + jnp.sum(expo, axis=0, keepdims=True)
                out = out + nn(vh[:, 0:q0], expo.astype(BF))
            line = gi * 4 + h
            att_t[gi * span + h * HD : gi * span + (h + 1) * HD, cols] = (out * (1.0 / total)).astype(BF)
            lse[line : line + 1, cols] = top * LOG2E + jnp.log2(total)

    blocks = seq // TILE

    def merge(c):
        def one(i, carry):
            here = rows_at(c * plan.half + i * TILE, TILE, TILE)
            total = None
            for gi in range(2):
                att = att_t[gi * span : (gi + 1) * span, here].astype(F32).T.astype(BF)
                value = nn(att, weight(gi, 0, 3 * span, 4 * span))
                total = value if total is None else total + value
            term[here, :] = total.astype(BF)
            return carry

        lax.fori_loop(0, plan.half // TILE, one, 0)

    project(0)
    for i in range(blocks):
        go()
        attend(0, i)
    go()
    need(names_of(MOVES, 0))
    landed(vec2, (vec_ss, vec_sr), 0, {"mp": at.across})
    project(1)
    for i in range(blocks):
        go()
        attend(1, i)
    go()
    tok.drain()
    for c in range(HALVES):
        merge(c)
        attn_sum.start(c)
    go()
    need("4567")
    for c in range(HALVES):
        packed = pack(c, cot_come)
        cot_p[rows_at(at.mine(c), part_rows), :] = packed.astype(BF)
        add_line(G_PROJB, packed)
        cot_mate.start(c)
        middle = own_x[c * part_rows : (c + 1) * part_rows, :].astype(F32) + (
            attn_sum.finish(c) + row(V_OUTB)
        )
        mid[c * part_rows : (c + 1) * part_rows, :] = middle
        normal, _ = normal_rows(middle)
        n2[rows_at(at.mine(c), part_rows), :] = (normal * row(V_LN2G) + row(V_LN2B)).astype(BF)
        n2_mate.start(c)
    attn_sum.drain()
    go()
    need(names_of(MOVES, 1, 2))
    tok_all.drain()
    cot_all.drain()
    cot.drain()
    for c in range(HALVES):
        n2_mate.finish(c)
        cot_mate.finish(c)

        def feed(i, carry, c=c):
            here = rows_at(c * plan.half + i * TILE, TILE, TILE)
            up, down = None, None
            for gi in range(2):
                there = rows_at(gi * seq + c * plan.half + i * TILE, TILE, TILE)
                v = nn(n2[here, :], weight(gi, 1)) + vec_g[gi][V_FCB : V_FCB + 1, :]
                square = v * v
                t = jnp.tanh(GELU * v * (1.0 + CUBE * square))
                halved = 0.5 * (1.0 + t)
                active = (v * halved).astype(BF)
                slope = halved + 0.5 * v * (1.0 - t * t) * (GELU * (1.0 + 3.0 * CUBE * square))
                act[there, :] = active
                more = nn(active, weight(gi, 2))
                up = more if up is None else up + more
                low = (nt(cot_p[here, :], weight(gi, 2)) * slope).astype(BF)
                dhid[there, :] = low
                add_line((G_FCB, G_FCB2)[gi], low.astype(F32))
                more = nt(low, weight(gi, 1))
                down = more if down is None else down + more
            mlp_term[here, :] = up.astype(BF)
            term[here, :] = down.astype(BF)
            return carry

        lax.fori_loop(0, plan.half // TILE, feed, 0)
        back_sum.start(c)
        mlp_sum.start(c)
        go()

    def weight_grad(left_ref, left_row, right_ref, right_row, dst, place):
        def one(i, carry):
            cols = rows_at(i * TILE, TILE, TILE)
            value = tn(left_ref[left_row : left_row + seq, cols], right_ref[right_row : right_row + seq, :])
            dst[rows_at(place + i * TILE, TILE, TILE), :] = value.astype(BF)
            return carry

        lax.fori_loop(0, width // TILE, one, 0)

    for gi in (1, 0):
        weight_grad(act, gi * seq, cot_p, 0, grads, gi * width)
        if gi:
            begin(TOTALS, "P", True)
            go()
    begin(TOTALS, "P", False)
    go()
    for c in range(HALVES):
        mine = slice(c * part_rows, (c + 1) * part_rows)
        where = rows_at(at.mine(c), part_rows)
        grad2 = back_sum.finish(c)
        middle = mid[mine, :]
        res[where, :] = (middle + (mlp_sum.finish(c) + row(V_PROJB))).astype(BF)
        res_mate.start(c)
        normal, inv = normal_rows(middle)
        grad_mid = cot_p[where, :].astype(F32) + norm_back(grad2, normal, inv, row(V_LN2G))
        low = grad_mid.astype(BF)
        mid[mine, :] = grad_mid
        dattn[where, :] = low
        dattn_mate.start(c)
        add_line(G_LN2G, grad2 * normal)
        add_line(G_LN2B, grad2)
        add_line(G_OUTB, low.astype(F32))
    mlp_sum.drain()
    go()
    for gi in (1, 0):
        weight_grad(n2, 0, dhid, gi * seq, grads, (2 + gi) * width)
        if gi:
            begin(TOTALS, "F", True)
            go()
    begin(TOTALS, "F", False)
    back_sum.drain()
    go()

    def unpack(c, out):
        start = (2 * c + at.core) * own
        out[c * own : (c + 1) * own, :] = nn(pick_rows(wrow[0:1, :], start, own), res[...]).astype(BF)

    for c in range(HALVES):
        res_mate.finish(c)
    for c in range(CHUNKS):
        unpack(c, going.at[0])
        pieces["ijkl"[c]].step()
    go()
    for c in range(HALVES):
        dattn_mate.finish(c)
    for gi in range(2):

        def back_out(i, carry, gi=gi):
            here = rows_at(i * TILE, TILE, TILE)
            there = rows_at(gi * seq + i * TILE, TILE, TILE)
            low = nt(dattn[here, :], weight(gi, 0, 3 * span, 4 * span)).astype(BF)
            dout[there, 0:span] = low
            turned = dout[there, :].astype(F32).T
            both = turned[0:span, :] * att_t[gi * span : (gi + 1) * span, here].astype(F32)
            for h in range(plan.heads):
                line = gi * 4 + h
                delta[line : line + 1, here] = jnp.sum(both[h * HD : (h + 1) * HD, :], axis=0, keepdims=True)
            return carry

        lax.fori_loop(0, seq // TILE, back_out, 0)
        grads2[gi * width + 3 * span : gi * width + 4 * span, :] = nn(
            att_t[gi * span : (gi + 1) * span, :], dattn[...]
        ).astype(BF)

    def attend_back(gi, i):
        k0, base = i * TILE, gi * seq
        k_rows = slice(base + k0, base + k0 + TILE)
        parts = []
        for h in range(plan.heads):
            lanes = (h // 2) * LANES
            q_lanes = slice(lanes, lanes + LANES)
            kh = head_lanes(qkv[k_rows, pad + lanes : pad + lanes + LANES], h % 2 == 1)
            vh = head_lanes(qkv[k_rows, 2 * pad + lanes : 2 * pad + lanes + LANES], h % 2 == 1)
            if h % 2 == 0:
                turned = qkv[k_rows, pad + lanes : pad + lanes + LANES].astype(F32).T.astype(BF)
            kt = turned[(h % 2) * HD : (h % 2 + 1) * HD, :]
            line = gi * 4 + h
            dk = dv = None
            for q0, q1 in ((k0, k0 + TILE), (k0 + TILE, seq)):
                if q0 == q1:
                    continue
                q_all = qkv[base + q0 : base + q1, q_lanes]
                do_all = dout[base + q0 : base + q1, q_lanes]
                prob = jnp.exp2(nt(kh, q_all) * LOG2E - lse[line : line + 1, q0:q1])
                if q0 == k0:
                    prob = jnp.where(seen, prob, 0.0)
                low = (prob * (nt(vh, do_all) - delta[line : line + 1, q0:q1])).astype(BF)
                more_v, more_k = nn(prob.astype(BF), do_all), nn(low, q_all)
                dv = more_v if dv is None else dv + more_v
                dk = more_k if dk is None else dk + more_k
                dq_acc[gi * span + h * HD : gi * span + (h + 1) * HD, q0:q1] += nn(kt, low)
            parts.append((dk, dv))
        for h in range(0, plan.heads, 2):
            lanes = (h // 2) * LANES
            for j in range(2):
                value = head_lanes(parts[h][j], False)
                if h + 1 < plan.heads:
                    value = value + head_lanes(parts[h + 1][j], True)
                start = (1 + j) * pad + lanes
                dqkv[k_rows, start : start + LANES] = value.astype(BF)

    def qkv_weight_grad(gi):
        def turn_dq(i, carry):
            here = rows_at(i * TILE, TILE, TILE)
            there = rows_at(gi * seq + i * TILE, TILE, TILE)
            turned = jnp.concatenate(
                [dq_acc[gi * span : (gi + 1) * span, here], jnp.zeros((pad - span, TILE), F32)], axis=0
            )
            dqkv[there, 0:pad] = (turned.T * HD**-0.5).astype(BF)
            return carry

        lax.fori_loop(0, seq // TILE, turn_dq, 0)
        return lambda: weigh(gi)

    def weigh(gi):
        for j in range(3):
            row0 = gi * width + j * span
            grads2[row0 : row0 + span, :] = tn(
                dqkv[gi * seq : (gi + 1) * seq, j * pad : j * pad + span], n1[...]
            ).astype(BF)

    for i in range(blocks):
        go()
        attend_back(1, i)
    go()
    qkv_weight_grad(1)()
    begin(TOTALS, "A", True)
    for i in range(blocks):
        go()
        attend_back(0, i)
    go()
    weigh_mine = qkv_weight_grad(0)
    for c in range(HALVES):

        def back_project(i, carry, c=c):
            here = rows_at(c * plan.half + i * TILE, TILE, TILE)
            total = None
            for gi in range(2):
                there = rows_at(gi * seq + c * plan.half + i * TILE, TILE, TILE)
                add_line((G_QKVB, G_QKVB2)[gi], dqkv[there, :].astype(F32))
                for j in range(3):
                    more = nn(dqkv[there, j * pad : j * pad + span], weight(gi, 0, j * span, (j + 1) * span))
                    total = more if total is None else total + more
            term[here, :] = total.astype(BF)
            return carry

        lax.fori_loop(0, plan.half // TILE, back_project, 0)
        norm_sum.start(c)
    go()
    for c in range(HALVES):
        mine = slice(c * part_rows, (c + 1) * part_rows)
        grad1 = norm_sum.finish(c)
        normal, inv = normal_rows(own_x[mine, :].astype(F32))
        dx = mid[mine, :] + norm_back(grad1, normal, inv, row(V_LN1G))
        if c == 0:
            res_mate.drain()
        res[rows_at(at.mine(c), part_rows), :] = dx.astype(BF)
        dx_mate.start(c)
        add_line(G_LN1G, grad1 * normal)
        add_line(G_LN1B, grad1)
    bias_copy.wait_send()
    pieces["v"].step()
    go()
    for c in range(HALVES):
        dx_mate.finish(c)
    for c in range(CHUNKS):
        unpack(c, going.at[1])
        pieces["rstu"[c]].step()
    go()
    weigh_mine()
    begin(TOTALS, "A", False)
    for _ in range(TAIL):
        go()
    need(pieces)
    out_way.drain()
    grad_way.drain()

    def told_all(j, carry):
        k = lax.rem(at.d + j, n)
        left(tab_out.at[rows_at(k * 8, 8, 8)], (tab_s, tab_r), j, {"dp": k})
        return carry

    lax.fori_loop(1, n, told_all, 0)
    tab_copy.wait_send()
    landed(tab.at[1 - at.side], (tab_s, tab_r), n, {"mp": at.across})
    for each in (n1_mate, cot_mate, n2_mate, dattn_mate, dx_mate, norm_sum):
        each.drain()


def finish_kernel(rows_a, rows_b, tab, vec, proj, fc, qkv, out, out_a, out_b, proj_f, fc_f, qkv_f, out_f, qv_f):
    proj_f[...] = proj[...].astype(F32)
    fc_f[...] = fc[...].astype(F32)
    qkv_f[...] = qkv[...].astype(F32)
    out_f[...] = out[...].astype(F32)
    span, pad = qv_f.shape[1], vec.shape[1] // 3
    qv_f[0:1, :] = vec[G_QKVB : G_QKVB + 1, 0:span]
    qv_f[1:2, :] = vec[G_QKVB : G_QKVB + 1, 2 * pad : 2 * pad + span]
    n = tab.shape[1] // 8
    slots = rows_a.shape[0] // n

    def one(k, carry):
        here = rows_at(k * slots, slots)
        lines = [tab[side, rows_at(k * 8, 8, 8), :][0:1, 0 : slots // 2] for side in range(2)]
        slot = jnp.concatenate(lines, axis=1).astype(jnp.int32) - 1
        place = lax.broadcasted_iota(jnp.int32, (slots, slots), 0)
        hot = jnp.where(place == slot, 1.0, 0.0).astype(BF)
        out_a[here, :] = nn(hot, rows_a[here, :]).astype(BF)
        out_b[here, :] = nn(hot, rows_b[here, :]).astype(BF)
        return carry

    lax.fori_loop(0, n, one, 0)


def body(
    tokens,
    cotangent,
    seq_lengths,
    source_slot,
    ln1_gain,
    ln1_bias,
    qkv_weight,
    qv_bias,
    output_projection_weight,
    out_bias,
    ln2_gain,
    ln2_bias,
    fc_weight,
    fc_bias,
    proj_weight,
    proj_bias,
):
    rows, width = tokens.shape
    span = qkv_weight.shape[2]
    n, members = lax.axis_size("dp"), lax.axis_size("mp")
    plan = Plan(n, members, rows, width, span // HD)
    pad, seq = plan.pad, plan.seq

    vectors = (ln1_gain, ln1_bias, out_bias, ln2_gain, ln2_bias, proj_bias, fc_bias)
    line = jnp.arange(8, dtype=jnp.int32)[:, None]
    vec = jnp.zeros((8, width), BF)
    for i, v in enumerate(vectors):
        vec = jnp.where(line == i, v[None, :], vec)
    vm = pl.BlockSpec(memory_space=pltpu.VMEM)
    hbm = pl.BlockSpec(memory_space=pl.ANY)
    shape = jax.ShapeDtypeStruct
    quarter = rows // members
    dma = pltpu.SemaphoreType.DMA
    rooms = [total_room(entry[3] - entry[2], n, entry[5]) for entry in TOTALS]
    landing, sems = (sum(room[i] for room in rooms) for i in range(2))
    hops = 2 + (n - 1).bit_length()

    def vmem(*dims, dtype=BF):
        return pltpu.VMEM(dims, dtype)

    block_rows, grad_rows, proj_total, fc_total, attn_total, vec_total, tab = pl.pallas_call(
        functools.partial(block_kernel, plan),
        out_shape=(
            shape((rows, width), BF),
            shape((rows, width), BF),
            shape((width, width), BF),
            shape((width, width), BF),
            shape((width, width), BF),
            shape((8, width), F32),
            shape((2, 8 * n, LANES), F32),
        ),
        in_specs=[hbm, hbm, vm, pl.BlockSpec(memory_space=pltpu.SMEM), vm, vm, hbm, hbm, vm, vm],
        out_specs=(hbm,) * 5 + (vm, vm),
        scratch_shapes=[
            vmem(8, width, dtype=F32),
            vmem(8 * n, LANES, dtype=F32),
            vmem(8, seq, dtype=jnp.int32),
            vmem(width, width),
            vmem(8, width, dtype=F32),
            vmem(3 * width, width),
            vmem(rows, width),
            vmem(rows, width),
            vmem(quarter, width),
            vmem(seq, width),
            vmem(seq, width),
            vmem(seq, width),
            vmem(seq, width),
            vmem(2 * seq, 3 * pad),
            vmem(2 * span, seq),
            vmem(2 * span, seq),
            vmem(8, seq, dtype=F32),
            vmem(8, seq, dtype=F32),
            vmem(seq, width),
            vmem(seq // 2, width),
            vmem(seq // 2, width),
            vmem(seq // 2, width),
            vmem(seq // 2, width, dtype=F32),
            vmem(2 * seq, pad),
            vmem(2 * span, seq, dtype=F32),
            vmem(4 * width, width),
            vmem(landing, width),
            vmem(seq, width),
            vmem(2, quarter, width),
            vmem(hops, GLINES, width, dtype=F32),
            vmem(hops, GLINES, width, dtype=F32),
            dma((plan.split, n)),
            dma((CHUNKS, plan.in_chunk)),
            dma((plan.split, n)),
            dma((CHUNKS, plan.in_chunk)),
            dma((2, CHUNKS)),
            dma((2, CHUNKS)),
            dma((6, HALVES)),
            dma((6, HALVES)),
            dma((4, HALVES)),
            dma((4, HALVES)),
            dma((len(MOVES), 4)),
            dma((len(MOVES), 4)),
            dma((n + 1,)),
            dma((n + 1,)),
            dma((2, CHUNKS, plan.in_chunk)),
            dma((2, plan.split, n)),
            dma((2, plan.split)),
            dma((2, 3, plan.split, n)),
            dma((2, 3, plan.split, n)),
            dma((sems,)),
            dma((sems,)),
            dma((hops + 1,)),
            dma((hops + 1,)),
            dma((4,)),
        ],
        compiler_params=pltpu.CompilerParams(
            collective_id=0, has_side_effects=True, vmem_limit_bytes=VMEM_LIMIT
        ),
        name="block",
    )(
        tokens,
        cotangent,
        source_slot.reshape(1, rows),
        seq_lengths,
        vec,
        qv_bias,
        qkv_weight.transpose(1, 2, 0).reshape(3 * span, width),
        output_projection_weight,
        fc_weight,
        proj_weight,
    )
    def tall(count):
        return pl.BlockSpec((count // STEPS, width), lambda i: (i, 0))

    block_out, input_grad, proj_grad, fc_grad, qkv_grad, out_grad, qv_grad = pl.pallas_call(
        finish_kernel,
        out_shape=(
            shape((rows, width), BF),
            shape((rows, width), BF),
            shape((width, width), F32),
            shape((width, width), F32),
            shape((3 * span, width), F32),
            shape((span, width), F32),
            shape((2, span), F32),
        ),
        grid=(STEPS,),
        in_specs=[
            tall(rows),
            tall(rows),
            pl.BlockSpec((2, 8 * n // STEPS, LANES), lambda i: (0, i, 0)),
            pl.BlockSpec((8, width), lambda i: (0, 0)),
            tall(width),
            tall(width),
            tall(3 * span),
            pl.BlockSpec((span // STEPS, width), lambda i: (3 * STEPS + i, 0)),
        ],
        out_specs=(tall(rows), tall(rows), tall(width), tall(width), tall(3 * span), tall(span))
        + (pl.BlockSpec((2, span), lambda i: (0, 0)),),
        compiler_params=pltpu.CompilerParams(vmem_limit_bytes=VMEM_LIMIT),
        name="finish",
    )(block_rows, grad_rows, tab, vec_total, proj_total, fc_total, attn_total, attn_total)
    return (
        block_out,
        input_grad,
        vec_total[G_LN1G],
        vec_total[G_LN1B],
        qkv_grad.reshape(3, span, width).transpose(2, 0, 1),
        qv_grad,
        out_grad,
        vec_total[G_OUTB],
        vec_total[G_LN2G],
        vec_total[G_LN2B],
        fc_grad,
        vec_total[G_FCB],
        proj_grad,
        vec_total[G_PROJB],
    )


def solution(mesh):
    return jax.shard_map(
        body,
        mesh=mesh,
        in_specs=(
            P("dp", None),
            P("dp", None),
            P("dp", None),
            P("dp"),
            P(),
            P(),
            P(None, None, "mp"),
            P(None, "mp"),
            P("mp", None),
            P(),
            P(),
            P(),
            P(None, "mp"),
            P("mp"),
            P("mp", None),
            P(),
        ),
        out_specs=(
            P("dp", None),
            P("dp", None),
            P(),
            P(),
            P(None, None, "mp"),
            P(None, "mp"),
            P("mp", None),
            P(),
            P(),
            P(),
            P(None, "mp"),
            P("mp"),
            P("mp", None),
            P(),
        ),
        check_vma=False,
    )
```
